128 devices in a mesh: section: 2 (over core), dp: 8 (over z, y_hi), tensor: 8 (over y_lo, x).
Axes of the slice: x: 4, y: 4 (y_hi: 2, y_lo: 2; y = y_hi * 2 + y_lo), z: 4, core: 2. Of those that a mesh axis runs over, the one named last changes fastest.
Arguments:
- inputs: bfloat16 [2, 576, 8, 1024], P(None, 'tensor', 'dp'), may hold values from -6 to 6
- cotangent: bfloat16 [2, 576, 8, 1024], P(None, 'tensor', 'dp'), may hold values from -6 to 6
- qkv_weight: bfloat16 [2, 1024, 3, 1024], P('section', 'dp', None, 'tensor'), may hold values from -0.1875 to 0.1875
- proj_weight: bfloat16 [2, 1024, 1024], P('section', 'tensor', 'dp'), may hold values from -0.75 to 0.75
- fc1_weight: bfloat16 [2, 1024, 4, 1024], P('section', 'dp', None, 'tensor'), may hold values from -0.1875 to 0.1875
- fc2_weight: bfloat16 [2, 4, 1024, 1024], P('section', None, 'tensor', 'dp'), may hold values from -0.09375 to 0.09375
- vectors: bfloat16 [2, 12, 1024], P('section', None, ('dp', 'tensor')), may hold values from -1.5 to 1.5
Outputs:
- activations: bfloat16 [2, 2, 576, 8, 1024], P('section', None, 'tensor', 'dp')
- grad_input: float32 [2, 2, 576, 8, 1024], P('section', None, 'tensor', 'dp')
- grad_qkv: float32 [2, 1024, 3, 1024], P('section', 'dp', None, 'tensor')
- grad_proj: float32 [2, 1024, 1024], P('section', 'tensor', 'dp')
- grad_fc1: float32 [2, 1024, 4, 1024], P('section', 'dp', None, 'tensor')
- grad_fc2: float32 [2, 4, 1024, 1024], P('section', None, 'tensor', 'dp')
- grad_vectors: float32 [2, 12, 1024], P('section', None, ('dp', 'tensor'))
The draws below stay inside these ranges and needn't reach their ends.
All inputs are finite; a program needn't handle non-finite values.
Results may differ from the reference program's by a relative error of at most 0.019.
Values may be sent and summed in bfloat16 or wider, within the bound.
No kernel may reach another device: no remote copies, remote signals or barrier semaphores. Data moves between devices by JAX's collectives and lax.ppermute only.
A program may use at most 128 MiB of HBM per device.

```python
import jax
import jax.numpy as jnp
from jax import lax

D = 1024
HEADS = 16
HDIM = 64
FF = 4096
SEQ = 576
MB = 2
SECTIONS = 2
IMAGES = 8


def draw_vectors(key, part):
    key = jax.random.fold_in(key, 7)
    spread = jax.random.normal(key, (SECTIONS, 12, D), jnp.float32)
    rows = jnp.arange(12)
    is_gain = ((rows == 0) | (rows == 2))[None, :, None]
    gains = 1.0 + 0.25 * jnp.clip(spread, -2.0, 2.0)
    biases = 0.5 * jnp.clip(spread, -3.0, 3.0)
    return jnp.where(is_gain, gains, biases).astype(jnp.bfloat16)


def shard_levels(key, extent, split, least, top_value):
    def one(dim, parts):
        draws = jax.random.uniform(jax.random.fold_in(jax.random.fold_in(key, 6), dim), (parts,), jnp.float32, least / len(split), top_value / len(split))
        return jnp.repeat(jnp.exp(draws), extent[dim] // parts).reshape((-1,) + (1,) * (len(extent) - dim - 1))

    level = one(*split[0])
    for cut in split[1:]:
        level = level * one(*cut)
    return level


def gaussian(stream_key, shape, deviation, limit, split=(), dtype=jnp.bfloat16):
    drawn = jax.random.normal(stream_key, shape, jnp.float32) * deviation
    if len(split) > 0:
        drawn = shard_levels(stream_key, shape, split, -0.22, 0.18) * drawn
    return jnp.clip(drawn, min=-limit, max=limit).astype(dtype)


def setup_inputs(seed: int = 0) -> dict:
    splits = jax.random.split(jax.random.key(seed), 8)
    inputs = gaussian(splits[0], (MB, SEQ, IMAGES, D), 1.0, 6.0, ((1, 8), (2, 8)))
    cotangent = gaussian(splits[1], (MB, SEQ, IMAGES, D), 1.0, 6.0, ((1, 8), (2, 8)))
    qkv_weight = gaussian(splits[2], (SECTIONS, D, 3, D), D ** -0.5, 0.1875, ((0, 2), (1, 8), (3, 8)))
    proj_weight = gaussian(splits[3], (SECTIONS, D, D), (D // 16) ** -0.5, 0.75, ((0, 2), (1, 8), (2, 8)))
    fc1_weight = gaussian(splits[4], (SECTIONS, D, 4, D), D ** -0.5, 0.1875, ((0, 2), (1, 8), (3, 8)))
    fc2_weight = gaussian(splits[5], (SECTIONS, 4, D, D), FF ** -0.5, 0.09375, ((0, 2), (2, 8), (3, 8)))
    vectors = draw_vectors(jax.random.fold_in(splits[7], 71), 0)
    return dict(inputs=inputs, cotangent=cotangent, qkv_weight=qkv_weight, proj_weight=proj_weight, fc1_weight=fc1_weight, fc2_weight=fc2_weight, vectors=vectors)


@jax.custom_vjp
def low(v):
    return lax.optimization_barrier(v.astype(jnp.bfloat16)).astype(jnp.float32)

@jax.custom_vjp
def low_back(v):
    return v

def low_keep(v):
    return (low(v), None)

def low_pass(kept, grad):
    return (grad,)

def back_keep(v):
    return (v, None)

def back_low(kept, grad):
    return (low(grad),)
low.defvjp(low_keep, low_pass)
low_back.defvjp(back_keep, back_low)
eps = 1e-06

def layer_norm(rows, gain, shift):
    center = rows - lax.optimization_barrier(jnp.mean(rows, axis=-1, keepdims=True))
    spread = lax.optimization_barrier(jnp.mean(center * center, axis=-1, keepdims=True))
    return center * lax.rsqrt(spread + eps) * gain + shift

def block(tokens, qkv_weight, proj_weight, fc1_weight, fc2_weight, vectors):
    best = lax.Precision.HIGHEST
    normed = low(layer_norm(tokens, vectors[0], vectors[1]))
    bias = jnp.stack([vectors[6], jnp.zeros_like(vectors[6]), vectors[7]])
    projected = jnp.einsum('sd,dke->ske', normed, qkv_weight, precision=best) + bias
    projected = low_back(low(projected))
    queries = projected[:, 0].reshape(SEQ, HEADS, HDIM)
    key_rows = projected[:, 1].reshape(SEQ, HEADS, HDIM)
    value_rows = projected[:, 2].reshape(SEQ, HEADS, HDIM)
    scale = HDIM ** (-0.5)
    scores = low_back(jnp.einsum('qhe,khe->hqk', queries, key_rows, precision=best) * scale)
    probs = low(jax.nn.softmax(scores, axis=-1))
    mixed = jnp.einsum('hqk,khe->qhe', probs, value_rows, precision=best).reshape(SEQ, D)
    mixed = low_back(low(mixed))
    branch = low_back(jnp.dot(mixed, proj_weight, precision=best) + vectors[4])
    middle = tokens + branch
    second = low(layer_norm(middle, vectors[2], vectors[3]))
    hidden = jnp.einsum('sd,dre->sre', second, fc1_weight, precision=best) + vectors[8:12]
    hidden = low_back(hidden)
    activated = low(jax.nn.gelu(hidden, approximate=False))
    down = low_back(jnp.einsum('sre,red->sd', activated, fc2_weight, precision=best) + vectors[5])
    return middle + down

def run_section(states, weights):
    flat = jnp.transpose(states, (0, 2, 1, 3)).reshape(MB * IMAGES, SEQ, D)

    def single(image):
        return block(image, *weights)
    done = lax.map(jax.checkpoint(single), flat)
    return jnp.transpose(done.reshape(MB, IMAGES, SEQ, D), (0, 2, 1, 3))

def reference(inputs, cotangent, qkv_weight, proj_weight, fc1_weight, fc2_weight, vectors):
    start = inputs.astype(jnp.float32)
    weights = tuple((weight.astype(jnp.float32) for weight in (qkv_weight, proj_weight, fc1_weight, fc2_weight, vectors)))
    opening = jnp.zeros_like(start)

    def forward(start, opening, qkv_all, proj_all, fc1_all, fc2_all, vector_all):
        everything = (qkv_all, proj_all, fc1_all, fc2_all, vector_all)
        first = run_section(start, tuple((weight[0] for weight in everything)))
        handed = low_back(low(first)) + opening
        second = run_section(handed, tuple((weight[1] for weight in everything)))
        return (first, second)
    outputs, pullback = jax.vjp(forward, start, opening, *weights)
    grads = pullback((jnp.zeros_like(outputs[0]), cotangent.astype(jnp.float32)))
    activations = jnp.stack([outputs[0], outputs[1]]).astype(jnp.bfloat16)
    grad_input = jnp.stack([grads[0], grads[1]])
    return (activations, grad_input, grads[2], grads[3], grads[4], grads[5], grads[6])
```

```python
import jax
import jax.numpy as jnp
from jax import lax
from jax.sharding import Mesh, PartitionSpec as P

HEADS = 16
HDIM = 64

eps = 1e-06
wide = jnp.float32
narrow = jnp.bfloat16


def swap_cores(value):
    return lax.ppermute(value, "core", [(0, 1), (1, 0)])


def along(value, axis, steps):
    count = lax.axis_size(axis)
    return lax.ppermute(value, axis, [(i, (i + steps) % count) for i in range(count)])


def turn(value, flip):
    pairs = []
    for core in range(2):
        for low in range(2):
            pairs.append((core * 2 + low, low * 2 + (core ^ flip)))
    return lax.ppermute(value, ("core", "ylo"), pairs)


def turn_back(value, flip):
    pairs = []
    for core in range(2):
        for low in range(2):
            pairs.append((core * 2 + low, (low ^ flip) * 2 + core))
    return lax.ppermute(value, ("core", "ylo"), pairs)


def gather_tokens(rows):
    count = lax.axis_size("x")
    parts = [rows] + [along(rows, "x", k) for k in range(1, count)]
    mine = jnp.concatenate(parts, axis=0)
    return mine, swap_cores(mine)


def scatter_tokens(make):
    count = lax.axis_size("x")
    arriving = swap_cores(make(1).astype(narrow))
    total = make(0) + arriving.astype(wide)
    rows = total.shape[0] // count
    result = total[:rows]
    sent = [along(total[k * rows : (k + 1) * rows].astype(narrow), "x", -k) for k in range(1, count)]
    for piece in sent:
        result = result + piece.astype(wide)
    return result


def normalise(rows):
    center = rows - jnp.mean(rows, axis=-1, keepdims=True)
    spread = jnp.mean(center * center, axis=-1, keepdims=True)
    inverse = lax.rsqrt(spread + eps)
    return center * inverse, inverse


def norm_back(grad, gain, unit, inverse):
    pulled = grad * gain
    mean_one = jnp.mean(pulled, axis=-1, keepdims=True)
    mean_two = jnp.mean(pulled * unit, axis=-1, keepdims=True)
    return inverse * (pulled - mean_one - unit * mean_two)


def dot(a, b):
    return jnp.dot(a, b, preferred_element_type=wide)


def dot_t(a, b):
    return lax.dot_general(a, b, (((1,), (1,)), ((), ())), preferred_element_type=wide)


def t_dot(a, b):
    return lax.dot_general(a, b, (((0,), (0,)), ((), ())), preferred_element_type=wide)


def heads_of(projected, which, local_width):
    part = projected[:, which * local_width : (which + 1) * local_width]
    return [part[:, h * HDIM : (h + 1) * HDIM] for h in range(local_width // HDIM)]


def attend(projected, local_width, scale):
    mixed, logs = [], []
    for q, k, v in zip(*(heads_of(projected, i, local_width) for i in range(3))):
        scores = dot_t(q, k) * scale
        peak = jnp.max(scores, axis=-1, keepdims=True)
        raised = jnp.exp(scores - peak)
        totals = jnp.sum(raised, axis=-1, keepdims=True)
        probs = (raised / totals).astype(narrow)
        mixed.append(dot(probs, v))
        logs.append(peak + jnp.log(totals))
    return jnp.concatenate(mixed, axis=1).astype(narrow), logs


def attend_back(projected, logs, mixed_grad, local_width, scale):
    query_grads, key_grads, value_grads = [], [], []
    out = [mixed_grad[:, h * HDIM : (h + 1) * HDIM] for h in range(local_width // HDIM)]
    for q, k, v, log_total, o in zip(
        *(heads_of(projected, i, local_width) for i in range(3)), logs, out
    ):
        probs = jnp.exp(dot_t(q, k) * scale - log_total)
        value_grads.append(t_dot(probs.astype(narrow), o))
        prob_grad = dot_t(o, v)
        score_grad = (
            probs * (prob_grad - jnp.sum(probs * prob_grad, axis=-1, keepdims=True))
        ).astype(narrow)
        query_grads.append(dot(score_grad, k) * scale)
        key_grads.append(t_dot(score_grad, q) * scale)
    return jnp.concatenate(query_grads + key_grads + value_grads, axis=1).astype(narrow)


def per_device(inputs, cotangent, qkv_weight, proj_weight, fc1_weight, fc2_weight, vectors):
    width = inputs.shape[3]
    core = lax.axis_index("core")
    low = lax.axis_index("ylo")
    part = core * lax.axis_size("x") + lax.axis_index("x")
    place = lax.axis_index("dp") * 8 + low * lax.axis_size("x") + lax.axis_index("x")
    local_width = qkv_weight.shape[3]
    scale = HDIM ** (-0.5)
    dp = lax.axis_size("dp")

    entering = turn(lax.dynamic_index_in_dim(inputs, core, 0, keepdims=False)[:, 0], 0)
    final_grad = turn(lax.dynamic_index_in_dim(cotangent, core, 0, keepdims=False)[:, 0], 0)

    columns = lax.broadcasted_iota(jnp.int32, (12, width), 1) // 16
    table = jnp.where(columns == place, jnp.tile(vectors[0], (1, width // 16)), 0).astype(narrow)
    for axis in ("x", "ylo", "dp"):
        pieces = [along(table, axis, k) for k in range(1, lax.axis_size(axis))]
        for piece in pieces:
            table = table + piece
    other_table = swap_cores(table)
    tables = [
        jnp.where(core == layer, table, other_table).astype(wide) for layer in range(2)
    ]

    packed = jnp.concatenate(
        [
            jnp.transpose(qkv_weight[0], (1, 0, 2)),
            proj_weight,
            jnp.transpose(fc1_weight[0], (1, 0, 2)),
            fc2_weight[0],
        ],
        axis=0,
    )
    half = packed.shape[1] // 2

    def half_of(which):
        return lax.dynamic_slice_in_dim(packed, which * half, half, 1)

    first, second_piece = turn(half_of(core), 0), turn(half_of(1 - core), 1)
    raw = [jnp.where(low == 0, first, second_piece), jnp.where(low == 0, second_piece, first)]
    weights = []
    for layer in range(2):
        parts = []
        for lo, hi in ((0, 3), (3, 12)):
            parts.append(lax.all_gather(raw[layer][lo:hi], ("dp", "ylo"), axis=0))
        qkv = parts[0].transpose(0, 2, 1, 3) if False else parts[0]
        qkv = jnp.transpose(qkv.reshape(dp, 2, 3, half, local_width), (0, 1, 3, 2, 4))
        qkv = qkv.reshape(width, 3 * local_width)
        rest = parts[1].reshape(dp, 2, 9, half, local_width)
        proj = jnp.transpose(rest[:, :, 0], (1, 2, 0, 3)).reshape(local_width, width)
        fc1 = jnp.transpose(rest[:, :, 1:5], (0, 1, 3, 2, 4)).reshape(width, 4 * local_width)
        fc2 = jnp.transpose(rest[:, :, 5:9], (2, 1, 3, 0, 4)).reshape(4 * local_width, width)
        weights.append((qkv, proj, fc1, fc2))

    def forward(layer, arriving):
        qkv, proj, fc1, fc2 = weights[layer]
        table = tables[layer]
        bias = lax.dynamic_slice_in_dim(table[6:12], part * local_width, local_width, 1)
        qkv_bias = jnp.concatenate([bias[0], jnp.zeros_like(bias[0]), bias[1]])
        fc1_bias = bias[2:6].reshape(4 * local_width)
        unit_one, inverse_one = normalise(arriving)
        normed = gather_tokens((unit_one * table[0] + table[1]).astype(narrow))
        projected = jnp.concatenate(
            [(dot(rows, qkv) + qkv_bias).astype(narrow) for rows in normed], axis=0
        )
        mixed, logs = attend(projected, local_width, scale)
        rows = mixed.shape[0] // 2
        middle = (
            arriving
            + scatter_tokens(lambda h: dot(mixed[h * rows : (h + 1) * rows], proj))
            + table[4]
        )
        unit_two, inverse_two = normalise(middle)
        second = gather_tokens((unit_two * table[2] + table[3]).astype(narrow))
        activated, slope = [], []
        for rows_in in second:
            hidden = dot(rows_in, fc1) + fc1_bias
            share = 0.5 * (1.0 + lax.erf(hidden * (0.5**0.5)))
            activated.append((hidden * share).astype(narrow))
            slope.append(share + hidden * jnp.exp(-0.5 * hidden * hidden) * 0.3989422804014327)
        leaving = middle + scatter_tokens(lambda h: dot(activated[h], fc2)) + table[5]
        kept = (
            unit_one, inverse_one, normed, projected, mixed, logs,
            unit_two, inverse_two, second, activated, slope,
        )
        return leaving.astype(narrow), kept

    def backward(layer, grad, kept):
        qkv, proj, fc1, fc2 = weights[layer]
        table = tables[layer]
        (
            unit_one, inverse_one, normed, projected, mixed, logs,
            unit_two, inverse_two, second, activated, slope,
        ) = kept
        down_grad = grad.astype(narrow)
        down = gather_tokens(down_grad)
        hidden_grad = [(dot_t(down[h], fc2) * slope[h]).astype(narrow) for h in range(2)]
        second_grad = scatter_tokens(lambda h: dot_t(hidden_grad[h], fc1))
        fc2_grad = t_dot(activated[0], down[0]) + t_dot(activated[1], down[1])
        fc1_grad = t_dot(second[0], hidden_grad[0]) + t_dot(second[1], hidden_grad[1])
        middle_grad = grad + norm_back(second_grad, table[2], unit_two, inverse_two)
        branch_grad = middle_grad.astype(narrow)
        branch = gather_tokens(branch_grad)
        mixed_grad = jnp.concatenate([dot_t(rows, proj).astype(narrow) for rows in branch], axis=0)
        rows = mixed.shape[0] // 2
        proj_grad = t_dot(mixed[:rows], branch[0]) + t_dot(mixed[rows:], branch[1])
        projected_grad = attend_back(projected, logs, mixed_grad, local_width, scale)
        normed_grad = scatter_tokens(
            lambda h: dot_t(projected_grad[h * rows : (h + 1) * rows], qkv)
        )
        qkv_grad = t_dot(normed[0], projected_grad[:rows]) + t_dot(normed[1], projected_grad[rows:])
        input_grad = middle_grad + norm_back(normed_grad, table[0], unit_one, inverse_one)

        def total(values):
            return jnp.sum(values.astype(wide), axis=0)

        projected_sums = total(projected_grad).reshape(3, local_width)
        hidden_sums = (total(hidden_grad[0]) + total(hidden_grad[1])).reshape(4, local_width)
        local_rows = jnp.concatenate([projected_sums[0:1], projected_sums[2:3], hidden_sums], axis=0)
        column = lax.broadcasted_iota(jnp.int32, (6, width), 1) // local_width
        placed = jnp.where(column == part, jnp.tile(local_rows, (1, width // local_width)), 0.0)
        shared = jnp.stack(
            [
                total(normed_grad * unit_one),
                total(normed_grad),
                total(second_grad * unit_two),
                total(second_grad),
                total(branch_grad),
                total(down_grad),
            ]
        )
        vector_grad = jnp.concatenate([shared, placed], axis=0)
        pieces = jnp.concatenate(
            [
                jnp.transpose(
                    qkv_grad.astype(narrow).reshape(dp, 2, half, 3, local_width), (0, 1, 3, 2, 4)
                ),
                jnp.transpose(
                    proj_grad.astype(narrow).reshape(1, 2, half, dp, local_width), (3, 1, 0, 2, 4)
                ),
                jnp.transpose(
                    fc1_grad.astype(narrow).reshape(dp, 2, half, 4, local_width), (0, 1, 3, 2, 4)
                ),
                jnp.transpose(
                    fc2_grad.astype(narrow).reshape(4, 2, half, dp, local_width), (3, 1, 0, 2, 4)
                ),
            ],
            axis=2,
        ).reshape(dp * 2, 12, half, local_width)
        owned = lax.psum_scatter(pieces, ("dp", "ylo"), scatter_dimension=0, tiled=False)
        return input_grad, vector_grad, owned

    left_zero, kept_zero = forward(0, entering.astype(wide))
    left_one, kept_one = forward(1, left_zero.astype(wide))
    grad_one, vector_one, owned_one = backward(1, final_grad.astype(wide), kept_one)
    grad_zero, vector_zero, owned_zero = backward(
        0, grad_one.astype(narrow).astype(wide), kept_zero
    )

    mine = jnp.where(low == 0, owned_zero, owned_one)
    other = jnp.where(low == 0, owned_one, owned_zero)
    got_mine, got_other = turn_back(mine, 0), turn_back(other, 1)
    lower = jnp.where(core == 0, got_mine, got_other)
    upper = jnp.where(core == 0, got_other, got_mine)
    blocks = jnp.concatenate([lower, upper], axis=1).astype(wide)

    vector_sum = jnp.where(core == 0, vector_zero, vector_one) + swap_cores(
        jnp.where(core == 0, vector_one, vector_zero)
    )
    for axis in ("x", "ylo", "dp"):
        arrived = [along(vector_sum, axis, k) for k in range(1, lax.axis_size(axis))]
        for piece in arrived:
            vector_sum = vector_sum + piece
    vector_owned = lax.dynamic_slice_in_dim(vector_sum, place * 16, 16, 1)

    def spread(zero, one):
        a = turn(jnp.where(low == 0, zero, one), 0)
        b = turn_back(jnp.where(low == 0, one, zero), 1)
        return jnp.stack([jnp.where(core == 0, a, b), jnp.where(core == 0, b, a)])[None, :, :, None]

    return (
        spread(left_zero, left_one),
        spread(grad_zero, grad_one),
        jnp.transpose(blocks[0:3], (1, 0, 2))[None],
        blocks[3][None],
        jnp.transpose(blocks[4:8], (1, 0, 2))[None],
        blocks[8:12][None],
        vector_owned[None],
    )


def solution(mesh):
    fine = Mesh(mesh.devices.reshape(2, 8, 2, 4), ("core", "dp", "ylo", "x"))
    tensor = ("ylo", "x")
    in_specs = (
        P(None, tensor, "dp", None),
        P(None, tensor, "dp", None),
        P("core", "dp", None, tensor),
        P("core", tensor, "dp"),
        P("core", "dp", None, tensor),
        P("core", None, tensor, "dp"),
        P("core", None, ("dp",) + tensor),
    )
    out_specs = (
        P("core", None, tensor, "dp", None),
        P("core", None, tensor, "dp", None),
        P("core", "dp", None, tensor),
        P("core", tensor, "dp"),
        P("core", "dp", None, tensor),
        P("core", None, tensor, "dp"),
        P("core", None, ("dp",) + tensor),
    )
    return jax.shard_map(
        per_device, mesh=fine, in_specs=in_specs, out_specs=out_specs, check_vma=False
    )
```

```python
import functools

import jax
import jax.numpy as jnp
from jax import lax
from jax.experimental import pallas as pl
from jax.experimental.pallas import tpu as pltpu
from jax.sharding import Mesh, PartitionSpec as P

HDIM = 64
SCALE = HDIM ** (-0.5)

eps = 1e-06
wide = jnp.float32
narrow = jnp.bfloat16


RING = ("yhi", "ylo")


def swap_cores(value):
    return lax.ppermute(value, "core", [(0, 1), (1, 0)])


def along(value, axis, steps):
    count = lax.axis_size(axis)
    return lax.ppermute(value, axis, [(i, (i + steps) % count) for i in range(count)])


def around(value, axis):
    return [along(value, axis, -k) for k in range(1, lax.axis_size(axis))]


def turn(value, flip):
    pairs = [(c * 2 + y, y * 2 + (c ^ flip)) for c in range(2) for y in range(2)]
    return lax.ppermute(value, ("core", "ylo"), pairs)


def turn_back(value, flip):
    pairs = [(c * 2 + y, (y ^ flip) * 2 + c) for c in range(2) for y in range(2)]
    return lax.ppermute(value, ("core", "ylo"), pairs)


def gather_tokens(rows, *others):
    mine = [rows] + around(rows, "x")
    mine[-1], *others = lax.optimization_barrier((mine[-1], *others))
    blocks = mine + [swap_cores(block) for block in mine]
    return (blocks, *others) if others else blocks


def normalise(rows):
    center = rows - jnp.mean(rows, axis=-1, keepdims=True)
    spread = jnp.mean(center * center, axis=-1, keepdims=True)
    inverse = lax.rsqrt(spread + eps)
    return center * inverse, inverse


def norm_back(grad, gain, unit, inverse):
    pulled = grad * gain
    mean_one = jnp.mean(pulled, axis=-1, keepdims=True)
    mean_two = jnp.mean(pulled * unit, axis=-1, keepdims=True)
    return inverse * (pulled - mean_one - unit * mean_two)


def dot(a, b):
    return jnp.dot(a, b, preferred_element_type=wide)


def dot_t(a, b):
    return lax.dot_general(a, b, (((1,), (1,)), ((), ())), preferred_element_type=wide)


def t_dot(a, b):
    return lax.dot_general(a, b, (((0,), (0,)), ((), ())), preferred_element_type=wide)


def whole(refs):
    return jnp.concatenate([ref[...].astype(wide) for ref in refs], axis=0)


def column_sums(values):
    return jnp.sum(values, axis=0, keepdims=True)


def my_part():
    return lax.axis_index("core") * lax.axis_size("x") + lax.axis_index("x")


def my_columns(table, row, size):
    start = pl.multiple_of(my_part() * size, size)
    return table[row : row + 1, pl.ds(start, size)]


class Fetch:
    def __init__(self, layer, source, start, held, semaphore):
        self.held = held
        columns = source.at[layer, :, lax.axis_index("core"), :, pl.ds(start, held.shape[-1])]
        self.copy = pltpu.make_async_copy(columns, held, semaphore)
        self.copy.start()

    def __getitem__(self, key):
        if self.copy is not None:
            self.copy.wait()
            self.copy = None
        part = self.held[:, :, key[1]]
        return part.reshape(-1, part.shape[-1])


def pack_kernel(qkv, proj, fc1, fc2, attention, packed):
    size = proj.shape[1]
    turned = proj[...].astype(wide).T.astype(narrow)
    attention[:, : 3 * size] = qkv[...]
    attention[:, 3 * size :] = turned
    packed[:, : 3 * size] = qkv[...]
    packed[:, 3 * size : 4 * size] = turned
    packed[:, 4 * size : 8 * size] = fc1[...]
    for k in range(4):
        packed[:, (8 + k) * size : (9 + k) * size] = fc2[k].astype(wide).T.astype(narrow)


def mlp_grad_kernel(kept, back, grads):
    width, columns = grads.shape[0], grads.shape[1] // 2
    grads[:, :columns] = t_dot(kept[:, :width], back[:, width:]).astype(narrow)
    grads[:, columns:] = t_dot(back[:, :width], kept[:, width : width + columns]).astype(narrow)


def attention_grad_kernel(kept, back, grads):
    width, local = grads.shape[0], grads.shape[1] // 4
    grads[:, : 3 * local] = t_dot(kept[:, :width], back[:, width:]).astype(narrow)
    grads[:, 3 * local :] = t_dot(back[:, :width], kept[:, width + 3 * local :]).astype(narrow)


def ring_kernel(mine, other, own, *pieces):
    total = mine[...] + other[...].astype(wide)
    rows = own.shape[0]
    own[...] = total[:rows]
    for k, piece in enumerate(pieces):
        piece[...] = total[(k + 1) * rows : (k + 2) * rows].astype(narrow)


def summed(refs):
    total = refs[0][...]
    for piece in refs[1:]:
        total = total + piece[...].astype(wide)
    return total


def middle_kernel(own, one, two, three, arriving, table, middle, second):
    total = arriving[...].astype(wide) + summed((own, one, two, three)) + table[4:5, :]
    middle[...] = total
    second[...] = (normalise(total)[0] * table[2:3, :] + table[3:4, :]).astype(narrow)


def leave_kernel(own, one, two, three, middle, table, *refs):
    left = (middle[...] + summed((own, one, two, three)) + table[5:6, :]).astype(narrow)
    if len(refs) == 1:
        refs[0][...] = left
    else:
        following, leaving, normed = refs
        leaving[...] = left
        unit = normalise(left.astype(wide))[0]
        normed[...] = (unit * following[0:1, :] + following[1:2, :]).astype(narrow)


def middle_back_kernel(own, one, two, three, grad, middle, table, middle_grad, branch_grad, sums):
    second_grad = summed((own, one, two, three))
    unit, inverse = normalise(middle[...])
    arriving = grad[...].astype(wide)
    total = arriving + norm_back(second_grad, table[2:3, :], unit, inverse)
    middle_grad[...] = total
    branch = total.astype(narrow)
    branch_grad[...] = branch
    sums[0:1, :] = column_sums(second_grad * unit)
    sums[1:2, :] = column_sums(second_grad)
    sums[2:3, :] = column_sums(branch.astype(wide))
    sums[3:4, :] = column_sums(arriving)


def input_back_kernel(own, one, two, three, middle_grad, arriving, table, grad, down_grad, sums):
    normed_grad = summed((own, one, two, three))
    unit, inverse = normalise(arriving[...].astype(wide))
    total = middle_grad[...] + norm_back(normed_grad, table[0:1, :], unit, inverse)
    grad[...] = total
    down_grad[...] = total.astype(narrow)
    sums[0:1, :] = column_sums(normed_grad * unit)
    sums[1:2, :] = column_sums(normed_grad)


def attend_kernel(layer, *refs):
    blocks, (matrix, table, kept, part_mine, part_other, *fetch) = refs[:8], refs[8:]
    rows, width, local = kept.shape[0], part_mine.shape[1], 2 * HDIM
    half = rows // 2
    if layer == 1:
        matrix = Fetch(layer, matrix, 0, *fetch)
    if layer == 0:
        unit = normalise(whole(blocks))[0]
        kept[:, width + 4 * local :] = unit.astype(narrow)
        kept[:, :width] = (unit * table[0:1, :] + table[1:2, :]).astype(narrow)
    else:
        kept[:, :width] = whole(blocks).astype(narrow)
    query_bias, value_bias = my_columns(table, 6, local), my_columns(table, 7, local)
    bias = jnp.concatenate([query_bias, jnp.zeros_like(query_bias), value_bias], axis=1)
    projected = (dot(kept[:, :width], matrix[:, : 3 * local]) + bias).astype(narrow)
    kept[:, width : width + 3 * local] = projected
    queries = projected[:, :local]
    key_rows = projected[:, local : 2 * local]
    value_rows = projected[:, 2 * local :]
    lower = lax.broadcasted_iota(jnp.int32, (rows, local), 1) < HDIM
    outs = []
    for keep in (lower, ~lower):
        scores = dot_t(jnp.where(keep, queries, jnp.zeros_like(queries)), key_rows) * SCALE
        raised = jnp.exp(scores - jnp.max(scores, axis=-1, keepdims=True))
        probs = raised * (1.0 / jnp.sum(raised, axis=-1, keepdims=True))
        outs.append(dot(probs.astype(narrow), value_rows))
    mixed = jnp.where(lower, outs[0], outs[1]).astype(narrow)
    kept[:, width + 3 * local : width + 4 * local] = mixed
    proj = matrix[:, 3 * local : 4 * local]
    part_other[...] = dot_t(mixed[half:, :], proj).astype(narrow)
    part_mine[...] = dot_t(mixed[:half, :], proj)


def attend_back_kernel(layer, *refs):
    blocks, (kept, matrix, *refs) = refs[:8], refs[8:]
    local = 2 * HDIM
    rows, width = kept.shape[0], kept.shape[1] - 4 * local
    if layer == 0:
        width = width // 2
    half = rows // 2
    if layer == 0:
        vectors, (part_mine, part_other, *slabs, back) = refs[:6], refs[6:]
    else:
        back, sums, part_mine, part_other, *fetch = refs
        matrix = Fetch(layer, matrix, 0, *fetch)
    back[:, :width] = whole(blocks).astype(narrow)
    out = dot(back[:, :width], matrix[:, 3 * local : 4 * local]).astype(narrow)
    queries = kept[:, width : width + local]
    key_rows = kept[:, width + local : width + 2 * local]
    value_rows = kept[:, width + 2 * local : width + 3 * local]
    lower = lax.broadcasted_iota(jnp.int32, (rows, local), 1) < HDIM
    query_grads, key_grad, value_grad = [], 0.0, 0.0
    for keep in (lower, ~lower):
        query = jnp.where(keep, queries, jnp.zeros_like(queries))
        grad = jnp.where(keep, out, jnp.zeros_like(out))
        scores = dot_t(query, key_rows) * SCALE
        raised = jnp.exp(scores - jnp.max(scores, axis=-1, keepdims=True))
        probs = raised * (1.0 / jnp.sum(raised, axis=-1, keepdims=True))
        prob_grad = dot_t(grad, value_rows)
        inner = jnp.sum(probs * prob_grad, axis=-1, keepdims=True)
        score_grad = (probs * (prob_grad - inner)).astype(narrow)
        query_grads.append(dot(score_grad, key_rows))
        value_grad = value_grad + t_dot(probs.astype(narrow), grad)
        key_grad = key_grad + t_dot(score_grad, query)
    back[:, width : width + local] = (jnp.where(lower, query_grads[0], query_grads[1]) * SCALE).astype(narrow)
    back[:, width + local : width + 2 * local] = (key_grad * SCALE).astype(narrow)
    back[:, width + 2 * local :] = value_grad.astype(narrow)
    projected_sums = column_sums(back[:, width:].astype(wide))
    qkv = matrix[:, : 3 * local]
    other = dot_t(back[half:, width:], qkv)
    mine = dot_t(back[:half, width:], qkv)
    part_other[...] = other.astype(narrow)
    part_mine[...] = mine
    if layer == 1:
        sums[...] = projected_sums
        return
    first_unit = width + 4 * local
    gain_sum = column_sums(mine * kept[:half, first_unit:].astype(wide))
    gain_sum += column_sums(other * kept[half:, first_unit:].astype(wide))
    shift_sum = column_sums(mine) + column_sums(other)
    column = lax.broadcasted_iota(jnp.int32, (1, width), 1) // local

    def rows_of(norm_sums, middle_sums, projected, hidden):
        found = [norm_sums, middle_sums]
        for values, k in ((projected, 0), (projected, 2), (hidden, 0), (hidden, 1), (hidden, 2), (hidden, 3)):
            row = jnp.concatenate([values[:, k * local : (k + 1) * local]] * (width // local), axis=1)
            found.append(jnp.where(column == my_part(), row, 0.0))
        return jnp.concatenate(found + [jnp.zeros((4, width), wide)], axis=0).astype(narrow)

    sums_zero, hidden_zero, norm_one, sums_one, projected_one, hidden_one = (ref[...] for ref in vectors)
    norm_zero = jnp.concatenate([gain_sum, shift_sum], axis=0)
    rows_zero = rows_of(norm_zero, sums_zero, projected_sums, hidden_zero)
    rows_one = rows_of(norm_one, sums_one, projected_one, hidden_one)
    count = len(slabs)
    size = width // count
    here = lax.axis_index("z")
    for k, slab in enumerate(slabs):
        first = pl.multiple_of(lax.rem(here + k, count) * size, size)
        normed = kept[:, pl.ds(first, size)]
        branch = back[:, pl.ds(first, size)]
        slab[:size, : 3 * local] = t_dot(normed, back[:, width:]).astype(narrow)
        slab[:size, 3 * local :] = t_dot(branch, kept[:, width + 3 * local : width + 4 * local]).astype(narrow)
    for k, slab in enumerate(slabs):
        for z in range(count):

            @pl.when(lax.rem(here + k, count) == z)
            def _():
                slab[size:, :size] = rows_zero[:, z * size : (z + 1) * size]
                slab[size:, size:] = rows_one[:, z * size : (z + 1) * size]


def hidden_parts(second, fc1, table):
    local = fc1.shape[1] // 4
    bias = jnp.concatenate([my_columns(table, 8 + r, local) for r in range(4)], axis=1)
    hidden = dot(second, fc1) + bias
    share = 0.5 * (1.0 + lax.erf(hidden * (0.5**0.5)))
    slope = share + hidden * jnp.exp(-0.5 * hidden * hidden) * 0.3989422804014327
    return (hidden * share).astype(narrow), slope


def mlp_kernel(*refs):
    blocks, (matrix, table, kept, part_mine, part_other, *fetch) = refs[:8], refs[8:]
    width, columns, half = part_mine.shape[1], fetch[0].shape[2] // 2, kept.shape[0] // 2
    matrix = Fetch(0, matrix, columns, *fetch)
    kept[:, :width] = whole(blocks).astype(narrow)
    activated, slope = hidden_parts(kept[:, :width], matrix[:, :columns], table)
    kept[:, width : width + columns] = activated
    kept[:, width + columns :] = slope.astype(narrow)
    part_other[...] = dot_t(activated[half:, :], matrix[:, columns:]).astype(narrow)
    part_mine[...] = dot_t(activated[:half, :], matrix[:, columns:])


def mlp_back_kernel(*refs):
    blocks, (kept, matrix, back, sums, part_mine, part_other, *fetch) = refs[:8], refs[8:]
    width, columns, half = part_mine.shape[1], fetch[0].shape[2] // 2, kept.shape[0] // 2
    matrix = Fetch(0, matrix, columns, *fetch)
    back[:, :width] = whole(blocks).astype(narrow)
    slope = kept[:, width + columns :].astype(wide)
    hidden_grad = (dot(back[:, :width], matrix[:, columns:]) * slope).astype(narrow)
    back[:, width:] = hidden_grad
    sums[...] = column_sums(hidden_grad.astype(wide))
    part_other[...] = dot_t(hidden_grad[half:, :], matrix[:, :columns]).astype(narrow)
    part_mine[...] = dot_t(hidden_grad[:half, :], matrix[:, :columns])


def mlp_both_kernel(*refs):
    blocks, final, (matrix, table, kept, back, sums, part_mine, part_other, *fetch) = refs[:8], refs[8:16], refs[16:]
    width, columns, half = part_mine.shape[1], fetch[0].shape[2] // 2, kept.shape[0] // 2
    matrix = Fetch(1, matrix, columns, *fetch)
    kept[:, :width] = whole(blocks).astype(narrow)
    back[:, :width] = whole(final).astype(narrow)
    activated, slope = hidden_parts(kept[:, :width], matrix[:, :columns], table)
    kept[:, width:] = activated
    hidden_grad = (dot(back[:, :width], matrix[:, columns:]) * slope).astype(narrow)
    back[:, width:] = hidden_grad
    sums[...] = column_sums(hidden_grad.astype(wide))
    part_other[...] = dot_t(hidden_grad[half:, :], matrix[:, :columns]).astype(narrow)
    part_mine[...] = dot_t(hidden_grad[:half, :], matrix[:, :columns])


def down_kernel(kept, matrix, part_mine, part_other, *fetch):
    width, columns, half = part_mine.shape[1], fetch[0].shape[2] // 2, kept.shape[0] // 2
    matrix = Fetch(1, matrix, columns, *fetch)
    part_other[...] = dot_t(kept[half:, width:], matrix[:, columns:]).astype(narrow)
    part_mine[...] = dot_t(kept[:half, width:], matrix[:, columns:])


def call(body, flops, outs, args, scratch=(), fetch=None, columns=None):
    specs = [pl.BlockSpec()] * len(args)
    scratch = list(scratch)
    if fetch is not None:
        shape = args[fetch].shape
        specs[fetch] = pl.BlockSpec(memory_space=pl.ANY)
        scratch += [pltpu.VMEM((shape[1], shape[3], columns), narrow), pltpu.SemaphoreType.DMA]
    return pl.pallas_call(
        body,
        out_shape=[jax.ShapeDtypeStruct(shape, kind) for shape, kind in outs],
        in_specs=specs,
        scratch_shapes=scratch,
        compiler_params=pltpu.CompilerParams(vmem_limit_bytes=48 << 20),
        cost_estimate=pl.CostEstimate(flops=flops, bytes_accessed=8 << 20, transcendentals=0),
    )(*args)


def partials(rows, width):
    return [((rows // 2, width), wide), ((rows // 2, width), narrow)]


def attend(layer, blocks, matrix, table):
    rows, width, columns = 8 * blocks[0].shape[0], blocks[0].shape[1], 8 * HDIM
    outs = [((rows, width + columns + width * (layer == 0)), narrow)] + partials(rows, width)
    body = functools.partial(attend_kernel, layer)
    fetch = (8, columns) if layer else (None, None)
    return call(body, 3 * 10**9, outs, [*blocks, matrix, table], (), *fetch)


def attend_back(layer, blocks, kept, matrix, vectors=()):
    rows, width, columns = kept.shape[0], blocks[0].shape[1], 8 * HDIM
    back = (rows, width + columns // 4 * 3)
    if layer == 0:
        count = lax.axis_size("z")
        outs = partials(rows, width) + [((width // count + 16, columns), narrow)] * count
        scratch = [pltpu.VMEM(back, narrow)]
    else:
        outs = [(back, narrow), ((1, columns // 4 * 3), wide)] + partials(rows, width)
        scratch = []
    body = functools.partial(attend_back_kernel, layer)
    fetch = (9, columns) if layer else (None, None)
    return call(body, 6 * 10**9, outs, [*blocks, kept, matrix, *vectors], scratch, *fetch)


def mlp(blocks, matrix, table):
    rows, width, columns = 8 * blocks[0].shape[0], blocks[0].shape[1], matrix.shape[4] // 3
    outs = [((rows, width + 2 * columns), narrow)] + partials(rows, width)
    return call(mlp_kernel, 4 * 10**9, outs, [*blocks, matrix, table], (), 8, 2 * columns)


def mlp_back(blocks, kept, matrix):
    rows, width, columns = kept.shape[0], blocks[0].shape[1], matrix.shape[4] // 3
    outs = [((rows, width + columns), narrow), ((1, columns), wide)] + partials(rows, width)
    return call(mlp_back_kernel, 4 * 10**9, outs, [*blocks, kept, matrix], (), 9, 2 * columns)


def mlp_both(blocks, final, matrix, table):
    rows, width, columns = 8 * blocks[0].shape[0], blocks[0].shape[1], matrix.shape[4] // 3
    outs = [((rows, width + columns), narrow)] * 2 + [((1, columns), wide)] + partials(rows, width)
    return call(mlp_both_kernel, 6 * 10**9, outs, [*blocks, *final, matrix, table], (), 16, 2 * columns)


def down(kept, matrix):
    outs = partials(kept.shape[0], matrix.shape[1] * matrix.shape[3])
    return call(down_kernel, 10**9, outs, [kept, matrix], (), 1, matrix.shape[4] // 3 * 2)


def pack(qkv, proj, fc1, fc2):
    rows, size = proj.shape
    outs = [((rows, 4 * size), narrow), ((rows, 12 * size), narrow)]
    return call(pack_kernel, 10**8, outs, [qkv, proj, fc1, fc2])


def ring_sums(mine, other):
    count = lax.axis_size("x")
    shape = (mine.shape[0] // count, mine.shape[1])
    outs = [(shape, wide)] + [(shape, narrow)] * (count - 1)
    return call(ring_kernel, 10**8, outs, [mine, other])


def around_pieces(sums):
    return [sums[0]] + [along(piece, "x", k) for k, piece in enumerate(sums[1:], 1)]


def ring_pieces(mine, other):
    return around_pieces(ring_sums(mine, other))


def middle_of(terms, arriving, table):
    shape = arriving.shape
    return call(middle_kernel, 10**8, [(shape, wide), (shape, narrow)], [*terms, arriving, table])


def leave(terms, middle, table, following=None):
    outs = [(middle.shape, narrow)] * (1 if following is None else 2)
    args = [*terms, middle, table] + ([] if following is None else [following])
    return call(leave_kernel, 10**8, outs, args)


def middle_back(terms, grad, middle, table):
    shape = middle.shape
    outs = [(shape, wide), (shape, narrow), ((4, shape[1]), wide)]
    return call(middle_back_kernel, 10**8, outs, [*terms, grad, middle, table])


def input_back(terms, middle_grad, arriving, table):
    shape = arriving.shape
    outs = [(shape, wide), (shape, narrow), ((2, shape[1]), wide)]
    return call(input_back_kernel, 10**8, outs, [*terms, middle_grad, arriving, table])


def mlp_grad(kept, back, shape):
    return call(mlp_grad_kernel, 2 * 10**9, [(shape, narrow)], [kept, back])[0]


def attention_grad(kept, back, shape):
    return call(attention_grad_kernel, 10**9, [(shape, narrow)], [kept, back])[0]


def tie(*values):
    return lax.optimization_barrier(values)


def hop(columns, layer):
    return lax.ppermute(columns, ("core", "ylo"), [(layer * 2, 0), (layer * 2 + 1, 3)])


def order_ring(own, arrived):
    core, high, low = (lax.axis_index(name) for name in ("core", "yhi", "ylo"))
    one, two, three = arrived
    holder = low == core
    a = jnp.where(holder, own, one)
    b = jnp.where(holder, two, three)
    place = high * 2 + low
    a_first = jnp.where(holder, high, (place + 1) % 4 // 2) == 0
    return jnp.concatenate([jnp.where(a_first, a, b), jnp.where(a_first, b, a)], axis=0)


def fold(zero, one):
    half = zero.shape[1] // 2
    return jnp.concatenate([zero[:, :half], zero[:, half:], one[:, :half], one[:, half:]], axis=0)


def unfold(rows):
    return [jnp.concatenate([rows[k : k + 12], rows[k + 12 : k + 24]], axis=1) for k in (0, 24)]


def per_device(inputs, cotangent, qkv_weight, proj_weight, fc1_weight, fc2_weight, vectors):
    width = inputs.shape[3]
    core = lax.axis_index("core")
    low = lax.axis_index("ylo")
    place = lax.axis_index(("z", "yhi", "ylo", "x"))
    local = qkv_weight.shape[3]
    own_rows = qkv_weight.shape[1]

    def added(values, arrived):
        return functools.reduce(lambda a, b: a + b, arrived, values)

    columns = lax.broadcasted_iota(jnp.int32, (12, width), 1) // 16
    table = jnp.where(columns == place, jnp.tile(vectors[0], (1, width // 16)), 0).astype(narrow)
    other_table = swap_cores(table)
    table = fold(jnp.where(core == 0, table, other_table), jnp.where(core == 0, other_table, table))
    attention_raw, raw = pack(
        qkv_weight[0].reshape(own_rows, 3 * local),
        proj_weight[0],
        fc1_weight[0].reshape(own_rows, 4 * local),
        fc2_weight[0],
    )
    table, attention_raw, raw = tie(table, attention_raw, raw)
    held = hop(attention_raw, 0)
    entering = turn(lax.dynamic_index_in_dim(inputs, core, 0, keepdims=False)[:, 0], 0)
    table = added(table, around(table, "x"))
    held, entering, table = tie(held, entering, table)
    mine = [entering] + around(entering, "x")
    arrived = around(jnp.concatenate([held, table], axis=0), RING)
    *arrived, raw = tie(*arrived, raw)
    blocks = order_ring(held, [piece[:own_rows] for piece in arrived])
    table = added(table, [piece[own_rows:] for piece in arrived])

    def gather_weights(rows):
        gathered = lax.all_gather(rows, ("core", "z", "yhi", "ylo"), axis=0, tiled=True)
        return gathered.reshape(2, 8, 2, own_rows, rows.shape[1])

    everything = gather_weights(raw)

    arrived = around(jnp.concatenate([blocks, table], axis=0), "z")
    entering_all = mine + [swap_cores(block) for block in mine]
    parts = [blocks] + [piece[: 2 * own_rows] for piece in arrived]
    start = (len(parts) - 1 - lax.axis_index("z")) * 2 * own_rows
    first = lax.dynamic_slice_in_dim(jnp.concatenate(parts[1:] + parts, axis=0), start, width, 0)
    tables = [t.astype(wide) for t in unfold(added(table, [piece[2 * own_rows :] for piece in arrived]))]

    def offload_sum(value, axis):
        return lax.psum_scatter(value, axis, scatter_dimension=0, tiled=True)

    kept_zero, mine, other = attend(0, entering_all, first, tables[0])
    terms = ring_pieces(mine, swap_cores(other))
    middle_zero, second = middle_of(terms, entering, tables[0])
    mlp_kept_zero, mine, other = mlp(gather_tokens(second), everything, tables[0])

    terms = ring_pieces(mine, swap_cores(other))

    *terms, cotangent = tie(*terms, cotangent)
    final_all = lax.all_gather(
        lax.dynamic_index_in_dim(cotangent, core, 0, keepdims=False)[:, 0], ("core", "ylo", "x")
    )
    final_all = final_all.reshape((2, 2, 4) + entering.shape)
    left_zero, normed = leave(terms, middle_zero, tables[0], tables[1])
    kept_one, mine, other = attend(1, gather_tokens(normed), everything, tables[1])
    terms = ring_pieces(mine, swap_cores(other))
    final_blocks = []
    for which in (core, 1 - core):
        for k in range(4):
            spot = (low, which, (lax.axis_index("x") + k) % 4, 0, 0)
            piece = lax.dynamic_slice(final_all, spot, (1, 1, 1) + entering.shape)
            final_blocks.append(piece.reshape(entering.shape))
    tied = tie(*terms, *final_blocks)
    terms, final_blocks = tied[:4], tied[4:]
    middle_one, second = middle_of(terms, left_zero, tables[1])

    mlp_kept_one, back, hidden_one, mine, other = mlp_both(
        gather_tokens(second), final_blocks, everything, tables[1]
    )
    other = swap_cores(other)
    mlp_one = mlp_grad(mlp_kept_one, back, (width, 8 * local))
    other, mlp_one = tie(other, mlp_one)
    terms = ring_pieces(mine, other)
    left_mine, left_other = down(mlp_kept_one, everything)
    left_pieces = ring_sums(left_mine, swap_cores(left_other))
    *terms, mlp_one = tie(*terms, mlp_one)
    mlp_one = offload_sum(mlp_one, "z")
    middle_grad, branch_grad, sums_one = middle_back(terms, final_blocks[0], middle_one, tables[1])
    blocks, *left_pieces = gather_tokens(branch_grad, *left_pieces)
    left_terms = around_pieces(left_pieces)
    back, projected_one, mine, other = attend_back(1, blocks, kept_one, everything)
    other, *left_terms = tie(other, *left_terms)
    other = swap_cores(other)
    attention_one = attention_grad(kept_one, back, (width, 4 * local))
    other, attention_one = tie(other, attention_one)
    terms = ring_pieces(mine, other)
    *terms, attention_one, mlp_one = tie(*terms, attention_one, mlp_one)
    mlp_one = offload_sum(mlp_one, RING)
    attention_one = offload_sum(attention_one, "z")
    grad_one, down_grad, norm_one = input_back(terms, middle_grad, left_zero, tables[1])

    blocks = gather_tokens(down_grad)
    (left_one,) = leave(left_terms, middle_one, tables[1])
    back, hidden_zero, mine, other = mlp_back(blocks, mlp_kept_zero, everything)
    other = swap_cores(other)
    mlp_zero = mlp_grad(mlp_kept_zero, back, (width, 8 * local))
    other, mlp_zero = tie(other, mlp_zero)
    terms = ring_pieces(mine, other)

    def spread(zero, one):
        a = turn_back(jnp.where(low == 0, zero, one), 0)
        b = turn_back(jnp.where(low == 0, one, zero), 1)
        return a, b

    def in_order(a, b):
        return jnp.stack([jnp.where(core == 0, a, b), jnp.where(core == 0, b, a)])[None, :, :, None]

    activations = spread(left_zero, left_one)
    tied = tie(*terms, mlp_zero, mlp_one, *activations)
    terms, mlp_zero, mlp_one, activations = tied[:4], tied[4], tied[5], tied[6:]
    mlp_zero = offload_sum(mlp_zero, "z")
    middle_grad, branch_grad, sums_zero = middle_back(terms, down_grad, middle_zero, tables[0])
    vectors = [sums_zero, hidden_zero, norm_one, sums_one, projected_one, hidden_one]

    mine, other, *slabs = attend_back(0, gather_tokens(branch_grad), kept_zero, first, vectors)

    sent = [along(slab, "z", k) for k, slab in enumerate(slabs) if k > 0]
    sums = ring_sums(mine, swap_cores(other))
    terms = around_pieces(sums)
    terms[0], mlp_zero, attention_one = tie(terms[0], mlp_zero, attention_one)
    bulk = offload_sum(jnp.concatenate([attention_one, mlp_zero], axis=1), RING)
    slab = added(slabs[0].astype(wide), [piece.astype(wide) for piece in sent]).astype(narrow)
    slab, *terms = tie(slab, *terms)
    grad_zero, _, _ = input_back(terms, middle_grad, entering, tables[0])
    count, rows = lax.axis_size(RING), own_rows // 2
    turn_rows = lax.axis_index(RING) * rows

    def ring_slab(k):
        start = (turn_rows + k * rows) % (count * rows)
        return jnp.concatenate(
            [lax.dynamic_slice_in_dim(slab, start, rows, 0), slab[count * rows :]], axis=0
        )

    sent = [along(ring_slab(k), RING, k) for k in range(1, count)]
    sent[0], grad_zero = tie(sent[0], grad_zero)
    input_grads = spread(grad_zero, grad_one)
    slab = added(ring_slab(0).astype(wide), [piece.astype(wide) for piece in sent])
    slab, *input_grads = tie(slab, *input_grads)

    owned_zero = jnp.concatenate([slab[:rows].astype(narrow), bulk[:, 4 * local :]], axis=1)
    owned_one = jnp.concatenate([bulk[:, : 4 * local], mlp_one], axis=1)
    got_mine = turn_back(jnp.where(low == 0, owned_zero, owned_one), 0)
    got_other = turn_back(jnp.where(low == 0, owned_one, owned_zero), 1)
    vector_sum = slab[rows:]
    vector_sum = added(vector_sum, around(vector_sum, "x"))
    vector_sum, got_mine, got_other = tie(vector_sum, got_mine, got_other)
    vector_zero, vector_one = vector_sum[:, : 2 * local], vector_sum[:, 2 * local :]
    vector_sum = jnp.where(core == 0, vector_zero, vector_one) + swap_cores(
        jnp.where(core == 0, vector_one, vector_zero)
    )
    start = turn_rows + lax.axis_index("x") * 16
    vector_owned = lax.dynamic_slice_in_dim(vector_sum[:12], start, 16, 1)
    lower = jnp.where(core == 0, got_mine, got_other)
    upper = jnp.where(core == 0, got_other, got_mine)
    owned = jnp.concatenate([lower, upper], axis=0).astype(wide)

    return (
        in_order(*activations),
        in_order(*input_grads),
        owned[:, : 3 * local].reshape(1, own_rows, 3, local),
        owned[:, 3 * local : 4 * local].T[None],
        owned[:, 4 * local : 8 * local].reshape(1, own_rows, 4, local),
        jnp.transpose(owned[:, 8 * local :].reshape(own_rows, 4, local), (1, 2, 0))[None],
        vector_owned[None],
    )


def solution(mesh):
    fine = Mesh(mesh.devices.reshape(2, 4, 2, 2, 4), ("core", "z", "yhi", "ylo", "x"))
    tensor = ("ylo", "x")
    dp = ("z", "yhi")
    in_specs = (
        P(None, tensor, dp, None),
        P(None, tensor, dp, None),
        P("core", dp, None, tensor),
        P("core", tensor, dp),
        P("core", dp, None, tensor),
        P("core", None, tensor, dp),
        P("core", None, dp + tensor),
    )
    out_specs = (
        P("core", None, tensor, dp, None),
        P("core", None, tensor, dp, None),
        P("core", dp, None, tensor),
        P("core", tensor, dp),
        P("core", dp, None, tensor),
        P("core", None, tensor, dp),
        P("core", None, dp + tensor),
    )
    return jax.shard_map(
        per_device, mesh=fine, in_specs=in_specs, out_specs=out_specs, check_vma=False
    )
```

```python
import functools

import jax
import jax.numpy as jnp
from jax import lax
from jax.experimental import pallas as pl
from jax.experimental.pallas import tpu as pltpu
from jax.sharding import Mesh, PartitionSpec as P

HDIM = 64
SCALE = HDIM ** (-0.5)

eps = 1e-06
wide = jnp.float32
narrow = jnp.bfloat16


RING = ("yhi", "ylo")


def swap_cores(value):
    return lax.ppermute(value, "core", [(0, 1), (1, 0)])


def along(value, axis, steps):
    count = lax.axis_size(axis)
    return lax.ppermute(value, axis, [(i, (i + steps) % count) for i in range(count)])


def around(value, axis):
    return [along(value, axis, -k) for k in range(1, lax.axis_size(axis))]


def turn(value, flip):
    pairs = [(c * 2 + y, y * 2 + (c ^ flip)) for c in range(2) for y in range(2)]
    return lax.ppermute(value, ("core", "ylo"), pairs)


def turn_back(value, flip):
    pairs = [(c * 2 + y, (y ^ flip) * 2 + c) for c in range(2) for y in range(2)]
    return lax.ppermute(value, ("core", "ylo"), pairs)


def gather_tokens(rows, *others):
    mine = [rows] + around(rows, "x")
    mine[-1], *others = lax.optimization_barrier((mine[-1], *others))
    blocks = mine + [swap_cores(block) for block in mine]
    return (blocks, *others) if others else blocks


def normalise(rows):
    center = rows - jnp.mean(rows, axis=-1, keepdims=True)
    spread = jnp.mean(center * center, axis=-1, keepdims=True)
    inverse = lax.rsqrt(spread + eps)
    return center * inverse, inverse


def norm_back(grad, gain, unit, inverse):
    pulled = grad * gain
    mean_one = jnp.mean(pulled, axis=-1, keepdims=True)
    mean_two = jnp.mean(pulled * unit, axis=-1, keepdims=True)
    return inverse * (pulled - mean_one - unit * mean_two)


def dot(a, b):
    return jnp.dot(a, b, preferred_element_type=wide)


def dot_t(a, b):
    return lax.dot_general(a, b, (((1,), (1,)), ((), ())), preferred_element_type=wide)


def t_dot(a, b):
    return lax.dot_general(a, b, (((0,), (0,)), ((), ())), preferred_element_type=wide)


def whole(refs):
    return jnp.concatenate([ref[...].astype(wide) for ref in refs], axis=0)


def column_sums(values):
    return jnp.sum(values, axis=0, keepdims=True)


def my_part():
    return lax.axis_index("core") * lax.axis_size("x") + lax.axis_index("x")


def my_columns(table, row, size):
    start = pl.multiple_of(my_part() * size, size)
    return table[row : row + 1, pl.ds(start, size)]


class Fetch:
    def __init__(self, layer, source, start, held, semaphore):
        self.held = held
        columns = source.at[layer, :, lax.axis_index("core"), :, pl.ds(start, held.shape[-1])]
        self.copy = pltpu.make_async_copy(columns, held, semaphore)
        self.copy.start()

    def __getitem__(self, key):
        if self.copy is not None:
            self.copy.wait()
            self.copy = None
        part = self.held[:, :, key[1]]
        return part.reshape(-1, part.shape[-1])


def pack_kernel(qkv, proj, fc1, fc2, attention, packed):
    size = proj.shape[1]
    turned = proj[...].astype(wide).T.astype(narrow)
    attention[:, : 3 * size] = qkv[...]
    attention[:, 3 * size :] = turned
    packed[:, : 3 * size] = qkv[...]
    packed[:, 3 * size : 4 * size] = turned
    packed[:, 4 * size : 8 * size] = fc1[...]
    for k in range(4):
        packed[:, (8 + k) * size : (9 + k) * size] = fc2[k].astype(wide).T.astype(narrow)


def finish_kernel(lower, upper, qkv, proj, fc1, fc2):
    size = proj.shape[0]
    flip = lax.axis_index("core") == 1
    first = jnp.where(flip, upper[...].astype(wide), lower[...].astype(wide))
    second = jnp.where(flip, lower[...].astype(wide), upper[...].astype(wide))
    owned = jnp.concatenate([first, second], axis=0)
    for k in range(3):
        qkv[k] = owned[:, k * size : (k + 1) * size]
    proj[...] = owned[:, 3 * size : 4 * size].T
    for k in range(4):
        fc1[:, k, :] = owned[:, (4 + k) * size : (5 + k) * size]
        fc2[k] = owned[:, (8 + k) * size : (9 + k) * size].T


def mlp_grad_kernel(ring_first, kept, back, grads):
    width, columns = grads.shape[0], grads.shape[1] // 2
    halves = [
        t_dot(kept[:, :width], back[:, width:]).astype(narrow),
        t_dot(back[:, :width], kept[:, width : width + columns]).astype(narrow),
    ]
    for k, half in enumerate(halves):
        if ring_first:
            size = width // 16
            order = [(z * 4 + y) * size for y in range(4) for z in range(4)]
            half = jnp.concatenate([half[start : start + size] for start in order], axis=0)
        grads[:, k * columns : (k + 1) * columns] = half


def layer_grad_kernel(kept, back, mlp_kept, mlp_back_rows, grads):
    width, local = grads.shape[0], grads.shape[1] // 12
    grads[:, : 3 * local] = t_dot(kept[:, :width], back[:, width:]).astype(narrow)
    grads[:, 3 * local : 4 * local] = t_dot(back[:, :width], kept[:, width + 3 * local :]).astype(narrow)
    grads[:, 4 * local : 8 * local] = t_dot(mlp_kept[:, :width], mlp_back_rows[:, width:]).astype(narrow)
    grads[:, 8 * local :] = t_dot(mlp_back_rows[:, :width], mlp_kept[:, width:]).astype(narrow)


def ring_kernel(mine, other, own, *pieces):
    total = mine[...] + other[...].astype(wide)
    rows = own.shape[0]
    own[...] = total[:rows]
    for k, piece in enumerate(pieces):
        piece[...] = total[(k + 1) * rows : (k + 2) * rows].astype(narrow)


def ring_order_kernel(mine, other, ordered, total):
    total[...] = mine[...].astype(wide) + other[...].astype(wide)
    count = lax.axis_size("x")
    rows = total.shape[0] // count
    blocks = []
    for k in range(count):
        first = lax.rem(k + count - lax.axis_index("x"), count) * rows
        blocks.append(total[pl.ds(pl.multiple_of(first, 8), rows), :])
    ordered[...] = jnp.concatenate(blocks, axis=0).astype(narrow)


def summed(refs):
    total = refs[0][...]
    for piece in refs[1:]:
        total = total + piece[...].astype(wide)
    return total


def middle_kernel(own, one, two, three, arriving, table, middle, second):
    total = arriving[...].astype(wide) + summed((own, one, two, three)) + table[4:5, :]
    middle[...] = total
    second[...] = (normalise(total)[0] * table[2:3, :] + table[3:4, :]).astype(narrow)


def leave_kernel(own, one, two, three, middle, table, *refs):
    left = (middle[...] + summed((own, one, two, three)) + table[5:6, :]).astype(narrow)
    following, leaving, normed = refs
    leaving[...] = left
    unit = normalise(left.astype(wide))[0]
    normed[...] = (unit * following[0:1, :] + following[1:2, :]).astype(narrow)


def middle_back_kernel(own, one, two, three, grad, middle, table, middle_grad, branch_grad, sums):
    second_grad = summed((own, one, two, three))
    unit, inverse = normalise(middle[...])
    arriving = grad[...].astype(wide)
    total = arriving + norm_back(second_grad, table[2:3, :], unit, inverse)
    middle_grad[...] = total
    branch = total.astype(narrow)
    branch_grad[...] = branch
    sums[0:1, :] = column_sums(second_grad * unit)
    sums[1:2, :] = column_sums(second_grad)
    sums[2:3, :] = column_sums(branch.astype(wide))
    sums[3:4, :] = column_sums(arriving)


def input_back_kernel(own, one, two, three, middle_grad, arriving, table, down_grad, sums):
    normed_grad = summed((own, one, two, three))
    unit, inverse = normalise(arriving[...].astype(wide))
    total = middle_grad[...] + norm_back(normed_grad, table[0:1, :], unit, inverse)
    down_grad[...] = total.astype(narrow)
    sums[0:1, :] = column_sums(normed_grad * unit)
    sums[1:2, :] = column_sums(normed_grad)


def attend_kernel(layer, *refs):
    blocks, (matrix, table, kept, part_mine, part_other, *fetch) = refs[:8], refs[8:]
    rows, width, local = kept.shape[0], part_mine.shape[1], 2 * HDIM
    half = rows // 2
    if layer == 1:
        matrix = Fetch(layer, matrix, 0, *fetch)
    if layer == 0:
        unit = normalise(whole(blocks))[0]
        kept[:, width + 4 * local :] = unit.astype(narrow)
        kept[:, :width] = (unit * table[0:1, :] + table[1:2, :]).astype(narrow)
    else:
        kept[:, :width] = whole(blocks).astype(narrow)
    query_bias, value_bias = my_columns(table, 6, local), my_columns(table, 7, local)
    bias = jnp.concatenate([query_bias, jnp.zeros_like(query_bias), value_bias], axis=1)
    projected = (dot(kept[:, :width], matrix[:, : 3 * local]) + bias).astype(narrow)
    kept[:, width : width + 3 * local] = projected
    queries = projected[:, :local]
    key_rows = projected[:, local : 2 * local]
    value_rows = projected[:, 2 * local :]
    lower = lax.broadcasted_iota(jnp.int32, (rows, local), 1) < HDIM
    outs = []
    for keep in (lower, ~lower):
        scores = dot_t(jnp.where(keep, queries, jnp.zeros_like(queries)), key_rows) * SCALE
        raised = jnp.exp(scores - jnp.max(scores, axis=-1, keepdims=True))
        probs = raised * (1.0 / jnp.sum(raised, axis=-1, keepdims=True))
        outs.append(dot(probs.astype(narrow), value_rows))
    mixed = jnp.where(lower, outs[0], outs[1]).astype(narrow)
    kept[:, width + 3 * local : width + 4 * local] = mixed
    proj = matrix[:, 3 * local : 4 * local]
    part_other[...] = dot_t(mixed[half:, :], proj).astype(narrow)
    part_mine[...] = dot_t(mixed[:half, :], proj)


def attend_back_kernel(layer, *refs):
    blocks, (kept, matrix, *refs) = refs[:8], refs[8:]
    local = 2 * HDIM
    rows, width = kept.shape[0], kept.shape[1] - 4 * local
    if layer == 0:
        width = width // 2
    half = rows // 2
    if layer == 0:
        vectors, (part_mine, part_other, *slabs, back) = refs[:6], refs[6:]
    else:
        back, sums, part_mine, part_other, *fetch = refs
        matrix = Fetch(layer, matrix, 0, *fetch)
    back[:, :width] = whole(blocks).astype(narrow)
    out = dot(back[:, :width], matrix[:, 3 * local : 4 * local]).astype(narrow)
    queries = kept[:, width : width + local]
    key_rows = kept[:, width + local : width + 2 * local]
    value_rows = kept[:, width + 2 * local : width + 3 * local]
    lower = lax.broadcasted_iota(jnp.int32, (rows, local), 1) < HDIM
    query_grads, key_grad, value_grad = [], 0.0, 0.0
    for keep in (lower, ~lower):
        query = jnp.where(keep, queries, jnp.zeros_like(queries))
        grad = jnp.where(keep, out, jnp.zeros_like(out))
        scores = dot_t(query, key_rows) * SCALE
        raised = jnp.exp(scores - jnp.max(scores, axis=-1, keepdims=True))
        probs = raised * (1.0 / jnp.sum(raised, axis=-1, keepdims=True))
        prob_grad = dot_t(grad, value_rows)
        inner = jnp.sum(probs * prob_grad, axis=-1, keepdims=True)
        score_grad = (probs * (prob_grad - inner)).astype(narrow)
        query_grads.append(dot(score_grad, key_rows))
        value_grad = value_grad + t_dot(probs.astype(narrow), grad)
        key_grad = key_grad + t_dot(score_grad, query)
    back[:, width : width + local] = (jnp.where(lower, query_grads[0], query_grads[1]) * SCALE).astype(narrow)
    back[:, width + local : width + 2 * local] = (key_grad * SCALE).astype(narrow)
    back[:, width + 2 * local :] = value_grad.astype(narrow)
    projected_sums = column_sums(back[:, width:].astype(wide))
    qkv = matrix[:, : 3 * local]
    other = dot_t(back[half:, width:], qkv)
    mine = dot_t(back[:half, width:], qkv)
    part_other[...] = other.astype(narrow)
    part_mine[...] = mine
    if layer == 1:
        sums[...] = projected_sums
        return
    first_unit = width + 4 * local
    gain_sum = column_sums(mine * kept[:half, first_unit:].astype(wide))
    gain_sum += column_sums(other * kept[half:, first_unit:].astype(wide))
    shift_sum = column_sums(mine) + column_sums(other)
    column = lax.broadcasted_iota(jnp.int32, (1, width), 1) // local

    def rows_of(norm_sums, middle_sums, projected, hidden):
        found = [norm_sums, middle_sums]
        for values, k in ((projected, 0), (projected, 2), (hidden, 0), (hidden, 1), (hidden, 2), (hidden, 3)):
            row = jnp.concatenate([values[:, k * local : (k + 1) * local]] * (width // local), axis=1)
            found.append(jnp.where(column == my_part(), row, 0.0))
        return jnp.concatenate(found + [jnp.zeros((4, width), wide)], axis=0).astype(narrow)

    sums_zero, hidden_zero, norm_one, sums_one, projected_one, hidden_one = (ref[...] for ref in vectors)
    norm_zero = jnp.concatenate([gain_sum, shift_sum], axis=0)
    rows_zero = rows_of(norm_zero, sums_zero, projected_sums, hidden_zero)
    rows_one = rows_of(norm_one, sums_one, projected_one, hidden_one)
    count = len(slabs)
    size = width // count
    here = lax.axis_index("z")
    for k, slab in enumerate(slabs):
        first = pl.multiple_of(lax.rem(here + k, count) * size, size)
        normed = kept[:, pl.ds(first, size)]
        branch = back[:, pl.ds(first, size)]
        slab[:size, : 3 * local] = t_dot(normed, back[:, width:]).astype(narrow)
        slab[:size, 3 * local :] = t_dot(branch, kept[:, width + 3 * local : width + 4 * local]).astype(narrow)
    for k, slab in enumerate(slabs):
        for z in range(count):

            @pl.when(lax.rem(here + k, count) == z)
            def _():
                slab[size:, :size] = rows_zero[:, z * size : (z + 1) * size]
                slab[size:, size:] = rows_one[:, z * size : (z + 1) * size]


def hidden_parts(second, fc1, table):
    local = fc1.shape[1] // 4
    bias = jnp.concatenate([my_columns(table, 8 + r, local) for r in range(4)], axis=1)
    hidden = dot(second, fc1) + bias
    share = 0.5 * (1.0 + lax.erf(hidden * (0.5**0.5)))
    slope = share + hidden * jnp.exp(-0.5 * hidden * hidden) * 0.3989422804014327
    return (hidden * share).astype(narrow), slope


def mlp_kernel(*refs):
    blocks, (matrix, table, kept, part_mine, part_other, *fetch) = refs[:8], refs[8:]
    width, columns, half = part_mine.shape[1], fetch[0].shape[2] // 2, kept.shape[0] // 2
    matrix = Fetch(0, matrix, columns, *fetch)
    kept[:, :width] = whole(blocks).astype(narrow)
    activated, slope = hidden_parts(kept[:, :width], matrix[:, :columns], table)
    kept[:, width : width + columns] = activated
    kept[:, width + columns :] = slope.astype(narrow)
    part_other[...] = dot_t(activated[half:, :], matrix[:, columns:]).astype(narrow)
    part_mine[...] = dot_t(activated[:half, :], matrix[:, columns:])


def mlp_back_kernel(*refs):
    blocks, (kept, matrix, back, sums, part_mine, part_other, *fetch) = refs[:8], refs[8:]
    width, columns, half = part_mine.shape[1], fetch[0].shape[2] // 2, kept.shape[0] // 2
    matrix = Fetch(0, matrix, columns, *fetch)
    back[:, :width] = whole(blocks).astype(narrow)
    slope = kept[:, width + columns :].astype(wide)
    hidden_grad = (dot(back[:, :width], matrix[:, columns:]) * slope).astype(narrow)
    back[:, width:] = hidden_grad
    sums[...] = column_sums(hidden_grad.astype(wide))
    part_other[...] = dot_t(hidden_grad[half:, :], matrix[:, :columns]).astype(narrow)
    part_mine[...] = dot_t(hidden_grad[:half, :], matrix[:, :columns])


def mlp_both_kernel(*refs):
    blocks, final, (matrix, table, kept, back, sums, part_mine, part_other, left_mine, left_other, *fetch) = refs[:8], refs[8:16], refs[16:]
    width, columns, half = part_mine.shape[1], fetch[0].shape[2] // 2, kept.shape[0] // 2
    matrix = Fetch(1, matrix, columns, *fetch)
    kept[:, :width] = whole(blocks).astype(narrow)
    back[:, :width] = whole(final).astype(narrow)
    activated, slope = hidden_parts(kept[:, :width], matrix[:, :columns], table)
    kept[:, width:] = activated
    hidden_grad = (dot(back[:, :width], matrix[:, columns:]) * slope).astype(narrow)
    back[:, width:] = hidden_grad
    sums[...] = column_sums(hidden_grad.astype(wide))
    part_other[...] = dot_t(hidden_grad[half:, :], matrix[:, :columns]).astype(narrow)
    part_mine[...] = dot_t(hidden_grad[:half, :], matrix[:, :columns])
    left_other[...] = dot_t(activated[half:, :], matrix[:, columns:]).astype(narrow)
    left_mine[...] = dot_t(activated[:half, :], matrix[:, columns:]).astype(narrow)


def call(body, flops, outs, args, scratch=(), fetch=None, columns=None):
    specs = [pl.BlockSpec()] * len(args)
    scratch = list(scratch)
    if fetch is not None:
        shape = args[fetch].shape
        specs[fetch] = pl.BlockSpec(memory_space=pl.ANY)
        scratch += [pltpu.VMEM((shape[1], shape[3], columns), narrow), pltpu.SemaphoreType.DMA]
    return pl.pallas_call(
        body,
        out_shape=[jax.ShapeDtypeStruct(shape, kind) for shape, kind in outs],
        in_specs=specs,
        scratch_shapes=scratch,
        compiler_params=pltpu.CompilerParams(vmem_limit_bytes=48 << 20),
        cost_estimate=pl.CostEstimate(flops=flops, bytes_accessed=8 << 20, transcendentals=0),
    )(*args)


def partials(rows, width):
    return [((rows // 2, width), wide), ((rows // 2, width), narrow)]


def attend(layer, blocks, matrix, table):
    rows, width, columns = 8 * blocks[0].shape[0], blocks[0].shape[1], 8 * HDIM
    outs = [((rows, width + columns + width * (layer == 0)), narrow)] + partials(rows, width)
    body = functools.partial(attend_kernel, layer)
    fetch = (8, columns) if layer else (None, None)
    return call(body, 3 * 10**9, outs, [*blocks, matrix, table], (), *fetch)


def attend_back(layer, blocks, kept, matrix, vectors=()):
    rows, width, columns = kept.shape[0], blocks[0].shape[1], 8 * HDIM
    back = (rows, width + columns // 4 * 3)
    if layer == 0:
        count = lax.axis_size("z")
        outs = partials(rows, width) + [((width // count + 16, columns), narrow)] * count
        scratch = [pltpu.VMEM(back, narrow)]
    else:
        outs = [(back, narrow), ((1, columns // 4 * 3), wide)] + partials(rows, width)
        scratch = []
    body = functools.partial(attend_back_kernel, layer)
    fetch = (9, columns) if layer else (None, None)
    return call(body, 6 * 10**9, outs, [*blocks, kept, matrix, *vectors], scratch, *fetch)


def mlp(blocks, matrix, table):
    rows, width, columns = 8 * blocks[0].shape[0], blocks[0].shape[1], matrix.shape[4] // 3
    outs = [((rows, width + 2 * columns), narrow)] + partials(rows, width)
    return call(mlp_kernel, 4 * 10**9, outs, [*blocks, matrix, table], (), 8, 2 * columns)


def mlp_back(blocks, kept, matrix):
    rows, width, columns = kept.shape[0], blocks[0].shape[1], matrix.shape[4] // 3
    outs = [((rows, width + columns), narrow), ((1, columns), wide)] + partials(rows, width)
    return call(mlp_back_kernel, 4 * 10**9, outs, [*blocks, kept, matrix], (), 9, 2 * columns)


def mlp_both(blocks, final, matrix, table):
    rows, width, columns = 8 * blocks[0].shape[0], blocks[0].shape[1], matrix.shape[4] // 3
    outs = [((rows, width + columns), narrow)] * 2 + [((1, columns), wide)] + partials(rows, width)
    outs += [((rows // 2, width), narrow)] * 2
    return call(mlp_both_kernel, 6 * 10**9, outs, [*blocks, *final, matrix, table], (), 16, 2 * columns)


def pack(qkv, proj, fc1, fc2):
    rows, size = proj.shape
    outs = [((rows, 4 * size), narrow), ((rows, 12 * size), narrow)]
    return call(pack_kernel, 10**8, outs, [qkv, proj, fc1, fc2])


def ring_sums(mine, other):
    count = lax.axis_size("x")
    shape = (mine.shape[0] // count, mine.shape[1])
    outs = [(shape, wide)] + [(shape, narrow)] * (count - 1)
    return list(call(ring_kernel, 10**8, outs, [mine, other]))


def around_pieces(sums):
    return [sums[0]] + [along(piece, "x", k) for k, piece in enumerate(sums[1:], 1)]


def ring_pieces(mine, other):
    return around_pieces(ring_sums(mine, other))


def ring_order(mine, other):
    scratch = [pltpu.VMEM(mine.shape, wide)]
    return call(ring_order_kernel, 10**8, [(mine.shape, narrow)], [mine, other], scratch)[0]


def middle_of(terms, arriving, table):
    shape = arriving.shape
    return call(middle_kernel, 10**8, [(shape, wide), (shape, narrow)], [*terms, arriving, table])


def leave(terms, middle, table, following):
    return call(leave_kernel, 10**8, [(middle.shape, narrow)] * 2, [*terms, middle, table, following])


def middle_back(terms, grad, middle, table):
    shape = middle.shape
    outs = [(shape, wide), (shape, narrow), ((4, shape[1]), wide)]
    return call(middle_back_kernel, 10**8, outs, [*terms, grad, middle, table])


def input_back(terms, middle_grad, arriving, table):
    shape = arriving.shape
    outs = [(shape, narrow), ((2, shape[1]), wide)]
    return call(input_back_kernel, 10**8, outs, [*terms, middle_grad, arriving, table])


def mlp_grad(kept, back, shape, ring_first=False):
    return call(functools.partial(mlp_grad_kernel, ring_first), 2 * 10**9, [(shape, narrow)], [kept, back])[0]


def layer_grad(kept, back, mlp_kept, mlp_back_rows, shape):
    args = [kept, back, mlp_kept, mlp_back_rows]
    return call(layer_grad_kernel, 3 * 10**9, [(shape, narrow)], args)[0]


def finish(lower, upper, size):
    shapes = [(3, size, size), (size, size), (size, 4, size), (4, size, size)]
    return call(finish_kernel, 10**8, [(shape, wide) for shape in shapes], [lower, upper])


def tie(*values):
    return lax.optimization_barrier(values)


def hop(columns, layer):
    return lax.ppermute(columns, ("core", "ylo"), [(layer * 2, 0), (layer * 2 + 1, 3)])


def order_ring(own, arrived):
    core, high, low = (lax.axis_index(name) for name in ("core", "yhi", "ylo"))
    one, two, three = arrived
    holder = low == core
    a = jnp.where(holder, own, one)
    b = jnp.where(holder, two, three)
    place = high * 2 + low
    a_first = jnp.where(holder, high, (place + 1) % 4 // 2) == 0
    return jnp.concatenate([jnp.where(a_first, a, b), jnp.where(a_first, b, a)], axis=0)


def fold(zero, one):
    half = zero.shape[1] // 2
    return jnp.concatenate([zero[:, :half], zero[:, half:], one[:, :half], one[:, half:]], axis=0)


def unfold(rows):
    return [jnp.concatenate([rows[k : k + 12], rows[k + 12 : k + 24]], axis=1) for k in (0, 24)]


def per_device(inputs, cotangent, qkv_weight, proj_weight, fc1_weight, fc2_weight, vectors):
    width = inputs.shape[3]
    core = lax.axis_index("core")
    low = lax.axis_index("ylo")
    place = lax.axis_index(("z", "yhi", "ylo", "x"))
    local = qkv_weight.shape[3]
    own_rows = qkv_weight.shape[1]

    def added(values, arrived):
        return functools.reduce(lambda a, b: a + b, arrived, values)

    columns = lax.broadcasted_iota(jnp.int32, (12, width), 1) // 16
    table = jnp.where(columns == place, jnp.tile(vectors[0], (1, width // 16)), 0).astype(narrow)
    other_table = swap_cores(table)
    table = fold(jnp.where(core == 0, table, other_table), jnp.where(core == 0, other_table, table))
    attention_raw, raw = pack(
        qkv_weight[0].reshape(own_rows, 3 * local),
        proj_weight[0],
        fc1_weight[0].reshape(own_rows, 4 * local),
        fc2_weight[0],
    )
    table, attention_raw, raw = tie(table, attention_raw, raw)
    held = hop(attention_raw, 0)
    entering = turn(lax.dynamic_index_in_dim(inputs, core, 0, keepdims=False)[:, 0], 0)
    table = added(table, around(table, "x"))
    held, entering, table = tie(held, entering, table)
    mine = [entering] + around(entering, "x")
    arrived = around(jnp.concatenate([held, table], axis=0), RING)
    *arrived, raw = tie(*arrived, raw)
    blocks = order_ring(held, [piece[:own_rows] for piece in arrived])
    table = added(table, [piece[own_rows:] for piece in arrived])

    def gather_weights(rows):
        gathered = lax.all_gather(rows, ("core", "z", "yhi", "ylo"), axis=0, tiled=True)
        return gathered.reshape(2, 8, 2, own_rows, rows.shape[1])

    everything = gather_weights(raw)

    arrived = around(jnp.concatenate([blocks, table], axis=0), "z")
    entering_all = mine + [swap_cores(block) for block in mine]
    parts = [blocks] + [piece[: 2 * own_rows] for piece in arrived]
    start = (len(parts) - 1 - lax.axis_index("z")) * 2 * own_rows
    first = lax.dynamic_slice_in_dim(jnp.concatenate(parts[1:] + parts, axis=0), start, width, 0)
    tables = [t.astype(wide) for t in unfold(added(table, [piece[2 * own_rows :] for piece in arrived]))]

    def offload_sum(value, axis):
        return lax.psum_scatter(value, axis, scatter_dimension=0, tiled=True)

    kept_zero, mine, other = attend(0, entering_all, first, tables[0])
    terms = ring_pieces(mine, swap_cores(other))

    *terms, cotangent = tie(*terms, cotangent)
    final_all = lax.all_gather(
        lax.dynamic_index_in_dim(cotangent, core, 0, keepdims=False)[:, 0], ("core", "ylo", "x")
    )
    final_all = final_all.reshape((2, 2, 4) + entering.shape)

    middle_zero, second = middle_of(terms, entering, tables[0])
    mlp_kept_zero, mine, other = mlp(gather_tokens(second), everything, tables[0])

    terms = ring_pieces(mine, swap_cores(other))
    left_zero, normed = leave(terms, middle_zero, tables[0], tables[1])
    kept_one, mine, other = attend(1, gather_tokens(normed), everything, tables[1])
    terms = ring_pieces(mine, swap_cores(other))
    final_blocks = []
    for which in (core, 1 - core):
        for k in range(4):
            spot = (low, which, (lax.axis_index("x") + k) % 4, 0, 0)
            piece = lax.dynamic_slice(final_all, spot, (1, 1, 1) + entering.shape)
            final_blocks.append(piece.reshape(entering.shape))
    tied = tie(*terms, *final_blocks)
    terms, final_blocks = tied[:4], tied[4:]
    middle_one, second = middle_of(terms, left_zero, tables[1])

    mlp_kept_one, mlp_back_one, hidden_one, mine, other, left_mine, left_other = mlp_both(
        gather_tokens(second), final_blocks, everything, tables[1]
    )
    terms = ring_pieces(mine, swap_cores(other))
    left_total = ring_order(left_mine, swap_cores(left_other))
    *terms, left_total = tie(*terms, left_total)
    left_total = offload_sum(left_total, "x")
    middle_grad, branch_grad, sums_one = middle_back(terms, final_blocks[0], middle_one, tables[1])
    back, projected_one, mine, other = attend_back(1, gather_tokens(branch_grad), kept_one, everything)
    terms = ring_pieces(mine, swap_cores(other))
    grads_one = layer_grad(kept_one, back, mlp_kept_one, mlp_back_one, (width, 12 * local))
    *terms, left_total = tie(*terms, left_total)
    grads_one = offload_sum(grads_one, "z")
    down_grad, norm_one = input_back(terms, middle_grad, left_zero, tables[1])

    back, hidden_zero, mine, other = mlp_back(gather_tokens(down_grad), mlp_kept_zero, everything)
    terms = ring_pieces(mine, swap_cores(other))
    mlp_zero = mlp_grad(mlp_kept_zero, back, (width, 8 * local), True)
    mlp_zero = offload_sum(mlp_zero, RING)
    *terms, grads_one = tie(*terms, grads_one)
    grads_one = offload_sum(grads_one, RING)
    middle_grad, branch_grad, sums_zero = middle_back(terms, down_grad, middle_zero, tables[0])
    vectors = [sums_zero, hidden_zero, norm_one, sums_one, projected_one, hidden_one]

    mine, other, *slabs = attend_back(0, gather_tokens(branch_grad), kept_zero, first, vectors)
    other, mlp_zero = tie(other, mlp_zero)
    mlp_zero = offload_sum(mlp_zero, "z")

    sent = [along(slab, "z", k) for k, slab in enumerate(slabs) if k > 0]
    sums = ring_sums(mine, swap_cores(other))
    terms = around_pieces(sums)
    terms[0], grads_one = tie(terms[0], grads_one)
    slab = added(slabs[0].astype(wide), [piece.astype(wide) for piece in sent]).astype(narrow)
    slab, *terms = tie(slab, *terms)
    grad_zero, _ = input_back(terms, middle_grad, entering, tables[0])
    left_one = (middle_one + left_total.astype(wide) + tables[1][5:6]).astype(narrow)

    done_zero = jnp.concatenate([left_zero, grad_zero], axis=0)
    done_one = jnp.concatenate([left_one, down_grad], axis=0)
    done_mine = turn_back(jnp.where(low == 0, done_zero, done_one), 0)
    done_other = turn_back(jnp.where(low == 0, done_one, done_zero), 1)
    count, rows = lax.axis_size(RING), own_rows // 2
    turn_rows = lax.axis_index(RING) * rows

    def ring_slab(k):
        start = (turn_rows + k * rows) % (count * rows)
        return jnp.concatenate(
            [lax.dynamic_slice_in_dim(slab, start, rows, 0), slab[count * rows :]], axis=0
        )

    sent = [along(ring_slab(k), RING, k) for k in range(1, count)]
    slab = added(ring_slab(0).astype(wide), [piece.astype(wide) for piece in sent])

    owned_zero = jnp.concatenate([slab[:rows].astype(narrow), mlp_zero], axis=1)
    owned_one = grads_one
    got_mine = turn_back(jnp.where(low == 0, owned_zero, owned_one), 0)
    got_other = turn_back(jnp.where(low == 0, owned_one, owned_zero), 1)
    vector_sum = slab[rows:]
    vector_sum = added(vector_sum, around(vector_sum, "x"))
    vector_sum, got_mine, got_other = tie(vector_sum, got_mine, got_other)
    vector_zero, vector_one = vector_sum[:, : 2 * local], vector_sum[:, 2 * local :]
    vector_sum = jnp.where(core == 0, vector_zero, vector_one) + swap_cores(
        jnp.where(core == 0, vector_one, vector_zero)
    )
    start = turn_rows + lax.axis_index("x") * 16
    vector_owned = lax.dynamic_slice_in_dim(vector_sum[:12], start, 16, 1)
    qkv_grad, proj_grad, fc1_grad, fc2_grad = finish(got_mine, got_other, local)
    done = jnp.stack([jnp.where(core == 0, done_mine, done_other), jnp.where(core == 0, done_other, done_mine)])
    tokens = entering.shape[0]
    return (
        done[None, :, :tokens, None],
        done[None, :, tokens:, None].astype(wide),
        jnp.transpose(qkv_grad, (1, 0, 2))[None],
        proj_grad[None],
        fc1_grad[None],
        fc2_grad[None],
        vector_owned[None],
    )


def solution(mesh):
    fine = Mesh(mesh.devices.reshape(2, 4, 2, 2, 4), ("core", "z", "yhi", "ylo", "x"))
    tensor = ("ylo", "x")
    dp = ("z", "yhi")
    in_specs = (
        P(None, tensor, dp, None),
        P(None, tensor, dp, None),
        P("core", dp, None, tensor),
        P("core", tensor, dp),
        P("core", dp, None, tensor),
        P("core", None, tensor, dp),
        P("core", None, dp + tensor),
    )
    out_specs = (
        P("core", None, tensor, dp, None),
        P("core", None, tensor, dp, None),
        P("core", dp, None, tensor),
        P("core", tensor, dp),
        P("core", dp, None, tensor),
        P("core", None, tensor, dp),
        P("core", None, dp + tensor),
    )
    return jax.shard_map(
        per_device, mesh=fine, in_specs=in_specs, out_specs=out_specs, check_vma=False
    )
```

```python
import functools

import jax
import jax.numpy as jnp
from jax import lax
from jax.experimental import pallas as pl
from jax.experimental.pallas import tpu as pltpu
from jax.sharding import Mesh, PartitionSpec as P

HDIM = 64
SCALE = HDIM ** (-0.5)

eps = 1e-06
wide = jnp.float32
narrow = jnp.bfloat16


RING = ("yhi", "ylo")


def swap_cores(value):
    return lax.ppermute(value, "core", [(0, 1), (1, 0)])


def along(value, axis, steps):
    count = lax.axis_size(axis)
    return lax.ppermute(value, axis, [(i, (i + steps) % count) for i in range(count)])


def around(value, axis):
    return [along(value, axis, -k) for k in range(1, lax.axis_size(axis))]


def turn(value, flip):
    pairs = [(c * 2 + y, y * 2 + (c ^ flip)) for c in range(2) for y in range(2)]
    return lax.ppermute(value, ("core", "ylo"), pairs)


def turn_back(value, flip):
    pairs = [(c * 2 + y, (y ^ flip) * 2 + c) for c in range(2) for y in range(2)]
    return lax.ppermute(value, ("core", "ylo"), pairs)


def gather_tokens(rows, *others):
    mine = [rows] + around(rows, "x")
    mine[-1], *others = lax.optimization_barrier((mine[-1], *others))
    blocks = mine + [swap_cores(block) for block in mine]
    return (blocks, *others) if others else blocks


def normalise(rows):
    center = rows - jnp.mean(rows, axis=-1, keepdims=True)
    spread = jnp.mean(center * center, axis=-1, keepdims=True)
    inverse = lax.rsqrt(spread + eps)
    return center * inverse, inverse


def norm_back(grad, gain, unit, inverse):
    pulled = grad * gain
    mean_one = jnp.mean(pulled, axis=-1, keepdims=True)
    mean_two = jnp.mean(pulled * unit, axis=-1, keepdims=True)
    return inverse * (pulled - mean_one - unit * mean_two)


def dot(a, b):
    return jnp.dot(a, b, preferred_element_type=wide)


def dot_t(a, b):
    return lax.dot_general(a, b, (((1,), (1,)), ((), ())), preferred_element_type=wide)


def t_dot(a, b):
    return lax.dot_general(a, b, (((0,), (0,)), ((), ())), preferred_element_type=wide)


def whole(refs):
    return jnp.concatenate([ref[...].astype(wide) for ref in refs], axis=0)


def column_sums(values):
    return jnp.sum(values, axis=0, keepdims=True)


def my_part():
    return lax.axis_index("core") * lax.axis_size("x") + lax.axis_index("x")


def my_columns(table, row, size):
    start = pl.multiple_of(my_part() * size, size)
    return table[row : row + 1, pl.ds(start, size)]


class Fetch:
    def __init__(self, layer, source, start, held, semaphore):
        self.held = held
        columns = source.at[layer, :, lax.axis_index("core"), :, pl.ds(start, held.shape[-1])]
        self.copy = pltpu.make_async_copy(columns, held, semaphore)
        self.copy.start()

    def __getitem__(self, key):
        if self.copy is not None:
            self.copy.wait()
            self.copy = None
        part = self.held[:, :, key[1]]
        return part.reshape(-1, part.shape[-1])


def pack_kernel(qkv, proj, packed):
    size = proj.shape[1]
    packed[:, : 3 * size] = qkv[...]
    packed[:, 3 * size :] = proj[...].astype(wide).T.astype(narrow)


def pack_all_kernel(attention, fc1, fc2, packed):
    size = fc2.shape[1]
    packed[:, : 4 * size] = attention[...]
    packed[:, 4 * size : 8 * size] = fc1[...]
    for k in range(4):
        packed[:, (8 + k) * size : (9 + k) * size] = fc2[k].astype(wide).T.astype(narrow)


def finish_kernel(lower, upper, qkv, proj, fc1, fc2):
    size = proj.shape[0]
    flip = lax.axis_index("core") == 1
    first = jnp.where(flip, upper[...].astype(wide), lower[...].astype(wide))
    second = jnp.where(flip, lower[...].astype(wide), upper[...].astype(wide))
    owned = jnp.concatenate([first, second], axis=0)
    for k in range(3):
        qkv[k] = owned[:, k * size : (k + 1) * size]
    proj[...] = owned[:, 3 * size : 4 * size].T
    for k in range(4):
        fc1[:, k, :] = owned[:, (4 + k) * size : (5 + k) * size]
        fc2[k] = owned[:, (8 + k) * size : (9 + k) * size].T


def mlp_grad_kernel(ring_first, kept, back, grads):
    width, columns = grads.shape[0], grads.shape[1] // 2
    halves = [
        t_dot(kept[:, :width], back[:, width:]).astype(narrow),
        t_dot(back[:, :width], kept[:, width : width + columns]).astype(narrow),
    ]
    for k, half in enumerate(halves):
        if ring_first:
            size = width // 16
            order = [(z * 4 + y) * size for y in range(4) for z in range(4)]
            half = jnp.concatenate([half[start : start + size] for start in order], axis=0)
        grads[:, k * columns : (k + 1) * columns] = half


def store_columns(held, grads, start, semaphore):
    columns = grads.at[:, pl.ds(start, held.shape[1])]
    copy = pltpu.make_async_copy(held, columns, semaphore)
    copy.start()
    copy.wait()


def mlp_part_kernel(kept, back, grads, held, semaphore):
    width, columns = held.shape[0], held.shape[1] // 2
    held[:, :columns] = t_dot(kept[:, :width], back[:, width:]).astype(narrow)
    held[:, columns:] = t_dot(back[:, :width], kept[:, width:]).astype(narrow)
    store_columns(held, grads, columns, semaphore)


def attention_part_kernel(kept, back, _, grads, held, semaphore):
    width, local = held.shape[0], held.shape[1] // 4
    held[:, : 3 * local] = t_dot(kept[:, :width], back[:, width:]).astype(narrow)
    held[:, 3 * local :] = t_dot(back[:, :width], kept[:, width + 3 * local :]).astype(narrow)
    store_columns(held, grads, 0, semaphore)


def ring_kernel(mine, other, own, *pieces):
    total = mine[...] + other[...].astype(wide)
    rows = own.shape[0]
    own[...] = total[:rows]
    for k, piece in enumerate(pieces):
        piece[...] = total[(k + 1) * rows : (k + 2) * rows].astype(narrow)


def ring_order_kernel(mine, other, ordered, total):
    total[...] = mine[...].astype(wide) + other[...].astype(wide)
    count = lax.axis_size("x")
    rows = total.shape[0] // count
    blocks = []
    for k in range(count):
        first = lax.rem(k + count - lax.axis_index("x"), count) * rows
        blocks.append(total[pl.ds(pl.multiple_of(first, 8), rows), :])
    ordered[...] = jnp.concatenate(blocks, axis=0).astype(narrow)


def summed(refs):
    total = refs[0][...]
    for piece in refs[1:]:
        total = total + piece[...].astype(wide)
    return total


def middle_kernel(own, one, two, three, arriving, table, middle, second):
    total = arriving[...].astype(wide) + summed((own, one, two, three)) + table[4:5, :]
    middle[...] = total
    second[...] = (normalise(total)[0] * table[2:3, :] + table[3:4, :]).astype(narrow)


def leave_kernel(own, one, two, three, middle, table, *refs):
    left = (middle[...] + summed((own, one, two, three)) + table[5:6, :]).astype(narrow)
    following, leaving, normed = refs
    leaving[...] = left
    unit = normalise(left.astype(wide))[0]
    normed[...] = (unit * following[0:1, :] + following[1:2, :]).astype(narrow)


def middle_back_kernel(own, one, two, three, grad, middle, table, middle_grad, branch_grad, sums):
    second_grad = summed((own, one, two, three))
    unit, inverse = normalise(middle[...])
    arriving = grad[...].astype(wide)
    total = arriving + norm_back(second_grad, table[2:3, :], unit, inverse)
    middle_grad[...] = total
    branch = total.astype(narrow)
    branch_grad[...] = branch
    sums[0:1, :] = column_sums(second_grad * unit)
    sums[1:2, :] = column_sums(second_grad)
    sums[2:3, :] = column_sums(branch.astype(wide))
    sums[3:4, :] = column_sums(arriving)


def input_back_kernel(own, one, two, three, middle_grad, arriving, table, down_grad, sums):
    normed_grad = summed((own, one, two, three))
    unit, inverse = normalise(arriving[...].astype(wide))
    total = middle_grad[...] + norm_back(normed_grad, table[0:1, :], unit, inverse)
    down_grad[...] = total.astype(narrow)
    sums[0:1, :] = column_sums(normed_grad * unit)
    sums[1:2, :] = column_sums(normed_grad)


def attend_kernel(layer, *refs):
    blocks, (matrix, table, kept, part_mine, part_other, *fetch) = refs[:8], refs[8:]
    rows, width, local = kept.shape[0], part_mine.shape[1], 2 * HDIM
    half = rows // 2
    if layer == 1:
        matrix = Fetch(layer, matrix, 0, *fetch)
    if layer == 0:
        unit = normalise(whole(blocks))[0]
        kept[:, width + 4 * local :] = unit.astype(narrow)
        kept[:, :width] = (unit * table[0:1, :] + table[1:2, :]).astype(narrow)
    else:
        kept[:, :width] = whole(blocks).astype(narrow)
    query_bias, value_bias = my_columns(table, 6, local), my_columns(table, 7, local)
    bias = jnp.concatenate([query_bias, jnp.zeros_like(query_bias), value_bias], axis=1)
    projected = (dot(kept[:, :width], matrix[:, : 3 * local]) + bias).astype(narrow)
    kept[:, width : width + 3 * local] = projected
    queries = projected[:, :local]
    key_rows = projected[:, local : 2 * local]
    value_rows = projected[:, 2 * local :]
    lower = lax.broadcasted_iota(jnp.int32, (rows, local), 1) < HDIM
    outs = []
    for keep in (lower, ~lower):
        scores = dot_t(jnp.where(keep, queries, jnp.zeros_like(queries)), key_rows) * SCALE
        raised = jnp.exp(scores - jnp.max(scores, axis=-1, keepdims=True))
        probs = raised * (1.0 / jnp.sum(raised, axis=-1, keepdims=True))
        outs.append(dot(probs.astype(narrow), value_rows))
    mixed = jnp.where(lower, outs[0], outs[1]).astype(narrow)
    kept[:, width + 3 * local : width + 4 * local] = mixed
    proj = matrix[:, 3 * local : 4 * local]
    part_other[...] = dot_t(mixed[half:, :], proj).astype(narrow)
    part_mine[...] = dot_t(mixed[:half, :], proj)


def attend_back_kernel(layer, *refs):
    blocks, (kept, matrix, *refs) = refs[:8], refs[8:]
    local = 2 * HDIM
    rows, width = kept.shape[0], kept.shape[1] - 4 * local
    if layer == 0:
        width = width // 2
    half = rows // 2
    if layer == 0:
        vectors, (part_mine, part_other, *slabs, back) = refs[:6], refs[6:]
    else:
        back, sums, part_mine, part_other, *fetch = refs
        matrix = Fetch(layer, matrix, 0, *fetch)
    back[:, :width] = whole(blocks).astype(narrow)
    out = dot(back[:, :width], matrix[:, 3 * local : 4 * local]).astype(narrow)
    queries = kept[:, width : width + local]
    key_rows = kept[:, width + local : width + 2 * local]
    value_rows = kept[:, width + 2 * local : width + 3 * local]
    lower = lax.broadcasted_iota(jnp.int32, (rows, local), 1) < HDIM
    query_grads, key_grad, value_grad = [], 0.0, 0.0
    for keep in (lower, ~lower):
        query = jnp.where(keep, queries, jnp.zeros_like(queries))
        grad = jnp.where(keep, out, jnp.zeros_like(out))
        scores = dot_t(query, key_rows) * SCALE
        raised = jnp.exp(scores - jnp.max(scores, axis=-1, keepdims=True))
        probs = raised * (1.0 / jnp.sum(raised, axis=-1, keepdims=True))
        prob_grad = dot_t(grad, value_rows)
        inner = jnp.sum(probs * prob_grad, axis=-1, keepdims=True)
        score_grad = (probs * (prob_grad - inner)).astype(narrow)
        query_grads.append(dot(score_grad, key_rows))
        value_grad = value_grad + t_dot(probs.astype(narrow), grad)
        key_grad = key_grad + t_dot(score_grad, query)
    back[:, width : width + local] = (jnp.where(lower, query_grads[0], query_grads[1]) * SCALE).astype(narrow)
    back[:, width + local : width + 2 * local] = (key_grad * SCALE).astype(narrow)
    back[:, width + 2 * local :] = value_grad.astype(narrow)
    projected_sums = column_sums(back[:, width:].astype(wide))
    qkv = matrix[:, : 3 * local]
    other = dot_t(back[half:, width:], qkv)
    mine = dot_t(back[:half, width:], qkv)
    part_other[...] = other.astype(narrow)
    part_mine[...] = mine
    if layer == 1:
        sums[...] = projected_sums
        return
    first_unit = width + 4 * local
    gain_sum = column_sums(mine * kept[:half, first_unit:].astype(wide))
    gain_sum += column_sums(other * kept[half:, first_unit:].astype(wide))
    shift_sum = column_sums(mine) + column_sums(other)
    column = lax.broadcasted_iota(jnp.int32, (1, width), 1) // local

    def rows_of(norm_sums, middle_sums, projected, hidden):
        found = [norm_sums, middle_sums]
        for values, k in ((projected, 0), (projected, 2), (hidden, 0), (hidden, 1), (hidden, 2), (hidden, 3)):
            row = jnp.concatenate([values[:, k * local : (k + 1) * local]] * (width // local), axis=1)
            found.append(jnp.where(column == my_part(), row, 0.0))
        return jnp.concatenate(found + [jnp.zeros((4, width), wide)], axis=0).astype(narrow)

    sums_zero, hidden_zero, norm_one, sums_one, projected_one, hidden_one = (ref[...] for ref in vectors)
    norm_zero = jnp.concatenate([gain_sum, shift_sum], axis=0)
    rows_zero = rows_of(norm_zero, sums_zero, projected_sums, hidden_zero)
    rows_one = rows_of(norm_one, sums_one, projected_one, hidden_one)
    count = len(slabs)
    size = width // count
    here = lax.axis_index("z")
    for k, slab in enumerate(slabs):
        first = pl.multiple_of(lax.rem(here + k, count) * size, size)
        normed = kept[:, pl.ds(first, size)]
        branch = back[:, pl.ds(first, size)]
        slab[:size, : 3 * local] = t_dot(normed, back[:, width:]).astype(narrow)
        slab[:size, 3 * local :] = t_dot(branch, kept[:, width + 3 * local : width + 4 * local]).astype(narrow)
    for k, slab in enumerate(slabs):
        for z in range(count):

            @pl.when(lax.rem(here + k, count) == z)
            def _():
                slab[size:, :size] = rows_zero[:, z * size : (z + 1) * size]
                slab[size:, size:] = rows_one[:, z * size : (z + 1) * size]


def hidden_parts(second, fc1, table):
    local = fc1.shape[1] // 4
    bias = jnp.concatenate([my_columns(table, 8 + r, local) for r in range(4)], axis=1)
    hidden = dot(second, fc1) + bias
    share = 0.5 * (1.0 + lax.erf(hidden * (0.5**0.5)))
    slope = share + hidden * jnp.exp(-0.5 * hidden * hidden) * 0.3989422804014327
    return (hidden * share).astype(narrow), slope


def mlp_kernel(*refs):
    blocks, (matrix, table, kept, part_mine, part_other, *fetch) = refs[:8], refs[8:]
    width, columns, half = part_mine.shape[1], fetch[0].shape[2] // 2, kept.shape[0] // 2
    matrix = Fetch(0, matrix, columns, *fetch)
    kept[:, :width] = whole(blocks).astype(narrow)
    activated, slope = hidden_parts(kept[:, :width], matrix[:, :columns], table)
    kept[:, width : width + columns] = activated
    kept[:, width + columns :] = slope.astype(narrow)
    part_other[...] = dot_t(activated[half:, :], matrix[:, columns:]).astype(narrow)
    part_mine[...] = dot_t(activated[:half, :], matrix[:, columns:])


def mlp_back_kernel(*refs):
    blocks, (kept, matrix, back, sums, part_mine, part_other, *fetch) = refs[:8], refs[8:]
    width, columns, half = part_mine.shape[1], fetch[0].shape[2] // 2, kept.shape[0] // 2
    matrix = Fetch(0, matrix, columns, *fetch)
    back[:, :width] = whole(blocks).astype(narrow)
    slope = kept[:, width + columns :].astype(wide)
    hidden_grad = (dot(back[:, :width], matrix[:, columns:]) * slope).astype(narrow)
    back[:, width:] = hidden_grad
    sums[...] = column_sums(hidden_grad.astype(wide))
    part_other[...] = dot_t(hidden_grad[half:, :], matrix[:, :columns]).astype(narrow)
    part_mine[...] = dot_t(hidden_grad[:half, :], matrix[:, :columns])


def mlp_both_kernel(*refs):
    blocks, final, (matrix, table, kept, back, sums, part_mine, part_other, left_mine, left_other, *fetch) = refs[:8], refs[8:16], refs[16:]
    width, columns, half = part_mine.shape[1], fetch[0].shape[2] // 2, kept.shape[0] // 2
    matrix = Fetch(1, matrix, columns, *fetch)
    kept[:, :width] = whole(blocks).astype(narrow)
    back[:, :width] = whole(final).astype(narrow)
    activated, slope = hidden_parts(kept[:, :width], matrix[:, :columns], table)
    kept[:, width:] = activated
    hidden_grad = (dot(back[:, :width], matrix[:, columns:]) * slope).astype(narrow)
    back[:, width:] = hidden_grad
    sums[...] = column_sums(hidden_grad.astype(wide))
    part_other[...] = dot_t(hidden_grad[half:, :], matrix[:, :columns]).astype(narrow)
    part_mine[...] = dot_t(hidden_grad[:half, :], matrix[:, :columns])
    left_other[...] = dot_t(activated[half:, :], matrix[:, columns:]).astype(narrow)
    left_mine[...] = dot_t(activated[:half, :], matrix[:, columns:]).astype(narrow)


def call(body, flops, outs, args, scratch=(), fetch=None, columns=None):
    specs = [pl.BlockSpec()] * len(args)
    scratch = list(scratch)
    if fetch is not None:
        shape = args[fetch].shape
        specs[fetch] = pl.BlockSpec(memory_space=pl.ANY)
        scratch += [pltpu.VMEM((shape[1], shape[3], columns), narrow), pltpu.SemaphoreType.DMA]
    return pl.pallas_call(
        body,
        out_shape=[jax.ShapeDtypeStruct(shape, kind) for shape, kind in outs],
        in_specs=specs,
        scratch_shapes=scratch,
        compiler_params=pltpu.CompilerParams(vmem_limit_bytes=48 << 20),
        cost_estimate=pl.CostEstimate(flops=flops, bytes_accessed=8 << 20, transcendentals=0),
    )(*args)


def partials(rows, width):
    return [((rows // 2, width), wide), ((rows // 2, width), narrow)]


def attend(layer, blocks, matrix, table):
    rows, width, columns = 8 * blocks[0].shape[0], blocks[0].shape[1], 8 * HDIM
    outs = [((rows, width + columns + width * (layer == 0)), narrow)] + partials(rows, width)
    body = functools.partial(attend_kernel, layer)
    fetch = (8, columns) if layer else (None, None)
    return call(body, 3 * 10**9, outs, [*blocks, matrix, table], (), *fetch)


def attend_back(layer, blocks, kept, matrix, vectors=()):
    rows, width, columns = kept.shape[0], blocks[0].shape[1], 8 * HDIM
    back = (rows, width + columns // 4 * 3)
    if layer == 0:
        count = lax.axis_size("z")
        outs = partials(rows, width) + [((width // count + 16, columns), narrow)] * count
        scratch = [pltpu.VMEM(back, narrow)]
    else:
        outs = [(back, narrow), ((1, columns // 4 * 3), wide)] + partials(rows, width)
        scratch = []
    body = functools.partial(attend_back_kernel, layer)
    fetch = (9, columns) if layer else (None, None)
    return call(body, 6 * 10**9, outs, [*blocks, kept, matrix, *vectors], scratch, *fetch)


def mlp(blocks, matrix, table):
    rows, width, columns = 8 * blocks[0].shape[0], blocks[0].shape[1], matrix.shape[4] // 3
    outs = [((rows, width + 2 * columns), narrow)] + partials(rows, width)
    return call(mlp_kernel, 4 * 10**9, outs, [*blocks, matrix, table], (), 8, 2 * columns)


def mlp_back(blocks, kept, matrix):
    rows, width, columns = kept.shape[0], blocks[0].shape[1], matrix.shape[4] // 3
    outs = [((rows, width + columns), narrow), ((1, columns), wide)] + partials(rows, width)
    return call(mlp_back_kernel, 4 * 10**9, outs, [*blocks, kept, matrix], (), 9, 2 * columns)


def mlp_both(blocks, final, matrix, table):
    rows, width, columns = 8 * blocks[0].shape[0], blocks[0].shape[1], matrix.shape[4] // 3
    outs = [((rows, width + columns), narrow)] * 2 + [((1, columns), wide)] + partials(rows, width)
    outs += [((rows // 2, width), narrow)] * 2
    return call(mlp_both_kernel, 6 * 10**9, outs, [*blocks, *final, matrix, table], (), 16, 2 * columns)


def pack(qkv, proj):
    rows, size = proj.shape
    return call(pack_kernel, 10**8, [((rows, 4 * size), narrow)], [qkv, proj])[0]


def pack_all(attention, fc1, fc2):
    shape = (attention.shape[0], 3 * attention.shape[1])
    return call(pack_all_kernel, 10**8, [(shape, narrow)], [attention, fc1, fc2])[0]


def ring_sums(mine, other):
    count = lax.axis_size("x")
    shape = (mine.shape[0] // count, mine.shape[1])
    outs = [(shape, wide)] + [(shape, narrow)] * (count - 1)
    return list(call(ring_kernel, 10**8, outs, [mine, other]))


def around_pieces(sums):
    return [sums[0]] + [along(piece, "x", k) for k, piece in enumerate(sums[1:], 1)]


def ring_pieces(mine, other):
    return around_pieces(ring_sums(mine, other))


def ring_order(mine, other):
    scratch = [pltpu.VMEM(mine.shape, wide)]
    return call(ring_order_kernel, 10**8, [(mine.shape, narrow)], [mine, other], scratch)[0]


def middle_of(terms, arriving, table):
    shape = arriving.shape
    return call(middle_kernel, 10**8, [(shape, wide), (shape, narrow)], [*terms, arriving, table])


def leave(terms, middle, table, following):
    return call(leave_kernel, 10**8, [(middle.shape, narrow)] * 2, [*terms, middle, table, following])


def middle_back(terms, grad, middle, table):
    shape = middle.shape
    outs = [(shape, wide), (shape, narrow), ((4, shape[1]), wide)]
    return call(middle_back_kernel, 10**8, outs, [*terms, grad, middle, table])


def input_back(terms, middle_grad, arriving, table):
    shape = arriving.shape
    outs = [(shape, narrow), ((2, shape[1]), wide)]
    return call(input_back_kernel, 10**8, outs, [*terms, middle_grad, arriving, table])


def mlp_grad(kept, back, shape, ring_first=False):
    return call(functools.partial(mlp_grad_kernel, ring_first), 2 * 10**9, [(shape, narrow)], [kept, back])[0]


def grad_part(body, flops, args, shape, columns):
    whole_array = pl.BlockSpec(memory_space=pl.ANY)
    added = len(args) == 3
    return pl.pallas_call(
        body,
        out_shape=jax.ShapeDtypeStruct(shape, narrow),
        in_specs=[pl.BlockSpec()] * 2 + [whole_array] * added,
        out_specs=whole_array,
        input_output_aliases={2: 0} if added else {},
        scratch_shapes=[pltpu.VMEM((shape[0], columns), narrow), pltpu.SemaphoreType.DMA],
        compiler_params=pltpu.CompilerParams(vmem_limit_bytes=48 << 20),
        cost_estimate=pl.CostEstimate(flops=flops, bytes_accessed=8 << 20, transcendentals=0),
    )(*args)


def finish(lower, upper, size):
    shapes = [(3, size, size), (size, size), (size, 4, size), (4, size, size)]
    return call(finish_kernel, 10**8, [(shape, wide) for shape in shapes], [lower, upper])


def tie(*values):
    return lax.optimization_barrier(values)


def hop(columns, layer):
    return lax.ppermute(columns, ("core", "ylo"), [(layer * 2, 0), (layer * 2 + 1, 3)])


def order_ring(own, arrived):
    core, high, low = (lax.axis_index(name) for name in ("core", "yhi", "ylo"))
    one, two, three = arrived
    holder = low == core
    a = jnp.where(holder, own, one)
    b = jnp.where(holder, two, three)
    place = high * 2 + low
    a_first = jnp.where(holder, high, (place + 1) % 4 // 2) == 0
    return jnp.concatenate([jnp.where(a_first, a, b), jnp.where(a_first, b, a)], axis=0)


def fold(zero, one):
    half = zero.shape[1] // 2
    return jnp.concatenate([zero[:, :half], zero[:, half:], one[:, :half], one[:, half:]], axis=0)


def unfold(rows):
    return [jnp.concatenate([rows[k : k + 12], rows[k + 12 : k + 24]], axis=1) for k in (0, 24)]


def per_device(inputs, cotangent, qkv_weight, proj_weight, fc1_weight, fc2_weight, vectors):
    width = inputs.shape[3]
    core = lax.axis_index("core")
    low = lax.axis_index("ylo")
    place = lax.axis_index(("z", "yhi", "ylo", "x"))
    local = qkv_weight.shape[3]
    own_rows = qkv_weight.shape[1]

    def added(values, arrived):
        return functools.reduce(lambda a, b: a + b, arrived, values)

    columns = lax.broadcasted_iota(jnp.int32, (12, width), 1) // 16
    table = jnp.where(columns == place, jnp.tile(vectors[0], (1, width // 16)), 0).astype(narrow)
    other_table = swap_cores(table)
    table = fold(jnp.where(core == 0, table, other_table), jnp.where(core == 0, other_table, table))
    attention_raw = pack(qkv_weight[0].reshape(own_rows, 3 * local), proj_weight[0])
    table, attention_raw, fc1_weight, fc2_weight = tie(table, attention_raw, fc1_weight, fc2_weight)
    raw = pack_all(attention_raw, fc1_weight[0].reshape(own_rows, 4 * local), fc2_weight[0])
    held = hop(attention_raw, 0)
    entering = turn(lax.dynamic_index_in_dim(inputs, core, 0, keepdims=False)[:, 0], 0)
    table = added(table, around(table, "x"))
    held, entering, table = tie(held, entering, table)
    mine = [entering] + around(entering, "x")
    arrived = around(jnp.concatenate([held, table], axis=0), RING)
    *arrived, raw = tie(*arrived, raw)
    blocks = order_ring(held, [piece[:own_rows] for piece in arrived])
    table = added(table, [piece[own_rows:] for piece in arrived])

    def gather_weights(rows):
        gathered = lax.all_gather(rows, ("core", "z", "yhi", "ylo"), axis=0, tiled=True)
        return gathered.reshape(2, 8, 2, own_rows, rows.shape[1])

    everything = gather_weights(raw)

    arrived = around(jnp.concatenate([blocks, table], axis=0), "z")
    mine[1], cotangent = tie(mine[1], cotangent)
    final_grad = turn(lax.dynamic_index_in_dim(cotangent, core, 0, keepdims=False)[:, 0], 0)
    entering_all = mine + [swap_cores(block) for block in mine]
    parts = [blocks] + [piece[: 2 * own_rows] for piece in arrived]
    start = (len(parts) - 1 - lax.axis_index("z")) * 2 * own_rows
    first = lax.dynamic_slice_in_dim(jnp.concatenate(parts[1:] + parts, axis=0), start, width, 0)
    tables = [t.astype(wide) for t in unfold(added(table, [piece[2 * own_rows :] for piece in arrived]))]

    def offload_sum(value, axis):
        return lax.psum_scatter(value, axis, scatter_dimension=0, tiled=True)

    kept_zero, mine, other = attend(0, entering_all, first, tables[0])
    terms = ring_pieces(mine, swap_cores(other))

    *terms, final_grad = tie(*terms, final_grad)
    final_all = lax.all_gather(final_grad, ("core", "x")).reshape((2, 4) + entering.shape)

    middle_zero, second = middle_of(terms, entering, tables[0])
    mlp_kept_zero, mine, other = mlp(gather_tokens(second), everything, tables[0])

    terms = ring_pieces(mine, swap_cores(other))
    left_zero, normed = leave(terms, middle_zero, tables[0], tables[1])
    kept_one, mine, other = attend(1, gather_tokens(normed), everything, tables[1])
    terms = ring_pieces(mine, swap_cores(other))
    final_blocks = []
    for which in (core, 1 - core):
        for k in range(4):
            spot = (which, (lax.axis_index("x") + k) % 4, 0, 0)
            piece = lax.dynamic_slice(final_all, spot, (1, 1) + entering.shape)
            final_blocks.append(piece.reshape(entering.shape))
    tied = tie(*terms, *final_blocks)
    terms, final_blocks = tied[:4], tied[4:]
    middle_one, second = middle_of(terms, left_zero, tables[1])

    mlp_kept_one, mlp_back_one, hidden_one, mine, other, left_mine, left_other = mlp_both(
        gather_tokens(second), final_blocks, everything, tables[1]
    )
    terms = ring_pieces(mine, swap_cores(other))
    left_total = ring_order(left_mine, swap_cores(left_other))
    *terms, left_total = tie(*terms, left_total)
    left_total = offload_sum(left_total, "x")
    middle_grad, branch_grad, sums_one = middle_back(terms, final_blocks[0], middle_one, tables[1])
    grads_shape = (width, 12 * local)
    grads_one = grad_part(mlp_part_kernel, 2 * 10**9, [mlp_kept_one, mlp_back_one], grads_shape, 8 * local)
    blocks, grads_one = gather_tokens(branch_grad, grads_one)
    back, projected_one, mine, other = attend_back(1, blocks, kept_one, everything)
    terms = ring_pieces(mine, swap_cores(other))
    grads_one = grad_part(attention_part_kernel, 10**9, [kept_one, back, grads_one], grads_shape, 4 * local)
    *terms, left_total = tie(*terms, left_total)
    grads_one = offload_sum(grads_one, "z")
    down_grad, norm_one = input_back(terms, middle_grad, left_zero, tables[1])

    back, hidden_zero, mine, other = mlp_back(gather_tokens(down_grad), mlp_kept_zero, everything)
    terms = ring_pieces(mine, swap_cores(other))
    mlp_zero = mlp_grad(mlp_kept_zero, back, (width, 8 * local), True)
    mlp_zero = offload_sum(mlp_zero, RING)
    *terms, grads_one = tie(*terms, grads_one)
    grads_one = offload_sum(grads_one, RING)
    middle_grad, branch_grad, sums_zero = middle_back(terms, down_grad, middle_zero, tables[0])
    vectors = [sums_zero, hidden_zero, norm_one, sums_one, projected_one, hidden_one]

    mine, other, *slabs = attend_back(0, gather_tokens(branch_grad), kept_zero, first, vectors)
    other, mlp_zero = tie(other, mlp_zero)
    mlp_zero = offload_sum(mlp_zero, "z")

    sent = [along(slab, "z", k) for k, slab in enumerate(slabs) if k > 0]
    sums = ring_sums(mine, swap_cores(other))
    terms = around_pieces(sums)
    terms[0], grads_one = tie(terms[0], grads_one)
    slab = added(slabs[0].astype(wide), [piece.astype(wide) for piece in sent]).astype(narrow)
    slab, *terms = tie(slab, *terms)
    grad_zero, _ = input_back(terms, middle_grad, entering, tables[0])
    left_one = (middle_one + left_total.astype(wide) + tables[1][5:6]).astype(narrow)

    done_zero = jnp.concatenate([left_zero, grad_zero], axis=0)
    done_one = jnp.concatenate([left_one, down_grad], axis=0)
    done_mine = turn_back(jnp.where(low == 0, done_zero, done_one), 0)
    done_other = turn_back(jnp.where(low == 0, done_one, done_zero), 1)
    count, rows = lax.axis_size(RING), own_rows // 2
    turn_rows = lax.axis_index(RING) * rows

    def ring_slab(k):
        start = (turn_rows + k * rows) % (count * rows)
        return jnp.concatenate(
            [lax.dynamic_slice_in_dim(slab, start, rows, 0), slab[count * rows :]], axis=0
        )

    sent = [along(ring_slab(k), RING, k) for k in range(1, count)]
    slab = added(ring_slab(0).astype(wide), [piece.astype(wide) for piece in sent])

    owned_zero = jnp.concatenate([slab[:rows].astype(narrow), mlp_zero], axis=1)
    owned_one = grads_one
    got_mine = turn_back(jnp.where(low == 0, owned_zero, owned_one), 0)
    got_other = turn_back(jnp.where(low == 0, owned_one, owned_zero), 1)
    vector_sum = slab[rows:]
    vector_sum = added(vector_sum, around(vector_sum, "x"))
    vector_sum, got_mine, got_other = tie(vector_sum, got_mine, got_other)
    vector_zero, vector_one = vector_sum[:, : 2 * local], vector_sum[:, 2 * local :]
    vector_sum = jnp.where(core == 0, vector_zero, vector_one) + swap_cores(
        jnp.where(core == 0, vector_one, vector_zero)
    )
    start = turn_rows + lax.axis_index("x") * 16
    vector_owned = lax.dynamic_slice_in_dim(vector_sum[:12], start, 16, 1)
    done = jnp.stack([jnp.where(core == 0, done_mine, done_other), jnp.where(core == 0, done_other, done_mine)])
    tokens = entering.shape[0]
    activations = done[None, :, :tokens, None]
    input_grads = done[None, :, tokens:, None].astype(wide)
    got_mine, activations, input_grads = tie(got_mine, activations, input_grads)
    qkv_grad, proj_grad, fc1_grad, fc2_grad = finish(got_mine, got_other, local)
    return (
        activations,
        input_grads,
        jnp.transpose(qkv_grad, (1, 0, 2))[None],
        proj_grad[None],
        fc1_grad[None],
        fc2_grad[None],
        vector_owned[None],
    )


def solution(mesh):
    fine = Mesh(mesh.devices.reshape(2, 4, 2, 2, 4), ("core", "z", "yhi", "ylo", "x"))
    tensor = ("ylo", "x")
    dp = ("z", "yhi")
    in_specs = (
        P(None, tensor, dp, None),
        P(None, tensor, dp, None),
        P("core", dp, None, tensor),
        P("core", tensor, dp),
        P("core", dp, None, tensor),
        P("core", None, tensor, dp),
        P("core", None, dp + tensor),
    )
    out_specs = (
        P("core", None, tensor, dp, None),
        P("core", None, tensor, dp, None),
        P("core", dp, None, tensor),
        P("core", tensor, dp),
        P("core", dp, None, tensor),
        P("core", None, tensor, dp),
        P("core", None, dp + tensor),
    )
    return jax.shard_map(
        per_device, mesh=fine, in_specs=in_specs, out_specs=out_specs, check_vma=False
    )
```

```python
import functools

import jax
import jax.numpy as jnp
from jax import lax
from jax.experimental import pallas as pl
from jax.experimental.pallas import tpu as pltpu
from jax.sharding import Mesh, PartitionSpec as P

HDIM = 64
SCALE = HDIM ** (-0.5)

eps = 1e-06
wide = jnp.float32
narrow = jnp.bfloat16


RING = ("yhi", "ylo")


def swap_cores(value):
    return lax.ppermute(value, "core", [(0, 1), (1, 0)])


def along(value, axis, steps):
    count = lax.axis_size(axis)
    return lax.ppermute(value, axis, [(i, (i + steps) % count) for i in range(count)])


def around(value, axis):
    return [along(value, axis, -k) for k in range(1, lax.axis_size(axis))]


def turn(value, flip):
    pairs = [(c * 2 + y, y * 2 + (c ^ flip)) for c in range(2) for y in range(2)]
    return lax.ppermute(value, ("core", "ylo"), pairs)


def turn_back(value, flip):
    pairs = [(c * 2 + y, (y ^ flip) * 2 + c) for c in range(2) for y in range(2)]
    return lax.ppermute(value, ("core", "ylo"), pairs)


def gather_tokens(rows, *others):
    mine = [rows] + around(rows, "x")
    mine[-1], *others = lax.optimization_barrier((mine[-1], *others))
    blocks = mine + [swap_cores(block) for block in mine]
    return (blocks, *others) if others else blocks


def normalise(rows):
    center = rows - jnp.mean(rows, axis=-1, keepdims=True)
    spread = jnp.mean(center * center, axis=-1, keepdims=True)
    inverse = lax.rsqrt(spread + eps)
    return center * inverse, inverse


def norm_back(grad, gain, unit, inverse):
    pulled = grad * gain
    mean_one = jnp.mean(pulled, axis=-1, keepdims=True)
    mean_two = jnp.mean(pulled * unit, axis=-1, keepdims=True)
    return inverse * (pulled - mean_one - unit * mean_two)


def dot(a, b):
    return jnp.dot(a, b, preferred_element_type=wide)


def dot_t(a, b):
    return lax.dot_general(a, b, (((1,), (1,)), ((), ())), preferred_element_type=wide)


def t_dot(a, b):
    return lax.dot_general(a, b, (((0,), (0,)), ((), ())), preferred_element_type=wide)


def whole(refs):
    return jnp.concatenate([ref[...].astype(wide) for ref in refs], axis=0)


def column_sums(values):
    return jnp.sum(values, axis=0, keepdims=True)


def my_part():
    return lax.axis_index("core") * lax.axis_size("x") + lax.axis_index("x")


def my_columns(table, row, size):
    start = pl.multiple_of(my_part() * size, size)
    return table[row : row + 1, pl.ds(start, size)]


class Fetch:
    def __init__(self, layer, source, start, held, semaphore):
        self.held = held
        columns = source.at[layer, :, lax.axis_index("core"), :, pl.ds(start, held.shape[-1])]
        self.copy = pltpu.make_async_copy(columns, held, semaphore)
        self.copy.start()

    def __getitem__(self, key):
        if self.copy is not None:
            self.copy.wait()
            self.copy = None
        part = self.held[:, :, key[1]]
        return part.reshape(-1, part.shape[-1])


def pack_kernel(qkv, proj, packed):
    size = proj.shape[1]
    packed[:, : 3 * size] = qkv[...]
    packed[:, 3 * size :] = proj[...].astype(wide).T.astype(narrow)


def pack_all_kernel(attention, fc1, fc2, packed):
    size = fc2.shape[1]
    packed[:, : 4 * size] = attention[...]
    packed[:, 4 * size : 8 * size] = fc1[...]
    for k in range(4):
        packed[:, (8 + k) * size : (9 + k) * size] = fc2[k].astype(wide).T.astype(narrow)


def finish_kernel(lower, upper, qkv, proj, fc1, fc2):
    size = proj.shape[0]
    flip = lax.axis_index("core") == 1
    first = jnp.where(flip, upper[...].astype(wide), lower[...].astype(wide))
    second = jnp.where(flip, lower[...].astype(wide), upper[...].astype(wide))
    owned = jnp.concatenate([first, second], axis=0)
    for k in range(3):
        qkv[k] = owned[:, k * size : (k + 1) * size]
    proj[...] = owned[:, 3 * size : 4 * size].T
    for k in range(4):
        fc1[:, k, :] = owned[:, (4 + k) * size : (5 + k) * size]
        fc2[k] = owned[:, (8 + k) * size : (9 + k) * size].T


def mlp_grad_kernel(ring_first, kept, back, grads):
    width, columns = grads.shape[0], grads.shape[1] // 2
    halves = [
        t_dot(kept[:, :width], back[:, width:]).astype(narrow),
        t_dot(back[:, :width], kept[:, width : width + columns]).astype(narrow),
    ]
    for k, half in enumerate(halves):
        if ring_first:
            size = width // 16
            order = [(z * 4 + y) * size for y in range(4) for z in range(4)]
            half = jnp.concatenate([half[start : start + size] for start in order], axis=0)
        grads[:, k * columns : (k + 1) * columns] = half


def store_columns(held, grads, start, semaphore):
    columns = grads.at[:, pl.ds(start, held.shape[1])]
    copy = pltpu.make_async_copy(held, columns, semaphore)
    copy.start()
    copy.wait()


def mlp_part_kernel(kept, back, grads, held, semaphore):
    width, columns = held.shape[0], held.shape[1] // 2
    held[:, :columns] = t_dot(kept[:, :width], back[:, width:]).astype(narrow)
    held[:, columns:] = t_dot(back[:, :width], kept[:, width:]).astype(narrow)
    store_columns(held, grads, columns, semaphore)


def attention_part_kernel(kept, back, _, grads, held, semaphore):
    width, local = held.shape[0], held.shape[1] // 4
    held[:, : 3 * local] = t_dot(kept[:, :width], back[:, width:]).astype(narrow)
    held[:, 3 * local :] = t_dot(back[:, :width], kept[:, width + 3 * local :]).astype(narrow)
    store_columns(held, grads, 0, semaphore)


def ring_kernel(mine, other, own, *pieces):
    total = mine[...] + other[...].astype(wide)
    rows = own.shape[0]
    own[...] = total[:rows]
    for k, piece in enumerate(pieces):
        piece[...] = total[(k + 1) * rows : (k + 2) * rows].astype(narrow)


def ring_order_kernel(mine, other, ordered, total):
    total[...] = mine[...].astype(wide) + other[...].astype(wide)
    count = lax.axis_size("x")
    rows = total.shape[0] // count
    blocks = []
    for k in range(count):
        first = lax.rem(k + count - lax.axis_index("x"), count) * rows
        blocks.append(total[pl.ds(pl.multiple_of(first, 8), rows), :])
    ordered[...] = jnp.concatenate(blocks, axis=0).astype(narrow)


def summed(refs):
    total = refs[0][...]
    for piece in refs[1:]:
        total = total + piece[...].astype(wide)
    return total


def middle_kernel(own, one, two, three, arriving, table, middle, second):
    total = arriving[...].astype(wide) + summed((own, one, two, three)) + table[4:5, :]
    middle[...] = total
    second[...] = (normalise(total)[0] * table[2:3, :] + table[3:4, :]).astype(narrow)


def leave_kernel(own, one, two, three, middle, table, *refs):
    left = (middle[...] + summed((own, one, two, three)) + table[5:6, :]).astype(narrow)
    following, leaving, normed = refs
    leaving[...] = left
    unit = normalise(left.astype(wide))[0]
    normed[...] = (unit * following[0:1, :] + following[1:2, :]).astype(narrow)


def middle_back_kernel(own, one, two, three, grad, middle, table, middle_grad, branch_grad, sums):
    second_grad = summed((own, one, two, three))
    unit, inverse = normalise(middle[...])
    arriving = grad[...].astype(wide)
    total = arriving + norm_back(second_grad, table[2:3, :], unit, inverse)
    middle_grad[...] = total
    branch = total.astype(narrow)
    branch_grad[...] = branch
    sums[0:1, :] = column_sums(second_grad * unit)
    sums[1:2, :] = column_sums(second_grad)
    sums[2:3, :] = column_sums(branch.astype(wide))
    sums[3:4, :] = column_sums(arriving)


def input_back_kernel(own, one, two, three, middle_grad, arriving, table, down_grad, sums):
    normed_grad = summed((own, one, two, three))
    unit, inverse = normalise(arriving[...].astype(wide))
    total = middle_grad[...] + norm_back(normed_grad, table[0:1, :], unit, inverse)
    down_grad[...] = total.astype(narrow)
    sums[0:1, :] = column_sums(normed_grad * unit)
    sums[1:2, :] = column_sums(normed_grad)


def attend_kernel(layer, *refs):
    blocks, (matrix, table, kept, part_mine, part_other, *fetch) = refs[:8], refs[8:]
    rows, width, local = kept.shape[0], part_mine.shape[1], 2 * HDIM
    half = rows // 2
    if layer == 1:
        matrix = Fetch(layer, matrix, 0, *fetch)
    if layer == 0:
        unit = normalise(whole(blocks))[0]
        kept[:, width + 4 * local :] = unit.astype(narrow)
        kept[:, :width] = (unit * table[0:1, :] + table[1:2, :]).astype(narrow)
    else:
        kept[:, :width] = whole(blocks).astype(narrow)
    query_bias, value_bias = my_columns(table, 6, local), my_columns(table, 7, local)
    bias = jnp.concatenate([query_bias, jnp.zeros_like(query_bias), value_bias], axis=1)
    projected = (dot(kept[:, :width], matrix[:, : 3 * local]) + bias).astype(narrow)
    kept[:, width : width + 3 * local] = projected
    queries = projected[:, :local]
    key_rows = projected[:, local : 2 * local]
    value_rows = projected[:, 2 * local :]
    lower = lax.broadcasted_iota(jnp.int32, (rows, local), 1) < HDIM
    outs = []
    for keep in (lower, ~lower):
        scores = dot_t(jnp.where(keep, queries, jnp.zeros_like(queries)), key_rows) * SCALE
        raised = jnp.exp(scores - jnp.max(scores, axis=-1, keepdims=True))
        probs = raised * (1.0 / jnp.sum(raised, axis=-1, keepdims=True))
        outs.append(dot(probs.astype(narrow), value_rows))
    mixed = jnp.where(lower, outs[0], outs[1]).astype(narrow)
    kept[:, width + 3 * local : width + 4 * local] = mixed
    proj = matrix[:, 3 * local : 4 * local]
    part_other[...] = dot_t(mixed[half:, :], proj).astype(narrow)
    part_mine[...] = dot_t(mixed[:half, :], proj)


def attend_back_kernel(layer, *refs):
    blocks, (kept, matrix, *refs) = refs[:8], refs[8:]
    local = 2 * HDIM
    rows, width = kept.shape[0], kept.shape[1] - 4 * local
    if layer == 0:
        width = width // 2
    half = rows // 2
    if layer == 0:
        vectors, (part_mine, part_other, *slabs, back) = refs[:6], refs[6:]
    else:
        back, sums, part_mine, part_other, *fetch = refs
        matrix = Fetch(layer, matrix, 0, *fetch)
    back[:, :width] = whole(blocks).astype(narrow)
    out = dot(back[:, :width], matrix[:, 3 * local : 4 * local]).astype(narrow)
    queries = kept[:, width : width + local]
    key_rows = kept[:, width + local : width + 2 * local]
    value_rows = kept[:, width + 2 * local : width + 3 * local]
    lower = lax.broadcasted_iota(jnp.int32, (rows, local), 1) < HDIM
    query_grads, key_grad, value_grad = [], 0.0, 0.0
    for keep in (lower, ~lower):
        query = jnp.where(keep, queries, jnp.zeros_like(queries))
        grad = jnp.where(keep, out, jnp.zeros_like(out))
        scores = dot_t(query, key_rows) * SCALE
        raised = jnp.exp(scores - jnp.max(scores, axis=-1, keepdims=True))
        probs = raised * (1.0 / jnp.sum(raised, axis=-1, keepdims=True))
        prob_grad = dot_t(grad, value_rows)
        inner = jnp.sum(probs * prob_grad, axis=-1, keepdims=True)
        score_grad = (probs * (prob_grad - inner)).astype(narrow)
        query_grads.append(dot(score_grad, key_rows))
        value_grad = value_grad + t_dot(probs.astype(narrow), grad)
        key_grad = key_grad + t_dot(score_grad, query)
    back[:, width : width + local] = (jnp.where(lower, query_grads[0], query_grads[1]) * SCALE).astype(narrow)
    back[:, width + local : width + 2 * local] = (key_grad * SCALE).astype(narrow)
    back[:, width + 2 * local :] = value_grad.astype(narrow)
    projected_sums = column_sums(back[:, width:].astype(wide))
    qkv = matrix[:, : 3 * local]
    other = dot_t(back[half:, width:], qkv)
    mine = dot_t(back[:half, width:], qkv)
    part_other[...] = other.astype(narrow)
    part_mine[...] = mine
    if layer == 1:
        sums[...] = projected_sums
        return
    first_unit = width + 4 * local
    gain_sum = column_sums(mine * kept[:half, first_unit:].astype(wide))
    gain_sum += column_sums(other * kept[half:, first_unit:].astype(wide))
    shift_sum = column_sums(mine) + column_sums(other)
    column = lax.broadcasted_iota(jnp.int32, (1, width), 1) // local

    def rows_of(norm_sums, middle_sums, projected, hidden):
        found = [norm_sums, middle_sums]
        for values, k in ((projected, 0), (projected, 2), (hidden, 0), (hidden, 1), (hidden, 2), (hidden, 3)):
            row = jnp.concatenate([values[:, k * local : (k + 1) * local]] * (width // local), axis=1)
            found.append(jnp.where(column == my_part(), row, 0.0))
        return jnp.concatenate(found + [jnp.zeros((4, width), wide)], axis=0).astype(narrow)

    sums_zero, hidden_zero, norm_one, sums_one, projected_one, hidden_one = (ref[...] for ref in vectors)
    norm_zero = jnp.concatenate([gain_sum, shift_sum], axis=0)
    rows_zero = rows_of(norm_zero, sums_zero, projected_sums, hidden_zero)
    rows_one = rows_of(norm_one, sums_one, projected_one, hidden_one)
    count = len(slabs)
    size = width // count
    here = lax.axis_index("z")
    for k, slab in enumerate(slabs):
        first = pl.multiple_of(lax.rem(here + k, count) * size, size)
        normed = kept[:, pl.ds(first, size)]
        branch = back[:, pl.ds(first, size)]
        slab[:size, : 3 * local] = t_dot(normed, back[:, width:]).astype(narrow)
        slab[:size, 3 * local :] = t_dot(branch, kept[:, width + 3 * local : width + 4 * local]).astype(narrow)
    for k, slab in enumerate(slabs):
        for z in range(count):

            @pl.when(lax.rem(here + k, count) == z)
            def _():
                slab[size:, :size] = rows_zero[:, z * size : (z + 1) * size]
                slab[size:, size:] = rows_one[:, z * size : (z + 1) * size]


def hidden_parts(second, fc1, table):
    local = fc1.shape[1] // 4
    bias = jnp.concatenate([my_columns(table, 8 + r, local) for r in range(4)], axis=1)
    hidden = dot(second, fc1) + bias
    share = 0.5 * (1.0 + lax.erf(hidden * (0.5**0.5)))
    slope = share + hidden * jnp.exp(-0.5 * hidden * hidden) * 0.3989422804014327
    return (hidden * share).astype(narrow), slope


def mlp_kernel(*refs):
    blocks, (matrix, table, kept, part_mine, part_other, *fetch) = refs[:8], refs[8:]
    width, columns, half = part_mine.shape[1], fetch[0].shape[2] // 2, kept.shape[0] // 2
    matrix = Fetch(0, matrix, columns, *fetch)
    kept[:, :width] = whole(blocks).astype(narrow)
    activated, slope = hidden_parts(kept[:, :width], matrix[:, :columns], table)
    kept[:, width : width + columns] = activated
    kept[:, width + columns :] = slope.astype(narrow)
    part_other[...] = dot_t(activated[half:, :], matrix[:, columns:]).astype(narrow)
    part_mine[...] = dot_t(activated[:half, :], matrix[:, columns:])


def mlp_back_kernel(*refs):
    blocks, (kept, matrix, back, sums, part_mine, part_other, *fetch) = refs[:8], refs[8:]
    width, columns, half = part_mine.shape[1], fetch[0].shape[2] // 2, kept.shape[0] // 2
    matrix = Fetch(0, matrix, columns, *fetch)
    back[:, :width] = whole(blocks).astype(narrow)
    slope = kept[:, width + columns :].astype(wide)
    hidden_grad = (dot(back[:, :width], matrix[:, columns:]) * slope).astype(narrow)
    back[:, width:] = hidden_grad
    sums[...] = column_sums(hidden_grad.astype(wide))
    part_other[...] = dot_t(hidden_grad[half:, :], matrix[:, :columns]).astype(narrow)
    part_mine[...] = dot_t(hidden_grad[:half, :], matrix[:, :columns])


def mlp_both_kernel(*refs):
    blocks, final, (matrix, table, kept, back, sums, part_mine, part_other, left_mine, left_other, *fetch) = refs[:8], refs[8:16], refs[16:]
    width, columns, half = part_mine.shape[1], fetch[0].shape[2] // 2, kept.shape[0] // 2
    matrix = Fetch(1, matrix, columns, *fetch)
    kept[:, :width] = whole(blocks).astype(narrow)
    back[:, :width] = whole(final).astype(narrow)
    activated, slope = hidden_parts(kept[:, :width], matrix[:, :columns], table)
    kept[:, width:] = activated
    hidden_grad = (dot(back[:, :width], matrix[:, columns:]) * slope).astype(narrow)
    back[:, width:] = hidden_grad
    sums[...] = column_sums(hidden_grad.astype(wide))
    part_other[...] = dot_t(hidden_grad[half:, :], matrix[:, :columns]).astype(narrow)
    part_mine[...] = dot_t(hidden_grad[:half, :], matrix[:, :columns])
    left_other[...] = dot_t(activated[half:, :], matrix[:, columns:]).astype(narrow)
    left_mine[...] = dot_t(activated[:half, :], matrix[:, columns:]).astype(narrow)


def call(body, flops, outs, args, scratch=(), fetch=None, columns=None):
    specs = [pl.BlockSpec()] * len(args)
    scratch = list(scratch)
    if fetch is not None:
        shape = args[fetch].shape
        specs[fetch] = pl.BlockSpec(memory_space=pl.ANY)
        scratch += [pltpu.VMEM((shape[1], shape[3], columns), narrow), pltpu.SemaphoreType.DMA]
    return pl.pallas_call(
        body,
        out_shape=[jax.ShapeDtypeStruct(shape, kind) for shape, kind in outs],
        in_specs=specs,
        scratch_shapes=scratch,
        compiler_params=pltpu.CompilerParams(vmem_limit_bytes=48 << 20),
        cost_estimate=pl.CostEstimate(flops=flops, bytes_accessed=8 << 20, transcendentals=0),
    )(*args)


def partials(rows, width):
    return [((rows // 2, width), wide), ((rows // 2, width), narrow)]


def attend(layer, blocks, matrix, table):
    rows, width, columns = 8 * blocks[0].shape[0], blocks[0].shape[1], 8 * HDIM
    outs = [((rows, width + columns + width * (layer == 0)), narrow)] + partials(rows, width)
    body = functools.partial(attend_kernel, layer)
    fetch = (8, columns) if layer else (None, None)
    return call(body, 3 * 10**9, outs, [*blocks, matrix, table], (), *fetch)


def attend_back(layer, blocks, kept, matrix, vectors=()):
    rows, width, columns = kept.shape[0], blocks[0].shape[1], 8 * HDIM
    back = (rows, width + columns // 4 * 3)
    if layer == 0:
        count = lax.axis_size("z")
        outs = partials(rows, width) + [((width // count + 16, columns), narrow)] * count
        scratch = [pltpu.VMEM(back, narrow)]
    else:
        outs = [(back, narrow), ((1, columns // 4 * 3), wide)] + partials(rows, width)
        scratch = []
    body = functools.partial(attend_back_kernel, layer)
    fetch = (9, columns) if layer else (None, None)
    return call(body, 6 * 10**9, outs, [*blocks, kept, matrix, *vectors], scratch, *fetch)


def mlp(blocks, matrix, table):
    rows, width, columns = 8 * blocks[0].shape[0], blocks[0].shape[1], matrix.shape[4] // 3
    outs = [((rows, width + 2 * columns), narrow)] + partials(rows, width)
    return call(mlp_kernel, 4 * 10**9, outs, [*blocks, matrix, table], (), 8, 2 * columns)


def mlp_back(blocks, kept, matrix):
    rows, width, columns = kept.shape[0], blocks[0].shape[1], matrix.shape[4] // 3
    outs = [((rows, width + columns), narrow), ((1, columns), wide)] + partials(rows, width)
    return call(mlp_back_kernel, 4 * 10**9, outs, [*blocks, kept, matrix], (), 9, 2 * columns)


def mlp_both(blocks, final, matrix, table):
    rows, width, columns = 8 * blocks[0].shape[0], blocks[0].shape[1], matrix.shape[4] // 3
    outs = [((rows, width + columns), narrow)] * 2 + [((1, columns), wide)] + partials(rows, width)
    outs += [((rows // 2, width), narrow)] * 2
    return call(mlp_both_kernel, 6 * 10**9, outs, [*blocks, *final, matrix, table], (), 16, 2 * columns)


def pack(qkv, proj):
    rows, size = proj.shape
    return call(pack_kernel, 10**8, [((rows, 4 * size), narrow)], [qkv, proj])[0]


def pack_all(attention, fc1, fc2):
    shape = (attention.shape[0], 3 * attention.shape[1])
    return call(pack_all_kernel, 10**8, [(shape, narrow)], [attention, fc1, fc2])[0]


def ring_sums(mine, other):
    count = lax.axis_size("x")
    shape = (mine.shape[0] // count, mine.shape[1])
    outs = [(shape, wide)] + [(shape, narrow)] * (count - 1)
    return list(call(ring_kernel, 10**8, outs, [mine, other]))


def around_pieces(sums):
    return [sums[0]] + [along(piece, "x", k) for k, piece in enumerate(sums[1:], 1)]


def ring_pieces(mine, other):
    return around_pieces(ring_sums(mine, other))


def ring_order(mine, other):
    scratch = [pltpu.VMEM(mine.shape, wide)]
    return call(ring_order_kernel, 10**8, [(mine.shape, narrow)], [mine, other], scratch)[0]


def middle_of(terms, arriving, table):
    shape = arriving.shape
    return call(middle_kernel, 10**8, [(shape, wide), (shape, narrow)], [*terms, arriving, table])


def leave(terms, middle, table, following):
    return call(leave_kernel, 10**8, [(middle.shape, narrow)] * 2, [*terms, middle, table, following])


def middle_back(terms, grad, middle, table):
    shape = middle.shape
    outs = [(shape, wide), (shape, narrow), ((4, shape[1]), wide)]
    return call(middle_back_kernel, 10**8, outs, [*terms, grad, middle, table])


def input_back(terms, middle_grad, arriving, table):
    shape = arriving.shape
    outs = [(shape, narrow), ((2, shape[1]), wide)]
    return call(input_back_kernel, 10**8, outs, [*terms, middle_grad, arriving, table])


def mlp_grad(kept, back, shape, ring_first=False):
    return call(functools.partial(mlp_grad_kernel, ring_first), 2 * 10**9, [(shape, narrow)], [kept, back])[0]


def grad_part(body, flops, args, shape, columns):
    whole_array = pl.BlockSpec(memory_space=pl.ANY)
    added = len(args) == 3
    return pl.pallas_call(
        body,
        out_shape=jax.ShapeDtypeStruct(shape, narrow),
        in_specs=[pl.BlockSpec()] * 2 + [whole_array] * added,
        out_specs=whole_array,
        input_output_aliases={2: 0} if added else {},
        scratch_shapes=[pltpu.VMEM((shape[0], columns), narrow), pltpu.SemaphoreType.DMA],
        compiler_params=pltpu.CompilerParams(vmem_limit_bytes=48 << 20),
        cost_estimate=pl.CostEstimate(flops=flops, bytes_accessed=8 << 20, transcendentals=0),
    )(*args)


def finish(lower, upper, size):
    shapes = [(3, size, size), (size, size), (size, 4, size), (4, size, size)]
    return call(finish_kernel, 10**8, [(shape, wide) for shape in shapes], [lower, upper])


def tie(*values):
    return lax.optimization_barrier(values)


def hop(columns, layer):
    return lax.ppermute(columns, ("core", "ylo"), [(layer * 2, 0), (layer * 2 + 1, 3)])


def order_ring(own, arrived):
    core, high, low = (lax.axis_index(name) for name in ("core", "yhi", "ylo"))
    one, two, three = arrived
    holder = low == core
    a = jnp.where(holder, own, one)
    b = jnp.where(holder, two, three)
    place = high * 2 + low
    a_first = jnp.where(holder, high, (place + 1) % 4 // 2) == 0
    return jnp.concatenate([jnp.where(a_first, a, b), jnp.where(a_first, b, a)], axis=0)


def fold(zero, one):
    half = zero.shape[1] // 2
    return jnp.concatenate([zero[:, :half], zero[:, half:], one[:, :half], one[:, half:]], axis=0)


def unfold(rows):
    return [jnp.concatenate([rows[k : k + 12], rows[k + 12 : k + 24]], axis=1) for k in (0, 24)]


def per_device(inputs, cotangent, qkv_weight, proj_weight, fc1_weight, fc2_weight, vectors):
    width = inputs.shape[3]
    core = lax.axis_index("core")
    low = lax.axis_index("ylo")
    place = lax.axis_index(("z", "yhi", "ylo", "x"))
    local = qkv_weight.shape[3]
    own_rows = qkv_weight.shape[1]

    def added(values, arrived):
        return functools.reduce(lambda a, b: a + b, arrived, values)

    columns = lax.broadcasted_iota(jnp.int32, (12, width), 1) // 16
    table = jnp.where(columns == place, jnp.tile(vectors[0], (1, width // 16)), 0).astype(narrow)
    other_table = swap_cores(table)
    table = fold(jnp.where(core == 0, table, other_table), jnp.where(core == 0, other_table, table))
    attention_raw = pack(qkv_weight[0].reshape(own_rows, 3 * local), proj_weight[0])
    table, attention_raw, fc1_weight, fc2_weight = tie(table, attention_raw, fc1_weight, fc2_weight)
    raw = pack_all(attention_raw, fc1_weight[0].reshape(own_rows, 4 * local), fc2_weight[0])
    held = hop(attention_raw, 0)
    entering = turn(lax.dynamic_index_in_dim(inputs, core, 0, keepdims=False)[:, 0], 0)
    table = added(table, around(table, "x"))
    held, entering, table = tie(held, entering, table)
    mine = [entering] + around(entering, "x")
    arrived = around(jnp.concatenate([held, table], axis=0), RING)
    *arrived, raw = tie(*arrived, raw)
    blocks = order_ring(held, [piece[:own_rows] for piece in arrived])
    table = added(table, [piece[own_rows:] for piece in arrived])

    def gather_weights(rows):
        gathered = lax.all_gather(rows, ("core", "z", "yhi", "ylo"), axis=0, tiled=True)
        return gathered.reshape(2, 8, 2, own_rows, rows.shape[1])

    everything = gather_weights(raw)

    arrived = around(jnp.concatenate([blocks, table], axis=0), "z")
    mine[1], cotangent = tie(mine[1], cotangent)
    final_grad = turn(lax.dynamic_index_in_dim(cotangent, core, 0, keepdims=False)[:, 0], 0)
    entering_all = mine + [swap_cores(block) for block in mine]
    parts = [blocks] + [piece[: 2 * own_rows] for piece in arrived]
    start = (len(parts) - 1 - lax.axis_index("z")) * 2 * own_rows
    first = lax.dynamic_slice_in_dim(jnp.concatenate(parts[1:] + parts, axis=0), start, width, 0)
    tables = [t.astype(wide) for t in unfold(added(table, [piece[2 * own_rows :] for piece in arrived]))]

    def offload_sum(value, axis):
        return lax.psum_scatter(value, axis, scatter_dimension=0, tiled=True)

    kept_zero, mine, other = attend(0, entering_all, first, tables[0])
    terms = ring_pieces(mine, swap_cores(other))

    *terms, final_grad = tie(*terms, final_grad)
    final_all = lax.all_gather(final_grad, ("core", "x")).reshape((2, 4) + entering.shape)

    middle_zero, second = middle_of(terms, entering, tables[0])
    mlp_kept_zero, mine, other = mlp(gather_tokens(second), everything, tables[0])

    terms = ring_pieces(mine, swap_cores(other))
    left_zero, normed = leave(terms, middle_zero, tables[0], tables[1])
    kept_one, mine, other = attend(1, gather_tokens(normed), everything, tables[1])
    terms = ring_pieces(mine, swap_cores(other))
    final_blocks = []
    for which in (core, 1 - core):
        for k in range(4):
            spot = (which, (lax.axis_index("x") + k) % 4, 0, 0)
            piece = lax.dynamic_slice(final_all, spot, (1, 1) + entering.shape)
            final_blocks.append(piece.reshape(entering.shape))
    tied = tie(*terms, *final_blocks)
    terms, final_blocks = tied[:4], tied[4:]
    middle_one, second = middle_of(terms, left_zero, tables[1])

    mlp_kept_one, mlp_back_one, hidden_one, mine, other, left_mine, left_other = mlp_both(
        gather_tokens(second), final_blocks, everything, tables[1]
    )
    terms = ring_pieces(mine, swap_cores(other))
    left_total = ring_order(left_mine, swap_cores(left_other))
    *terms, left_total = tie(*terms, left_total)
    left_total = offload_sum(left_total, "x")
    middle_grad, branch_grad, sums_one = middle_back(terms, final_blocks[0], middle_one, tables[1])
    grads_shape = (width, 12 * local)
    grads_one = grad_part(mlp_part_kernel, 2 * 10**9, [mlp_kept_one, mlp_back_one], grads_shape, 8 * local)
    blocks, grads_one = gather_tokens(branch_grad, grads_one)
    back, projected_one, mine, other = attend_back(1, blocks, kept_one, everything)
    terms = ring_pieces(mine, swap_cores(other))
    grads_one = grad_part(attention_part_kernel, 10**9, [kept_one, back, grads_one], grads_shape, 4 * local)
    *terms, left_total = tie(*terms, left_total)
    grads_one = offload_sum(grads_one, "z")
    down_grad, norm_one = input_back(terms, middle_grad, left_zero, tables[1])

    back, hidden_zero, mine, other = mlp_back(gather_tokens(down_grad), mlp_kept_zero, everything)
    terms = ring_pieces(mine, swap_cores(other))
    mlp_zero = mlp_grad(mlp_kept_zero, back, (width, 8 * local), True)
    mlp_zero = offload_sum(mlp_zero, RING)
    *terms, grads_one = tie(*terms, grads_one)
    grads_one = offload_sum(grads_one, RING)
    middle_grad, branch_grad, sums_zero = middle_back(terms, down_grad, middle_zero, tables[0])
    vectors = [sums_zero, hidden_zero, norm_one, sums_one, projected_one, hidden_one]

    mine, other, *slabs = attend_back(0, gather_tokens(branch_grad), kept_zero, first, vectors)
    other, mlp_zero = tie(other, mlp_zero)
    mlp_zero = offload_sum(mlp_zero, "z")

    sent = [along(slab, "z", k) for k, slab in enumerate(slabs) if k > 0]
    sums = ring_sums(mine, swap_cores(other))
    terms = around_pieces(sums)
    terms[0], grads_one = tie(terms[0], grads_one)
    slab = added(slabs[0].astype(wide), [piece.astype(wide) for piece in sent]).astype(narrow)
    slab, *terms = tie(slab, *terms)
    grad_zero, _ = input_back(terms, middle_grad, entering, tables[0])
    left_one = (middle_one + left_total.astype(wide) + tables[1][5:6]).astype(narrow)

    done_zero = jnp.concatenate([left_zero, grad_zero], axis=0)
    done_one = jnp.concatenate([left_one, down_grad], axis=0)
    done_mine = turn_back(jnp.where(low == 0, done_zero, done_one), 0)
    done_other = turn_back(jnp.where(low == 0, done_one, done_zero), 1)
    count, rows = lax.axis_size(RING), own_rows // 2
    turn_rows = lax.axis_index(RING) * rows

    def ring_slab(k):
        start = (turn_rows + k * rows) % (count * rows)
        return jnp.concatenate(
            [lax.dynamic_slice_in_dim(slab, start, rows, 0), slab[count * rows :]], axis=0
        )

    sent = [along(ring_slab(k), RING, k) for k in range(1, count)]
    slab = added(ring_slab(0).astype(wide), [piece.astype(wide) for piece in sent])

    done = jnp.stack([jnp.where(core == 0, done_mine, done_other), jnp.where(core == 0, done_other, done_mine)])
    tokens = entering.shape[0]
    activations = done[None, :, :tokens, None]
    input_grads = done[None, :, tokens:, None].astype(wide)
    grads_one, activations, input_grads = tie(grads_one, activations, input_grads)

    owned_zero = jnp.concatenate([slab[:rows].astype(narrow), mlp_zero], axis=1)
    owned_one = grads_one
    got_mine = turn_back(jnp.where(low == 0, owned_zero, owned_one), 0)
    got_other = turn_back(jnp.where(low == 0, owned_one, owned_zero), 1)
    vector_sum = slab[rows:]
    vector_sum = added(vector_sum, around(vector_sum, "x"))
    vector_sum, got_mine, got_other = tie(vector_sum, got_mine, got_other)
    vector_zero, vector_one = vector_sum[:, : 2 * local], vector_sum[:, 2 * local :]
    vector_sum = jnp.where(core == 0, vector_zero, vector_one) + swap_cores(
        jnp.where(core == 0, vector_one, vector_zero)
    )
    start = turn_rows + lax.axis_index("x") * 16
    vector_owned = lax.dynamic_slice_in_dim(vector_sum[:12], start, 16, 1)
    qkv_grad, proj_grad, fc1_grad, fc2_grad = finish(got_mine, got_other, local)
    return (
        activations,
        input_grads,
        jnp.transpose(qkv_grad, (1, 0, 2))[None],
        proj_grad[None],
        fc1_grad[None],
        fc2_grad[None],
        vector_owned[None],
    )


def solution(mesh):
    fine = Mesh(mesh.devices.reshape(2, 4, 2, 2, 4), ("core", "z", "yhi", "ylo", "x"))
    tensor = ("ylo", "x")
    dp = ("z", "yhi")
    in_specs = (
        P(None, tensor, dp, None),
        P(None, tensor, dp, None),
        P("core", dp, None, tensor),
        P("core", tensor, dp),
        P("core", dp, None, tensor),
        P("core", None, tensor, dp),
        P("core", None, dp + tensor),
    )
    out_specs = (
        P("core", None, tensor, dp, None),
        P("core", None, tensor, dp, None),
        P("core", dp, None, tensor),
        P("core", tensor, dp),
        P("core", dp, None, tensor),
        P("core", None, tensor, dp),
        P("core", None, dp + tensor),
    )
    return jax.shard_map(
        per_device, mesh=fine, in_specs=in_specs, out_specs=out_specs, check_vma=False
    )
```

```python
import functools

import jax
import jax.numpy as jnp
from jax import lax
from jax.experimental import pallas as pl
from jax.experimental.pallas import tpu as pltpu
from jax.sharding import Mesh, PartitionSpec as P

HDIM = 64
SCALE = HDIM ** (-0.5)

eps = 1e-06
wide = jnp.float32
narrow = jnp.bfloat16


RING = ("yhi", "ylo")


def swap_cores(value):
    return lax.ppermute(value, "core", [(0, 1), (1, 0)])


def along(value, axis, steps):
    count = lax.axis_size(axis)
    return lax.ppermute(value, axis, [(i, (i + steps) % count) for i in range(count)])


def around(value, axis):
    return [along(value, axis, -k) for k in range(1, lax.axis_size(axis))]


def turn(value, flip):
    pairs = [(c * 2 + y, y * 2 + (c ^ flip)) for c in range(2) for y in range(2)]
    return lax.ppermute(value, ("core", "ylo"), pairs)


def turn_back(value, flip):
    pairs = [(c * 2 + y, (y ^ flip) * 2 + c) for c in range(2) for y in range(2)]
    return lax.ppermute(value, ("core", "ylo"), pairs)


def gather_tokens(rows, *others):
    mine = [rows] + around(rows, "x")
    mine[-1], *others = lax.optimization_barrier((mine[-1], *others))
    blocks = mine + [swap_cores(block) for block in mine]
    return (blocks, *others) if others else blocks


def normalise(rows):
    center = rows - jnp.mean(rows, axis=-1, keepdims=True)
    spread = jnp.mean(center * center, axis=-1, keepdims=True)
    inverse = lax.rsqrt(spread + eps)
    return center * inverse, inverse


def norm_back(grad, gain, unit, inverse):
    pulled = grad * gain
    mean_one = jnp.mean(pulled, axis=-1, keepdims=True)
    mean_two = jnp.mean(pulled * unit, axis=-1, keepdims=True)
    return inverse * (pulled - mean_one - unit * mean_two)


def dot(a, b):
    return jnp.dot(a, b, preferred_element_type=wide)


def dot_t(a, b):
    return lax.dot_general(a, b, (((1,), (1,)), ((), ())), preferred_element_type=wide)


def t_dot(a, b):
    return lax.dot_general(a, b, (((0,), (0,)), ((), ())), preferred_element_type=wide)


def whole(refs):
    return jnp.concatenate([ref[...].astype(wide) for ref in refs], axis=0)


def column_sums(values):
    return jnp.sum(values, axis=0, keepdims=True)


def my_part():
    return lax.axis_index("core") * lax.axis_size("x") + lax.axis_index("x")


def my_columns(table, row, size):
    start = pl.multiple_of(my_part() * size, size)
    return table[row : row + 1, pl.ds(start, size)]


class Fetch:
    def __init__(self, layer, source, start, held, semaphore):
        self.held = held
        columns = source.at[layer, :, lax.axis_index("core"), :, pl.ds(start, held.shape[-1])]
        self.copy = pltpu.make_async_copy(columns, held, semaphore)
        self.copy.start()

    def __getitem__(self, key):
        if self.copy is not None:
            self.copy.wait()
            self.copy = None
        part = self.held[:, :, key[1]]
        return part.reshape(-1, part.shape[-1])


def pack_kernel(qkv, proj, packed):
    size = proj.shape[1]
    packed[:, : 3 * size] = qkv[...]
    packed[:, 3 * size :] = proj[...].astype(wide).T.astype(narrow)


def pack_all_kernel(attention, fc1, fc2, packed):
    size = fc2.shape[1]
    packed[:, : 4 * size] = attention[...]
    packed[:, 4 * size : 8 * size] = fc1[...]
    for k in range(4):
        packed[:, (8 + k) * size : (9 + k) * size] = fc2[k].astype(wide).T.astype(narrow)


def finish_kernel(lower, upper, qkv, proj, fc1, fc2):
    size = proj.shape[0]
    flip = lax.axis_index("core") == 1
    first = jnp.where(flip, upper[...].astype(wide), lower[...].astype(wide))
    second = jnp.where(flip, lower[...].astype(wide), upper[...].astype(wide))
    owned = jnp.concatenate([first, second], axis=0)
    for k in range(3):
        qkv[k] = owned[:, k * size : (k + 1) * size]
    proj[...] = owned[:, 3 * size : 4 * size].T
    for k in range(4):
        fc1[:, k, :] = owned[:, (4 + k) * size : (5 + k) * size]
        fc2[k] = owned[:, (8 + k) * size : (9 + k) * size].T


def mlp_grad_kernel(ring_first, kept, back, grads):
    width, columns = grads.shape[0], grads.shape[1] // 2
    halves = [
        t_dot(kept[:, :width], back[:, width:]).astype(narrow),
        t_dot(back[:, :width], kept[:, width : width + columns]).astype(narrow),
    ]
    for k, half in enumerate(halves):
        if ring_first:
            size = width // 16
            order = [(z * 4 + y) * size for y in range(4) for z in range(4)]
            half = jnp.concatenate([half[start : start + size] for start in order], axis=0)
        grads[:, k * columns : (k + 1) * columns] = half


def store_columns(held, grads, start, semaphore):
    columns = grads.at[:, pl.ds(start, held.shape[1])]
    copy = pltpu.make_async_copy(held, columns, semaphore)
    copy.start()
    copy.wait()


def mlp_part_kernel(kept, back, grads, held, semaphore):
    width, columns = held.shape[0], held.shape[1] // 2
    held[:, :columns] = t_dot(kept[:, :width], back[:, width:]).astype(narrow)
    held[:, columns:] = t_dot(back[:, :width], kept[:, width:]).astype(narrow)
    store_columns(held, grads, columns, semaphore)


def attention_part_kernel(kept, back, _, grads, held, semaphore):
    width, local = held.shape[0], held.shape[1] // 4
    held[:, : 3 * local] = t_dot(kept[:, :width], back[:, width:]).astype(narrow)
    held[:, 3 * local :] = t_dot(back[:, :width], kept[:, width + 3 * local :]).astype(narrow)
    store_columns(held, grads, 0, semaphore)


def ring_kernel(mine, other, own, *pieces):
    total = mine[...] + other[...].astype(wide)
    rows = own.shape[0]
    own[...] = total[:rows]
    for k, piece in enumerate(pieces):
        piece[...] = total[(k + 1) * rows : (k + 2) * rows].astype(narrow)


def ring_order_kernel(mine, other, ordered, total):
    total[...] = mine[...].astype(wide) + other[...].astype(wide)
    count = lax.axis_size("x")
    rows = total.shape[0] // count
    blocks = []
    for k in range(count):
        first = lax.rem(k + count - lax.axis_index("x"), count) * rows
        blocks.append(total[pl.ds(pl.multiple_of(first, 8), rows), :])
    ordered[...] = jnp.concatenate(blocks, axis=0).astype(narrow)


def summed(refs):
    total = refs[0][...]
    for piece in refs[1:]:
        total = total + piece[...].astype(wide)
    return total


def middle_kernel(own, one, two, three, arriving, table, middle, second):
    total = arriving[...].astype(wide) + summed((own, one, two, three)) + table[4:5, :]
    middle[...] = total
    second[...] = (normalise(total)[0] * table[2:3, :] + table[3:4, :]).astype(narrow)


def leave_kernel(own, one, two, three, middle, table, *refs):
    left = (middle[...] + summed((own, one, two, three)) + table[5:6, :]).astype(narrow)
    following, leaving, normed = refs
    leaving[...] = left
    unit = normalise(left.astype(wide))[0]
    normed[...] = (unit * following[0:1, :] + following[1:2, :]).astype(narrow)


def middle_back_kernel(own, one, two, three, grad, middle, table, middle_grad, branch_grad, sums):
    second_grad = summed((own, one, two, three))
    unit, inverse = normalise(middle[...])
    arriving = grad[...].astype(wide)
    total = arriving + norm_back(second_grad, table[2:3, :], unit, inverse)
    middle_grad[...] = total
    branch = total.astype(narrow)
    branch_grad[...] = branch
    sums[0:1, :] = column_sums(second_grad * unit)
    sums[1:2, :] = column_sums(second_grad)
    sums[2:3, :] = column_sums(branch.astype(wide))
    sums[3:4, :] = column_sums(arriving)


def input_back_kernel(own, one, two, three, middle_grad, arriving, table, down_grad, sums):
    normed_grad = summed((own, one, two, three))
    unit, inverse = normalise(arriving[...].astype(wide))
    total = middle_grad[...] + norm_back(normed_grad, table[0:1, :], unit, inverse)
    down_grad[...] = total.astype(narrow)
    sums[0:1, :] = column_sums(normed_grad * unit)
    sums[1:2, :] = column_sums(normed_grad)


def attend_kernel(layer, *refs):
    blocks, (matrix, table, kept, part_mine, part_other, *fetch) = refs[:8], refs[8:]
    rows, width, local = kept.shape[0], part_mine.shape[1], 2 * HDIM
    half = rows // 2
    if layer == 1:
        matrix = Fetch(layer, matrix, 0, *fetch)
    if layer == 0:
        unit = normalise(whole(blocks))[0]
        kept[:, width + 4 * local :] = unit.astype(narrow)
        kept[:, :width] = (unit * table[0:1, :] + table[1:2, :]).astype(narrow)
    else:
        kept[:, :width] = whole(blocks).astype(narrow)
    query_bias, value_bias = my_columns(table, 6, local), my_columns(table, 7, local)
    bias = jnp.concatenate([query_bias, jnp.zeros_like(query_bias), value_bias], axis=1)
    projected = (dot(kept[:, :width], matrix[:, : 3 * local]) + bias).astype(narrow)
    kept[:, width : width + 3 * local] = projected
    queries = projected[:, :local]
    key_rows = projected[:, local : 2 * local]
    value_rows = projected[:, 2 * local :]
    lower = lax.broadcasted_iota(jnp.int32, (rows, local), 1) < HDIM
    outs = []
    for keep in (lower, ~lower):
        scores = dot_t(jnp.where(keep, queries, jnp.zeros_like(queries)), key_rows) * SCALE
        raised = jnp.exp(scores - jnp.max(scores, axis=-1, keepdims=True))
        probs = raised * (1.0 / jnp.sum(raised, axis=-1, keepdims=True))
        outs.append(dot(probs.astype(narrow), value_rows))
    mixed = jnp.where(lower, outs[0], outs[1]).astype(narrow)
    kept[:, width + 3 * local : width + 4 * local] = mixed
    proj = matrix[:, 3 * local : 4 * local]
    part_other[...] = dot_t(mixed[half:, :], proj).astype(narrow)
    part_mine[...] = dot_t(mixed[:half, :], proj)


def attend_back_kernel(layer, *refs):
    blocks, (kept, matrix, *refs) = refs[:8], refs[8:]
    local = 2 * HDIM
    rows, width = kept.shape[0], kept.shape[1] - 4 * local
    if layer == 0:
        width = width // 2
    half = rows // 2
    if layer == 0:
        vectors, (part_mine, part_other, *slabs, back) = refs[:6], refs[6:]
    else:
        back, sums, part_mine, part_other, *fetch = refs
        matrix = Fetch(layer, matrix, 0, *fetch)
    back[:, :width] = whole(blocks).astype(narrow)
    out = dot(back[:, :width], matrix[:, 3 * local : 4 * local]).astype(narrow)
    queries = kept[:, width : width + local]
    key_rows = kept[:, width + local : width + 2 * local]
    value_rows = kept[:, width + 2 * local : width + 3 * local]
    lower = lax.broadcasted_iota(jnp.int32, (rows, local), 1) < HDIM
    query_grads, key_grad, value_grad = [], 0.0, 0.0
    for keep in (lower, ~lower):
        query = jnp.where(keep, queries, jnp.zeros_like(queries))
        grad = jnp.where(keep, out, jnp.zeros_like(out))
        scores = dot_t(query, key_rows) * SCALE
        raised = jnp.exp(scores - jnp.max(scores, axis=-1, keepdims=True))
        probs = raised * (1.0 / jnp.sum(raised, axis=-1, keepdims=True))
        prob_grad = dot_t(grad, value_rows)
        inner = jnp.sum(probs * prob_grad, axis=-1, keepdims=True)
        score_grad = (probs * (prob_grad - inner)).astype(narrow)
        query_grads.append(dot(score_grad, key_rows))
        value_grad = value_grad + t_dot(probs.astype(narrow), grad)
        key_grad = key_grad + t_dot(score_grad, query)
    back[:, width : width + local] = (jnp.where(lower, query_grads[0], query_grads[1]) * SCALE).astype(narrow)
    back[:, width + local : width + 2 * local] = (key_grad * SCALE).astype(narrow)
    back[:, width + 2 * local :] = value_grad.astype(narrow)
    projected_sums = column_sums(back[:, width:].astype(wide))
    qkv = matrix[:, : 3 * local]
    other = dot_t(back[half:, width:], qkv)
    mine = dot_t(back[:half, width:], qkv)
    part_other[...] = other.astype(narrow)
    part_mine[...] = mine
    if layer == 1:
        sums[...] = projected_sums
        return
    first_unit = width + 4 * local
    gain_sum = column_sums(mine * kept[:half, first_unit:].astype(wide))
    gain_sum += column_sums(other * kept[half:, first_unit:].astype(wide))
    shift_sum = column_sums(mine) + column_sums(other)
    column = lax.broadcasted_iota(jnp.int32, (1, width), 1) // local

    def rows_of(norm_sums, middle_sums, projected, hidden):
        found = [norm_sums, middle_sums]
        for values, k in ((projected, 0), (projected, 2), (hidden, 0), (hidden, 1), (hidden, 2), (hidden, 3)):
            row = jnp.concatenate([values[:, k * local : (k + 1) * local]] * (width // local), axis=1)
            found.append(jnp.where(column == my_part(), row, 0.0))
        return jnp.concatenate(found + [jnp.zeros((4, width), wide)], axis=0).astype(narrow)

    sums_zero, hidden_zero, norm_one, sums_one, projected_one, hidden_one = (ref[...] for ref in vectors)
    norm_zero = jnp.concatenate([gain_sum, shift_sum], axis=0)
    rows_zero = rows_of(norm_zero, sums_zero, projected_sums, hidden_zero)
    rows_one = rows_of(norm_one, sums_one, projected_one, hidden_one)
    count = len(slabs)
    size = width // count
    here = lax.axis_index("z")
    for k, slab in enumerate(slabs):
        first = pl.multiple_of(lax.rem(here + k, count) * size, size)
        normed = kept[:, pl.ds(first, size)]
        branch = back[:, pl.ds(first, size)]
        slab[:size, : 3 * local] = t_dot(normed, back[:, width:]).astype(narrow)
        slab[:size, 3 * local :] = t_dot(branch, kept[:, width + 3 * local : width + 4 * local]).astype(narrow)
    for k, slab in enumerate(slabs):
        for z in range(count):

            @pl.when(lax.rem(here + k, count) == z)
            def _():
                slab[size:, :size] = rows_zero[:, z * size : (z + 1) * size]
                slab[size:, size:] = rows_one[:, z * size : (z + 1) * size]


def hidden_parts(second, fc1, table):
    local = fc1.shape[1] // 4
    bias = jnp.concatenate([my_columns(table, 8 + r, local) for r in range(4)], axis=1)
    hidden = dot(second, fc1) + bias
    share = 0.5 * (1.0 + lax.erf(hidden * (0.5**0.5)))
    slope = share + hidden * jnp.exp(-0.5 * hidden * hidden) * 0.3989422804014327
    return (hidden * share).astype(narrow), slope


def mlp_kernel(*refs):
    blocks, (matrix, table, kept, part_mine, part_other, *fetch) = refs[:8], refs[8:]
    width, columns, half = part_mine.shape[1], fetch[0].shape[2] // 2, kept.shape[0] // 2
    matrix = Fetch(0, matrix, columns, *fetch)
    kept[:, :width] = whole(blocks).astype(narrow)
    activated, slope = hidden_parts(kept[:, :width], matrix[:, :columns], table)
    kept[:, width : width + columns] = activated
    kept[:, width + columns :] = slope.astype(narrow)
    part_other[...] = dot_t(activated[half:, :], matrix[:, columns:]).astype(narrow)
    part_mine[...] = dot_t(activated[:half, :], matrix[:, columns:])


def mlp_back_kernel(*refs):
    blocks, (kept, matrix, back, sums, part_mine, part_other, *fetch) = refs[:8], refs[8:]
    width, columns, half = part_mine.shape[1], fetch[0].shape[2] // 2, kept.shape[0] // 2
    matrix = Fetch(0, matrix, columns, *fetch)
    back[:, :width] = whole(blocks).astype(narrow)
    slope = kept[:, width + columns :].astype(wide)
    hidden_grad = (dot(back[:, :width], matrix[:, columns:]) * slope).astype(narrow)
    back[:, width:] = hidden_grad
    sums[...] = column_sums(hidden_grad.astype(wide))
    part_other[...] = dot_t(hidden_grad[half:, :], matrix[:, :columns]).astype(narrow)
    part_mine[...] = dot_t(hidden_grad[:half, :], matrix[:, :columns])


def mlp_both_kernel(*refs):
    blocks, final, (matrix, table, kept, back, sums, part_mine, part_other, left_mine, left_other, *fetch) = refs[:8], refs[8:16], refs[16:]
    width, columns, half = part_mine.shape[1], fetch[0].shape[2] // 2, kept.shape[0] // 2
    matrix = Fetch(1, matrix, columns, *fetch)
    kept[:, :width] = whole(blocks).astype(narrow)
    back[:, :width] = whole(final).astype(narrow)
    activated, slope = hidden_parts(kept[:, :width], matrix[:, :columns], table)
    kept[:, width:] = activated
    hidden_grad = (dot(back[:, :width], matrix[:, columns:]) * slope).astype(narrow)
    back[:, width:] = hidden_grad
    sums[...] = column_sums(hidden_grad.astype(wide))
    part_other[...] = dot_t(hidden_grad[half:, :], matrix[:, :columns]).astype(narrow)
    part_mine[...] = dot_t(hidden_grad[:half, :], matrix[:, :columns])
    left_other[...] = dot_t(activated[half:, :], matrix[:, columns:]).astype(narrow)
    left_mine[...] = dot_t(activated[:half, :], matrix[:, columns:]).astype(narrow)


def call(body, flops, outs, args, scratch=(), fetch=None, columns=None):
    specs = [pl.BlockSpec()] * len(args)
    scratch = list(scratch)
    if fetch is not None:
        shape = args[fetch].shape
        specs[fetch] = pl.BlockSpec(memory_space=pl.ANY)
        scratch += [pltpu.VMEM((shape[1], shape[3], columns), narrow), pltpu.SemaphoreType.DMA]
    return pl.pallas_call(
        body,
        out_shape=[jax.ShapeDtypeStruct(shape, kind) for shape, kind in outs],
        in_specs=specs,
        scratch_shapes=scratch,
        compiler_params=pltpu.CompilerParams(vmem_limit_bytes=48 << 20),
        cost_estimate=pl.CostEstimate(flops=flops, bytes_accessed=8 << 20, transcendentals=0),
    )(*args)


def partials(rows, width):
    return [((rows // 2, width), wide), ((rows // 2, width), narrow)]


def attend(layer, blocks, matrix, table):
    rows, width, columns = 8 * blocks[0].shape[0], blocks[0].shape[1], 8 * HDIM
    outs = [((rows, width + columns + width * (layer == 0)), narrow)] + partials(rows, width)
    body = functools.partial(attend_kernel, layer)
    fetch = (8, columns) if layer else (None, None)
    return call(body, 3 * 10**9, outs, [*blocks, matrix, table], (), *fetch)


def attend_back(layer, blocks, kept, matrix, vectors=()):
    rows, width, columns = kept.shape[0], blocks[0].shape[1], 8 * HDIM
    back = (rows, width + columns // 4 * 3)
    if layer == 0:
        count = lax.axis_size("z")
        outs = partials(rows, width) + [((width // count + 16, columns), narrow)] * count
        scratch = [pltpu.VMEM(back, narrow)]
    else:
        outs = [(back, narrow), ((1, columns // 4 * 3), wide)] + partials(rows, width)
        scratch = []
    body = functools.partial(attend_back_kernel, layer)
    fetch = (9, columns) if layer else (None, None)
    return call(body, 6 * 10**9, outs, [*blocks, kept, matrix, *vectors], scratch, *fetch)


def mlp(blocks, matrix, table):
    rows, width, columns = 8 * blocks[0].shape[0], blocks[0].shape[1], matrix.shape[4] // 3
    outs = [((rows, width + 2 * columns), narrow)] + partials(rows, width)
    return call(mlp_kernel, 4 * 10**9, outs, [*blocks, matrix, table], (), 8, 2 * columns)


def mlp_back(blocks, kept, matrix):
    rows, width, columns = kept.shape[0], blocks[0].shape[1], matrix.shape[4] // 3
    outs = [((rows, width + columns), narrow), ((1, columns), wide)] + partials(rows, width)
    return call(mlp_back_kernel, 4 * 10**9, outs, [*blocks, kept, matrix], (), 9, 2 * columns)


def mlp_both(blocks, final, matrix, table):
    rows, width, columns = 8 * blocks[0].shape[0], blocks[0].shape[1], matrix.shape[4] // 3
    outs = [((rows, width + columns), narrow)] * 2 + [((1, columns), wide)] + partials(rows, width)
    outs += [((rows // 2, width), narrow)] * 2
    return call(mlp_both_kernel, 6 * 10**9, outs, [*blocks, *final, matrix, table], (), 16, 2 * columns)


def pack(qkv, proj):
    rows, size = proj.shape
    return call(pack_kernel, 10**8, [((rows, 4 * size), narrow)], [qkv, proj])[0]


def pack_all(attention, fc1, fc2):
    shape = (attention.shape[0], 3 * attention.shape[1])
    return call(pack_all_kernel, 10**8, [(shape, narrow)], [attention, fc1, fc2])[0]


def ring_sums(mine, other):
    count = lax.axis_size("x")
    shape = (mine.shape[0] // count, mine.shape[1])
    outs = [(shape, wide)] + [(shape, narrow)] * (count - 1)
    return list(call(ring_kernel, 10**8, outs, [mine, other]))


def around_pieces(sums):
    return [sums[0]] + [along(piece, "x", k) for k, piece in enumerate(sums[1:], 1)]


def ring_pieces(mine, other):
    return around_pieces(ring_sums(mine, other))


def ring_order(mine, other):
    scratch = [pltpu.VMEM(mine.shape, wide)]
    return call(ring_order_kernel, 10**8, [(mine.shape, narrow)], [mine, other], scratch)[0]


def middle_of(terms, arriving, table):
    shape = arriving.shape
    return call(middle_kernel, 10**8, [(shape, wide), (shape, narrow)], [*terms, arriving, table])


def leave(terms, middle, table, following):
    return call(leave_kernel, 10**8, [(middle.shape, narrow)] * 2, [*terms, middle, table, following])


def middle_back(terms, grad, middle, table):
    shape = middle.shape
    outs = [(shape, wide), (shape, narrow), ((4, shape[1]), wide)]
    return call(middle_back_kernel, 10**8, outs, [*terms, grad, middle, table])


def input_back(terms, middle_grad, arriving, table):
    shape = arriving.shape
    outs = [(shape, narrow), ((2, shape[1]), wide)]
    return call(input_back_kernel, 10**8, outs, [*terms, middle_grad, arriving, table])


def mlp_grad(kept, back, shape, ring_first=False):
    return call(functools.partial(mlp_grad_kernel, ring_first), 2 * 10**9, [(shape, narrow)], [kept, back])[0]


def grad_part(body, flops, args, shape, columns):
    whole_array = pl.BlockSpec(memory_space=pl.ANY)
    added = len(args) == 3
    return pl.pallas_call(
        body,
        out_shape=jax.ShapeDtypeStruct(shape, narrow),
        in_specs=[pl.BlockSpec()] * 2 + [whole_array] * added,
        out_specs=whole_array,
        input_output_aliases={2: 0} if added else {},
        scratch_shapes=[pltpu.VMEM((shape[0], columns), narrow), pltpu.SemaphoreType.DMA],
        compiler_params=pltpu.CompilerParams(vmem_limit_bytes=48 << 20),
        cost_estimate=pl.CostEstimate(flops=flops, bytes_accessed=8 << 20, transcendentals=0),
    )(*args)


def finish(lower, upper, size):
    shapes = [(3, size, size), (size, size), (size, 4, size), (4, size, size)]
    return call(finish_kernel, 10**8, [(shape, wide) for shape in shapes], [lower, upper])


def tie(*values):
    return lax.optimization_barrier(values)


def hop(columns, layer):
    return lax.ppermute(columns, ("core", "ylo"), [(layer * 2, 0), (layer * 2 + 1, 3)])


def order_ring(own, arrived):
    core, high, low = (lax.axis_index(name) for name in ("core", "yhi", "ylo"))
    one, two, three = arrived
    holder = low == core
    a = jnp.where(holder, own, one)
    b = jnp.where(holder, two, three)
    place = high * 2 + low
    a_first = jnp.where(holder, high, (place + 1) % 4 // 2) == 0
    return jnp.concatenate([jnp.where(a_first, a, b), jnp.where(a_first, b, a)], axis=0)


def fold(zero, one):
    half = zero.shape[1] // 2
    return jnp.concatenate([zero[:, :half], zero[:, half:], one[:, :half], one[:, half:]], axis=0)


def unfold(rows):
    return [jnp.concatenate([rows[k : k + 12], rows[k + 12 : k + 24]], axis=1) for k in (0, 24)]


def per_device(inputs, cotangent, qkv_weight, proj_weight, fc1_weight, fc2_weight, vectors):
    width = inputs.shape[3]
    core = lax.axis_index("core")
    low = lax.axis_index("ylo")
    place = lax.axis_index(("z", "yhi", "ylo", "x"))
    local = qkv_weight.shape[3]
    own_rows = qkv_weight.shape[1]

    def added(values, arrived):
        return functools.reduce(lambda a, b: a + b, arrived, values)

    columns = lax.broadcasted_iota(jnp.int32, (12, width), 1) // 16
    table = jnp.where(columns == place, jnp.tile(vectors[0], (1, width // 16)), 0).astype(narrow)
    other_table = swap_cores(table)
    table = fold(jnp.where(core == 0, table, other_table), jnp.where(core == 0, other_table, table))
    attention_raw = pack(qkv_weight[0].reshape(own_rows, 3 * local), proj_weight[0])
    table, attention_raw, fc1_weight, fc2_weight = tie(table, attention_raw, fc1_weight, fc2_weight)
    raw = pack_all(attention_raw, fc1_weight[0].reshape(own_rows, 4 * local), fc2_weight[0])
    held = hop(attention_raw, 0)
    entering = turn(lax.dynamic_index_in_dim(inputs, core, 0, keepdims=False)[:, 0], 0)
    table = added(table, around(table, "x"))
    held, entering, table = tie(held, entering, table)
    mine = [entering] + around(entering, "x")
    arrived = around(jnp.concatenate([held, table], axis=0), RING)
    *arrived, raw = tie(*arrived, raw)
    blocks = order_ring(held, [piece[:own_rows] for piece in arrived])
    table = added(table, [piece[own_rows:] for piece in arrived])

    def gather_weights(rows):
        gathered = lax.all_gather(rows, ("core", "z", "yhi", "ylo"), axis=0, tiled=True)
        return gathered.reshape(2, 8, 2, own_rows, rows.shape[1])

    everything = gather_weights(raw)

    arrived = around(jnp.concatenate([blocks, table], axis=0), "z")
    mine[1], cotangent = tie(mine[1], cotangent)
    final_grad = turn(lax.dynamic_index_in_dim(cotangent, core, 0, keepdims=False)[:, 0], 0)
    entering_all = mine + [swap_cores(block) for block in mine]
    parts = [blocks] + [piece[: 2 * own_rows] for piece in arrived]
    start = (len(parts) - 1 - lax.axis_index("z")) * 2 * own_rows
    first = lax.dynamic_slice_in_dim(jnp.concatenate(parts[1:] + parts, axis=0), start, width, 0)
    tables = [t.astype(wide) for t in unfold(added(table, [piece[2 * own_rows :] for piece in arrived]))]

    def offload_sum(value, axis):
        return lax.psum_scatter(value, axis, scatter_dimension=0, tiled=True)

    kept_zero, mine, other = attend(0, entering_all, first, tables[0])
    terms = ring_pieces(mine, swap_cores(other))

    middle_zero, second = middle_of(terms, entering, tables[0])
    mlp_kept_zero, mine, other = mlp(gather_tokens(second), everything, tables[0])

    terms = ring_pieces(mine, swap_cores(other))
    *terms, final_grad = tie(*terms, final_grad)
    final_all = lax.all_gather(final_grad, ("core", "x")).reshape((2, 4) + entering.shape)

    left_zero, normed = leave(terms, middle_zero, tables[0], tables[1])
    kept_one, mine, other = attend(1, gather_tokens(normed), everything, tables[1])
    terms = ring_pieces(mine, swap_cores(other))
    final_blocks = []
    for which in (core, 1 - core):
        for k in range(4):
            spot = (which, (lax.axis_index("x") + k) % 4, 0, 0)
            piece = lax.dynamic_slice(final_all, spot, (1, 1) + entering.shape)
            final_blocks.append(piece.reshape(entering.shape))
    tied = tie(*terms, *final_blocks)
    terms, final_blocks = tied[:4], tied[4:]
    middle_one, second = middle_of(terms, left_zero, tables[1])

    mlp_kept_one, mlp_back_one, hidden_one, mine, other, left_mine, left_other = mlp_both(
        gather_tokens(second), final_blocks, everything, tables[1]
    )
    terms = ring_pieces(mine, swap_cores(other))
    left_total = ring_order(left_mine, swap_cores(left_other))
    *terms, left_total = tie(*terms, left_total)
    left_total = offload_sum(left_total, "x")
    middle_grad, branch_grad, sums_one = middle_back(terms, final_blocks[0], middle_one, tables[1])
    grads_shape = (width, 12 * local)
    grads_one = grad_part(mlp_part_kernel, 2 * 10**9, [mlp_kept_one, mlp_back_one], grads_shape, 8 * local)
    blocks, grads_one = gather_tokens(branch_grad, grads_one)
    back, projected_one, mine, other = attend_back(1, blocks, kept_one, everything)
    terms = ring_pieces(mine, swap_cores(other))
    grads_one = grad_part(attention_part_kernel, 10**9, [kept_one, back, grads_one], grads_shape, 4 * local)
    *terms, left_total = tie(*terms, left_total)
    grads_one = offload_sum(grads_one, "z")
    down_grad, norm_one = input_back(terms, middle_grad, left_zero, tables[1])

    back, hidden_zero, mine, other = mlp_back(gather_tokens(down_grad), mlp_kept_zero, everything)
    terms = ring_pieces(mine, swap_cores(other))
    mlp_zero = mlp_grad(mlp_kept_zero, back, (width, 8 * local), True)
    mlp_zero = offload_sum(mlp_zero, RING)
    *terms, grads_one = tie(*terms, grads_one)
    grads_one = offload_sum(grads_one, RING)
    middle_grad, branch_grad, sums_zero = middle_back(terms, down_grad, middle_zero, tables[0])
    vectors = [sums_zero, hidden_zero, norm_one, sums_one, projected_one, hidden_one]

    mine, other, *slabs = attend_back(0, gather_tokens(branch_grad), kept_zero, first, vectors)
    other, mlp_zero = tie(other, mlp_zero)
    mlp_zero = offload_sum(mlp_zero, "z")

    sent = [along(slab, "z", k) for k, slab in enumerate(slabs) if k > 0]
    sums = ring_sums(mine, swap_cores(other))
    terms = around_pieces(sums)
    terms[0], grads_one = tie(terms[0], grads_one)
    slab = added(slabs[0].astype(wide), [piece.astype(wide) for piece in sent]).astype(narrow)
    slab, *terms = tie(slab, *terms)
    grad_zero, _ = input_back(terms, middle_grad, entering, tables[0])
    left_one = (middle_one + left_total.astype(wide) + tables[1][5:6]).astype(narrow)

    done_zero = jnp.concatenate([left_zero, grad_zero], axis=0)
    done_one = jnp.concatenate([left_one, down_grad], axis=0)
    done_mine = turn_back(jnp.where(low == 0, done_zero, done_one), 0)
    done_other = turn_back(jnp.where(low == 0, done_one, done_zero), 1)
    count, rows = lax.axis_size(RING), own_rows // 2
    turn_rows = lax.axis_index(RING) * rows

    def ring_slab(k):
        start = (turn_rows + k * rows) % (count * rows)
        return jnp.concatenate(
            [lax.dynamic_slice_in_dim(slab, start, rows, 0), slab[count * rows :]], axis=0
        )

    sent = [along(ring_slab(k), RING, k) for k in range(1, count)]
    slab = added(ring_slab(0).astype(wide), [piece.astype(wide) for piece in sent])

    done = jnp.stack([jnp.where(core == 0, done_mine, done_other), jnp.where(core == 0, done_other, done_mine)])
    tokens = entering.shape[0]
    activations = done[None, :, :tokens, None]
    input_grads = done[None, :, tokens:, None].astype(wide)
    grads_one, activations, input_grads = tie(grads_one, activations, input_grads)

    owned_zero = jnp.concatenate([slab[:rows].astype(narrow), mlp_zero], axis=1)
    owned_one = grads_one
    got_mine = turn_back(jnp.where(low == 0, owned_zero, owned_one), 0)
    got_other = turn_back(jnp.where(low == 0, owned_one, owned_zero), 1)
    vector_sum = slab[rows:]
    vector_sum = added(vector_sum, around(vector_sum, "x"))
    vector_sum, got_mine, got_other = tie(vector_sum, got_mine, got_other)
    vector_zero, vector_one = vector_sum[:, : 2 * local], vector_sum[:, 2 * local :]
    vector_sum = jnp.where(core == 0, vector_zero, vector_one) + swap_cores(
        jnp.where(core == 0, vector_one, vector_zero)
    )
    start = turn_rows + lax.axis_index("x") * 16
    vector_owned = lax.dynamic_slice_in_dim(vector_sum[:12], start, 16, 1)
    qkv_grad, proj_grad, fc1_grad, fc2_grad = finish(got_mine, got_other, local)
    return (
        activations,
        input_grads,
        jnp.transpose(qkv_grad, (1, 0, 2))[None],
        proj_grad[None],
        fc1_grad[None],
        fc2_grad[None],
        vector_owned[None],
    )


def solution(mesh):
    fine = Mesh(mesh.devices.reshape(2, 4, 2, 2, 4), ("core", "z", "yhi", "ylo", "x"))
    tensor = ("ylo", "x")
    dp = ("z", "yhi")
    in_specs = (
        P(None, tensor, dp, None),
        P(None, tensor, dp, None),
        P("core", dp, None, tensor),
        P("core", tensor, dp),
        P("core", dp, None, tensor),
        P("core", None, tensor, dp),
        P("core", None, dp + tensor),
    )
    out_specs = (
        P("core", None, tensor, dp, None),
        P("core", None, tensor, dp, None),
        P("core", dp, None, tensor),
        P("core", tensor, dp),
        P("core", dp, None, tensor),
        P("core", None, tensor, dp),
        P("core", None, dp + tensor),
    )
    return jax.shard_map(
        per_device, mesh=fine, in_specs=in_specs, out_specs=out_specs, check_vma=False
    )
```

```python
import functools

import jax
import jax.numpy as jnp
from jax import lax
from jax.experimental import pallas as pl
from jax.experimental.pallas import tpu as pltpu
from jax.sharding import Mesh, PartitionSpec as P

HDIM = 64
SCALE = HDIM ** (-0.5)

eps = 1e-06
wide = jnp.float32
narrow = jnp.bfloat16


RING = ("yhi", "ylo")


def swap_cores(value):
    return lax.ppermute(value, "core", [(0, 1), (1, 0)])


def along(value, axis, steps):
    count = lax.axis_size(axis)
    return lax.ppermute(value, axis, [(i, (i + steps) % count) for i in range(count)])


def around(value, axis):
    return [along(value, axis, -k) for k in range(1, lax.axis_size(axis))]


def turn(value, flip):
    pairs = [(c * 2 + y, y * 2 + (c ^ flip)) for c in range(2) for y in range(2)]
    return lax.ppermute(value, ("core", "ylo"), pairs)


def turn_back(value, flip):
    pairs = [(c * 2 + y, (y ^ flip) * 2 + c) for c in range(2) for y in range(2)]
    return lax.ppermute(value, ("core", "ylo"), pairs)


def gather_tokens(rows, *others):
    mine = [rows] + around(rows, "x")
    mine[-1], *others = lax.optimization_barrier((mine[-1], *others))
    blocks = mine + [swap_cores(block) for block in mine]
    return (blocks, *others) if others else blocks


def normalise(rows):
    center = rows - jnp.mean(rows, axis=-1, keepdims=True)
    spread = jnp.mean(center * center, axis=-1, keepdims=True)
    inverse = lax.rsqrt(spread + eps)
    return center * inverse, inverse


def norm_back(grad, gain, unit, inverse):
    pulled = grad * gain
    mean_one = jnp.mean(pulled, axis=-1, keepdims=True)
    mean_two = jnp.mean(pulled * unit, axis=-1, keepdims=True)
    return inverse * (pulled - mean_one - unit * mean_two)


def dot(a, b):
    return jnp.dot(a, b, preferred_element_type=wide)


def dot_t(a, b):
    return lax.dot_general(a, b, (((1,), (1,)), ((), ())), preferred_element_type=wide)


def t_dot(a, b):
    return lax.dot_general(a, b, (((0,), (0,)), ((), ())), preferred_element_type=wide)


def whole(refs):
    return jnp.concatenate([ref[...].astype(wide) for ref in refs], axis=0)


def column_sums(values):
    return jnp.sum(values, axis=0, keepdims=True)


def my_part():
    return lax.axis_index("core") * lax.axis_size("x") + lax.axis_index("x")


def my_columns(table, row, size):
    start = pl.multiple_of(my_part() * size, size)
    return table[row : row + 1, pl.ds(start, size)]


class Fetch:
    def __init__(self, layer, source, start, held, semaphore):
        self.held = held
        columns = source.at[layer, :, lax.axis_index("core"), :, pl.ds(start, held.shape[-1])]
        self.copy = pltpu.make_async_copy(columns, held, semaphore)
        self.copy.start()

    def __getitem__(self, key):
        if self.copy is not None:
            self.copy.wait()
            self.copy = None
        part = self.held[:, :, key[1]]
        return part.reshape(-1, part.shape[-1])


def pack_kernel(qkv, proj, packed):
    size = proj.shape[1]
    packed[:, : 3 * size] = qkv[...]
    packed[:, 3 * size :] = proj[...].astype(wide).T.astype(narrow)


def pack_all_kernel(attention, fc1, fc2, packed):
    size = fc2.shape[1]
    packed[:, : 4 * size] = attention[...]
    packed[:, 4 * size : 8 * size] = fc1[...]
    for k in range(4):
        packed[:, (8 + k) * size : (9 + k) * size] = fc2[k].astype(wide).T.astype(narrow)


def finish_kernel(lower, upper, qkv, proj, fc1, fc2):
    size = proj.shape[0]
    flip = lax.axis_index("core") == 1
    first = jnp.where(flip, upper[...].astype(wide), lower[...].astype(wide))
    second = jnp.where(flip, lower[...].astype(wide), upper[...].astype(wide))
    owned = jnp.concatenate([first, second], axis=0)
    for k in range(3):
        qkv[k] = owned[:, k * size : (k + 1) * size]
    proj[...] = owned[:, 3 * size : 4 * size].T
    for k in range(4):
        fc1[:, k, :] = owned[:, (4 + k) * size : (5 + k) * size]
        fc2[k] = owned[:, (8 + k) * size : (9 + k) * size].T


def mlp_grad_kernel(ring_first, kept, back, grads):
    width, columns = grads.shape[0], grads.shape[1] // 2
    halves = [
        t_dot(kept[:, :width], back[:, width:]).astype(narrow),
        t_dot(back[:, :width], kept[:, width : width + columns]).astype(narrow),
    ]
    for k, half in enumerate(halves):
        if ring_first:
            size = width // 16
            order = [(z * 4 + y) * size for y in range(4) for z in range(4)]
            half = jnp.concatenate([half[start : start + size] for start in order], axis=0)
        grads[:, k * columns : (k + 1) * columns] = half


def store_columns(held, grads, start, semaphore):
    columns = grads.at[:, pl.ds(start, held.shape[1])]
    copy = pltpu.make_async_copy(held, columns, semaphore)
    copy.start()
    copy.wait()


def mlp_part_kernel(kept, back, grads, held, semaphore):
    width, columns = held.shape[0], held.shape[1] // 2
    held[:, :columns] = t_dot(kept[:, :width], back[:, width:]).astype(narrow)
    held[:, columns:] = t_dot(back[:, :width], kept[:, width:]).astype(narrow)
    store_columns(held, grads, columns, semaphore)


def attention_part_kernel(kept, back, _, grads, held, semaphore):
    width, local = held.shape[0], held.shape[1] // 4
    held[:, : 3 * local] = t_dot(kept[:, :width], back[:, width:]).astype(narrow)
    held[:, 3 * local :] = t_dot(back[:, :width], kept[:, width + 3 * local :]).astype(narrow)
    store_columns(held, grads, 0, semaphore)


def ring_kernel(mine, other, own, *pieces):
    total = mine[...] + other[...].astype(wide)
    rows = own.shape[0]
    own[...] = total[:rows]
    for k, piece in enumerate(pieces):
        piece[...] = total[(k + 1) * rows : (k + 2) * rows].astype(narrow)


def ring_order_kernel(mine, other, ordered, total):
    total[...] = mine[...].astype(wide) + other[...].astype(wide)
    count = lax.axis_size("x")
    rows = total.shape[0] // count
    blocks = []
    for k in range(count):
        first = lax.rem(k + count - lax.axis_index("x"), count) * rows
        blocks.append(total[pl.ds(pl.multiple_of(first, 8), rows), :])
    ordered[...] = jnp.concatenate(blocks, axis=0).astype(narrow)


def summed(refs):
    total = refs[0][...]
    for piece in refs[1:]:
        total = total + piece[...].astype(wide)
    return total


def middle_kernel(own, one, two, three, arriving, table, middle, second):
    total = arriving[...].astype(wide) + summed((own, one, two, three)) + table[4:5, :]
    middle[...] = total
    second[...] = (normalise(total)[0] * table[2:3, :] + table[3:4, :]).astype(narrow)


def leave_kernel(own, one, two, three, middle, table, *refs):
    left = (middle[...] + summed((own, one, two, three)) + table[5:6, :]).astype(narrow)
    following, leaving, normed = refs
    leaving[...] = left
    unit = normalise(left.astype(wide))[0]
    normed[...] = (unit * following[0:1, :] + following[1:2, :]).astype(narrow)


def middle_back_kernel(own, one, two, three, grad, middle, table, branch_grad, sums):
    second_grad = summed((own, one, two, three))
    unit, inverse = normalise(middle[...])
    arriving = grad[...].astype(wide)
    total = arriving + norm_back(second_grad, table[2:3, :], unit, inverse)
    branch = total.astype(narrow)
    branch_grad[...] = branch
    sums[0:1, :] = column_sums(second_grad * unit)
    sums[1:2, :] = column_sums(second_grad)
    sums[2:3, :] = column_sums(branch.astype(wide))
    sums[3:4, :] = column_sums(arriving)


def input_back_kernel(own, one, two, three, branch_grad, arriving, table, down_grad, sums):
    normed_grad = summed((own, one, two, three))
    unit, inverse = normalise(arriving[...].astype(wide))
    total = branch_grad[...].astype(wide) + norm_back(normed_grad, table[0:1, :], unit, inverse)
    down_grad[...] = total.astype(narrow)
    sums[0:1, :] = column_sums(normed_grad * unit)
    sums[1:2, :] = column_sums(normed_grad)


def attend_kernel(layer, *refs):
    blocks, (matrix, table, kept, part_mine, part_other, *fetch) = refs[:8], refs[8:]
    rows, width, local = kept.shape[0], part_mine.shape[1], 2 * HDIM
    half = rows // 2
    if layer == 1:
        matrix = Fetch(layer, matrix, 0, *fetch)
    if layer == 0:
        unit = normalise(whole(blocks))[0]
        kept[:, width + 4 * local :] = unit.astype(narrow)
        kept[:, :width] = (unit * table[0:1, :] + table[1:2, :]).astype(narrow)
    else:
        kept[:, :width] = whole(blocks).astype(narrow)
    query_bias, value_bias = my_columns(table, 6, local), my_columns(table, 7, local)
    bias = jnp.concatenate([query_bias, jnp.zeros_like(query_bias), value_bias], axis=1)
    projected = (dot(kept[:, :width], matrix[:, : 3 * local]) + bias).astype(narrow)
    kept[:, width : width + 3 * local] = projected
    queries = projected[:, :local]
    key_rows = projected[:, local : 2 * local]
    value_rows = projected[:, 2 * local :]
    lower = lax.broadcasted_iota(jnp.int32, (rows, local), 1) < HDIM
    outs = []
    for keep in (lower, ~lower):
        scores = dot_t(jnp.where(keep, queries, jnp.zeros_like(queries)), key_rows) * SCALE
        raised = jnp.exp(scores - jnp.max(scores, axis=-1, keepdims=True))
        probs = raised * (1.0 / jnp.sum(raised, axis=-1, keepdims=True))
        outs.append(dot(probs.astype(narrow), value_rows))
    mixed = jnp.where(lower, outs[0], outs[1]).astype(narrow)
    kept[:, width + 3 * local : width + 4 * local] = mixed
    proj = matrix[:, 3 * local : 4 * local]
    part_other[...] = dot_t(mixed[half:, :], proj).astype(narrow)
    part_mine[...] = dot_t(mixed[:half, :], proj)


def attend_back_kernel(layer, *refs):
    blocks, (kept, matrix, *refs) = refs[:8], refs[8:]
    local = 2 * HDIM
    rows, width = kept.shape[0], kept.shape[1] - 4 * local
    if layer == 0:
        width = width // 2
    half = rows // 2
    if layer == 0:
        vectors, (part_mine, part_other, *slabs, back) = refs[:6], refs[6:]
    else:
        back, sums, part_mine, part_other, *fetch = refs
        matrix = Fetch(layer, matrix, 0, *fetch)
    back[:, :width] = whole(blocks).astype(narrow)
    out = dot(back[:, :width], matrix[:, 3 * local : 4 * local]).astype(narrow)
    queries = kept[:, width : width + local]
    key_rows = kept[:, width + local : width + 2 * local]
    value_rows = kept[:, width + 2 * local : width + 3 * local]
    lower = lax.broadcasted_iota(jnp.int32, (rows, local), 1) < HDIM
    query_grads, key_grad, value_grad = [], 0.0, 0.0
    for keep in (lower, ~lower):
        query = jnp.where(keep, queries, jnp.zeros_like(queries))
        grad = jnp.where(keep, out, jnp.zeros_like(out))
        scores = dot_t(query, key_rows) * SCALE
        raised = jnp.exp(scores - jnp.max(scores, axis=-1, keepdims=True))
        probs = raised * (1.0 / jnp.sum(raised, axis=-1, keepdims=True))
        prob_grad = dot_t(grad, value_rows)
        inner = jnp.sum(probs * prob_grad, axis=-1, keepdims=True)
        score_grad = (probs * (prob_grad - inner)).astype(narrow)
        query_grads.append(dot(score_grad, key_rows))
        value_grad = value_grad + t_dot(probs.astype(narrow), grad)
        key_grad = key_grad + t_dot(score_grad, query)
    back[:, width : width + local] = (jnp.where(lower, query_grads[0], query_grads[1]) * SCALE).astype(narrow)
    back[:, width + local : width + 2 * local] = (key_grad * SCALE).astype(narrow)
    back[:, width + 2 * local :] = value_grad.astype(narrow)
    projected_sums = column_sums(back[:, width:].astype(wide))
    qkv = matrix[:, : 3 * local]
    other = dot_t(back[half:, width:], qkv)
    mine = dot_t(back[:half, width:], qkv)
    part_other[...] = other.astype(narrow)
    part_mine[...] = mine
    if layer == 1:
        sums[...] = projected_sums
        return
    first_unit = width + 4 * local
    gain_sum = column_sums(mine * kept[:half, first_unit:].astype(wide))
    gain_sum += column_sums(other * kept[half:, first_unit:].astype(wide))
    shift_sum = column_sums(mine) + column_sums(other)
    column = lax.broadcasted_iota(jnp.int32, (1, width), 1) // local

    def rows_of(norm_sums, middle_sums, projected, hidden):
        found = [norm_sums, middle_sums]
        for values, k in ((projected, 0), (projected, 2), (hidden, 0), (hidden, 1), (hidden, 2), (hidden, 3)):
            row = jnp.concatenate([values[:, k * local : (k + 1) * local]] * (width // local), axis=1)
            found.append(jnp.where(column == my_part(), row, 0.0))
        return jnp.concatenate(found + [jnp.zeros((4, width), wide)], axis=0).astype(narrow)

    sums_zero, hidden_zero, norm_one, sums_one, projected_one, hidden_one = (ref[...] for ref in vectors)
    norm_zero = jnp.concatenate([gain_sum, shift_sum], axis=0)
    rows_zero = rows_of(norm_zero, sums_zero, projected_sums, hidden_zero)
    rows_one = rows_of(norm_one, sums_one, projected_one, hidden_one)
    count = len(slabs)
    size = width // count
    here = lax.axis_index("z")
    for k, slab in enumerate(slabs):
        first = pl.multiple_of(lax.rem(here + k, count) * size, size)
        normed = kept[:, pl.ds(first, size)]
        branch = back[:, pl.ds(first, size)]
        slab[:size, : 3 * local] = t_dot(normed, back[:, width:]).astype(narrow)
        slab[:size, 3 * local :] = t_dot(branch, kept[:, width + 3 * local : width + 4 * local]).astype(narrow)
    for k, slab in enumerate(slabs):
        for z in range(count):

            @pl.when(lax.rem(here + k, count) == z)
            def _():
                slab[size:, :size] = rows_zero[:, z * size : (z + 1) * size]
                slab[size:, size:] = rows_one[:, z * size : (z + 1) * size]


def hidden_parts(second, fc1, table):
    local = fc1.shape[1] // 4
    bias = jnp.concatenate([my_columns(table, 8 + r, local) for r in range(4)], axis=1)
    hidden = dot(second, fc1) + bias
    share = 0.5 * (1.0 + lax.erf(hidden * (0.5**0.5)))
    slope = share + hidden * jnp.exp(-0.5 * hidden * hidden) * 0.3989422804014327
    return (hidden * share).astype(narrow), slope


def mlp_kernel(*refs):
    blocks, (matrix, table, kept, part_mine, part_other, *fetch) = refs[:8], refs[8:]
    width, columns, half = part_mine.shape[1], fetch[0].shape[2] // 2, kept.shape[0] // 2
    matrix = Fetch(0, matrix, columns, *fetch)
    kept[:, :width] = whole(blocks).astype(narrow)
    activated, slope = hidden_parts(kept[:, :width], matrix[:, :columns], table)
    kept[:, width : width + columns] = activated
    kept[:, width + columns :] = slope.astype(narrow)
    part_other[...] = dot_t(activated[half:, :], matrix[:, columns:]).astype(narrow)
    part_mine[...] = dot_t(activated[:half, :], matrix[:, columns:])


def mlp_back_kernel(*refs):
    blocks, (kept, matrix, back, sums, part_mine, part_other, *fetch) = refs[:8], refs[8:]
    width, columns, half = part_mine.shape[1], fetch[0].shape[2] // 2, kept.shape[0] // 2
    matrix = Fetch(0, matrix, columns, *fetch)
    back[:, :width] = whole(blocks).astype(narrow)
    slope = kept[:, width + columns :].astype(wide)
    hidden_grad = (dot(back[:, :width], matrix[:, columns:]) * slope).astype(narrow)
    back[:, width:] = hidden_grad
    sums[...] = column_sums(hidden_grad.astype(wide))
    part_other[...] = dot_t(hidden_grad[half:, :], matrix[:, :columns]).astype(narrow)
    part_mine[...] = dot_t(hidden_grad[:half, :], matrix[:, :columns])


def mlp_both_kernel(*refs):
    blocks, final, (matrix, table, kept, back, sums, part_mine, part_other, left_mine, left_other, *fetch) = refs[:8], refs[8:16], refs[16:]
    width, columns, half = part_mine.shape[1], fetch[0].shape[2] // 2, kept.shape[0] // 2
    matrix = Fetch(1, matrix, columns, *fetch)
    kept[:, :width] = whole(blocks).astype(narrow)
    back[:, :width] = whole(final).astype(narrow)
    activated, slope = hidden_parts(kept[:, :width], matrix[:, :columns], table)
    kept[:, width:] = activated
    hidden_grad = (dot(back[:, :width], matrix[:, columns:]) * slope).astype(narrow)
    back[:, width:] = hidden_grad
    sums[...] = column_sums(hidden_grad.astype(wide))
    part_other[...] = dot_t(hidden_grad[half:, :], matrix[:, :columns]).astype(narrow)
    part_mine[...] = dot_t(hidden_grad[:half, :], matrix[:, :columns])
    left_other[...] = dot_t(activated[half:, :], matrix[:, columns:]).astype(narrow)
    left_mine[...] = dot_t(activated[:half, :], matrix[:, columns:]).astype(narrow)


def call(body, flops, outs, args, scratch=(), fetch=None, columns=None):
    specs = [pl.BlockSpec()] * len(args)
    scratch = list(scratch)
    if fetch is not None:
        shape = args[fetch].shape
        specs[fetch] = pl.BlockSpec(memory_space=pl.ANY)
        scratch += [pltpu.VMEM((shape[1], shape[3], columns), narrow), pltpu.SemaphoreType.DMA]
    return pl.pallas_call(
        body,
        out_shape=[jax.ShapeDtypeStruct(shape, kind) for shape, kind in outs],
        in_specs=specs,
        scratch_shapes=scratch,
        compiler_params=pltpu.CompilerParams(vmem_limit_bytes=48 << 20),
        cost_estimate=pl.CostEstimate(flops=flops, bytes_accessed=8 << 20, transcendentals=0),
    )(*args)


def partials(rows, width):
    return [((rows // 2, width), wide), ((rows // 2, width), narrow)]


def attend(layer, blocks, matrix, table):
    rows, width, columns = 8 * blocks[0].shape[0], blocks[0].shape[1], 8 * HDIM
    outs = [((rows, width + columns + width * (layer == 0)), narrow)] + partials(rows, width)
    body = functools.partial(attend_kernel, layer)
    fetch = (8, columns) if layer else (None, None)
    return call(body, 3 * 10**9, outs, [*blocks, matrix, table], (), *fetch)


def attend_back(layer, blocks, kept, matrix, vectors=()):
    rows, width, columns = kept.shape[0], blocks[0].shape[1], 8 * HDIM
    back = (rows, width + columns // 4 * 3)
    if layer == 0:
        count = lax.axis_size("z")
        outs = partials(rows, width) + [((width // count + 16, columns), narrow)] * count
        scratch = [pltpu.VMEM(back, narrow)]
    else:
        outs = [(back, narrow), ((1, columns // 4 * 3), wide)] + partials(rows, width)
        scratch = []
    body = functools.partial(attend_back_kernel, layer)
    fetch = (9, columns) if layer else (None, None)
    return call(body, 6 * 10**9, outs, [*blocks, kept, matrix, *vectors], scratch, *fetch)


def mlp(blocks, matrix, table):
    rows, width, columns = 8 * blocks[0].shape[0], blocks[0].shape[1], matrix.shape[4] // 3
    outs = [((rows, width + 2 * columns), narrow)] + partials(rows, width)
    return call(mlp_kernel, 4 * 10**9, outs, [*blocks, matrix, table], (), 8, 2 * columns)


def mlp_back(blocks, kept, matrix):
    rows, width, columns = kept.shape[0], blocks[0].shape[1], matrix.shape[4] // 3
    outs = [((rows, width + columns), narrow), ((1, columns), wide)] + partials(rows, width)
    return call(mlp_back_kernel, 4 * 10**9, outs, [*blocks, kept, matrix], (), 9, 2 * columns)


def mlp_both(blocks, final, matrix, table):
    rows, width, columns = 8 * blocks[0].shape[0], blocks[0].shape[1], matrix.shape[4] // 3
    outs = [((rows, width + columns), narrow)] * 2 + [((1, columns), wide)] + partials(rows, width)
    outs += [((rows // 2, width), narrow)] * 2
    return call(mlp_both_kernel, 6 * 10**9, outs, [*blocks, *final, matrix, table], (), 16, 2 * columns)


def pack(qkv, proj):
    rows, size = proj.shape
    return call(pack_kernel, 10**8, [((rows, 4 * size), narrow)], [qkv, proj])[0]


def pack_all(attention, fc1, fc2):
    shape = (attention.shape[0], 3 * attention.shape[1])
    return call(pack_all_kernel, 10**8, [(shape, narrow)], [attention, fc1, fc2])[0]


def ring_sums(mine, other):
    count = lax.axis_size("x")
    shape = (mine.shape[0] // count, mine.shape[1])
    outs = [(shape, wide)] + [(shape, narrow)] * (count - 1)
    return list(call(ring_kernel, 10**8, outs, [mine, other]))


def around_pieces(sums):
    return [sums[0]] + [along(piece, "x", k) for k, piece in enumerate(sums[1:], 1)]


def ring_pieces(mine, other):
    return around_pieces(ring_sums(mine, other))


def ring_order(mine, other):
    scratch = [pltpu.VMEM(mine.shape, wide)]
    return call(ring_order_kernel, 10**8, [(mine.shape, narrow)], [mine, other], scratch)[0]


def middle_of(terms, arriving, table):
    shape = arriving.shape
    return call(middle_kernel, 10**8, [(shape, wide), (shape, narrow)], [*terms, arriving, table])


def leave(terms, middle, table, following):
    return call(leave_kernel, 10**8, [(middle.shape, narrow)] * 2, [*terms, middle, table, following])


def middle_back(terms, grad, middle, table):
    shape = middle.shape
    outs = [(shape, narrow), ((4, shape[1]), wide)]
    return call(middle_back_kernel, 10**8, outs, [*terms, grad, middle, table])


def input_back(terms, branch_grad, arriving, table):
    shape = arriving.shape
    outs = [(shape, narrow), ((2, shape[1]), wide)]
    return call(input_back_kernel, 10**8, outs, [*terms, branch_grad, arriving, table])


def mlp_grad(kept, back, shape, ring_first=False):
    return call(functools.partial(mlp_grad_kernel, ring_first), 2 * 10**9, [(shape, narrow)], [kept, back])[0]


def grad_part(body, flops, args, shape, columns):
    whole_array = pl.BlockSpec(memory_space=pl.ANY)
    added = len(args) == 3
    return pl.pallas_call(
        body,
        out_shape=jax.ShapeDtypeStruct(shape, narrow),
        in_specs=[pl.BlockSpec()] * 2 + [whole_array] * added,
        out_specs=whole_array,
        input_output_aliases={2: 0} if added else {},
        scratch_shapes=[pltpu.VMEM((shape[0], columns), narrow), pltpu.SemaphoreType.DMA],
        compiler_params=pltpu.CompilerParams(vmem_limit_bytes=48 << 20),
        cost_estimate=pl.CostEstimate(flops=flops, bytes_accessed=8 << 20, transcendentals=0),
    )(*args)


def finish(lower, upper, size):
    shapes = [(3, size, size), (size, size), (size, 4, size), (4, size, size)]
    return call(finish_kernel, 10**8, [(shape, wide) for shape in shapes], [lower, upper])


def tie(*values):
    return lax.optimization_barrier(values)


def hop(columns, layer):
    return lax.ppermute(columns, ("core", "ylo"), [(layer * 2, 0), (layer * 2 + 1, 3)])


def order_ring(own, arrived):
    core, high, low = (lax.axis_index(name) for name in ("core", "yhi", "ylo"))
    one, two, three = arrived
    holder = low == core
    a = jnp.where(holder, own, one)
    b = jnp.where(holder, two, three)
    place = high * 2 + low
    a_first = jnp.where(holder, high, (place + 1) % 4 // 2) == 0
    return jnp.concatenate([jnp.where(a_first, a, b), jnp.where(a_first, b, a)], axis=0)


def fold(zero, one):
    half = zero.shape[1] // 2
    return jnp.concatenate([zero[:, :half], zero[:, half:], one[:, :half], one[:, half:]], axis=0)


def unfold(rows):
    return [jnp.concatenate([rows[k : k + 12], rows[k + 12 : k + 24]], axis=1) for k in (0, 24)]


def per_device(inputs, cotangent, qkv_weight, proj_weight, fc1_weight, fc2_weight, vectors):
    width = inputs.shape[3]
    core = lax.axis_index("core")
    low = lax.axis_index("ylo")
    place = lax.axis_index(("z", "yhi", "ylo", "x"))
    local = qkv_weight.shape[3]
    own_rows = qkv_weight.shape[1]

    def added(values, arrived):
        return functools.reduce(lambda a, b: a + b, arrived, values)

    columns = lax.broadcasted_iota(jnp.int32, (12, width), 1) // 16
    table = jnp.where(columns == place, jnp.tile(vectors[0], (1, width // 16)), 0).astype(narrow)
    other_table = swap_cores(table)
    table = fold(jnp.where(core == 0, table, other_table), jnp.where(core == 0, other_table, table))
    attention_raw = pack(qkv_weight[0].reshape(own_rows, 3 * local), proj_weight[0])
    table, attention_raw, fc1_weight, fc2_weight = tie(table, attention_raw, fc1_weight, fc2_weight)
    raw = pack_all(attention_raw, fc1_weight[0].reshape(own_rows, 4 * local), fc2_weight[0])
    held = hop(attention_raw, 0)
    entering = turn(lax.dynamic_index_in_dim(inputs, core, 0, keepdims=False)[:, 0], 0)
    table = added(table, around(table, "x"))
    held, entering, table = tie(held, entering, table)
    mine = [entering] + around(entering, "x")
    arrived = around(jnp.concatenate([held, table], axis=0), RING)
    *arrived, raw = tie(*arrived, raw)
    blocks = order_ring(held, [piece[:own_rows] for piece in arrived])
    table = added(table, [piece[own_rows:] for piece in arrived])

    def gather_weights(rows):
        gathered = lax.all_gather(rows, ("core", "z", "yhi", "ylo"), axis=0, tiled=True)
        return gathered.reshape(2, 8, 2, own_rows, rows.shape[1])

    everything = gather_weights(raw)

    arrived = around(jnp.concatenate([blocks, table], axis=0), "z")
    mine[1], cotangent = tie(mine[1], cotangent)
    final_grad = turn(lax.dynamic_index_in_dim(cotangent, core, 0, keepdims=False)[:, 0], 0)
    entering_all = mine + [swap_cores(block) for block in mine]
    parts = [blocks] + [piece[: 2 * own_rows] for piece in arrived]
    start = (len(parts) - 1 - lax.axis_index("z")) * 2 * own_rows
    first = lax.dynamic_slice_in_dim(jnp.concatenate(parts[1:] + parts, axis=0), start, width, 0)
    tables = [t.astype(wide) for t in unfold(added(table, [piece[2 * own_rows :] for piece in arrived]))]

    def offload_sum(value, axis):
        return lax.psum_scatter(value, axis, scatter_dimension=0, tiled=True)

    kept_zero, mine, other = attend(0, entering_all, first, tables[0])
    terms = ring_pieces(mine, swap_cores(other))

    middle_zero, second = middle_of(terms, entering, tables[0])
    mlp_kept_zero, mine, other = mlp(gather_tokens(second), everything, tables[0])

    terms = ring_pieces(mine, swap_cores(other))
    *terms, final_grad = tie(*terms, final_grad)
    final_all = lax.all_gather(final_grad, ("core", "x")).reshape((2, 4) + entering.shape)

    left_zero, normed = leave(terms, middle_zero, tables[0], tables[1])
    kept_one, mine, other = attend(1, gather_tokens(normed), everything, tables[1])
    terms = ring_pieces(mine, swap_cores(other))
    final_blocks = []
    for which in (core, 1 - core):
        for k in range(4):
            spot = (which, (lax.axis_index("x") + k) % 4, 0, 0)
            piece = lax.dynamic_slice(final_all, spot, (1, 1) + entering.shape)
            final_blocks.append(piece.reshape(entering.shape))
    tied = tie(*terms, *final_blocks)
    terms, final_blocks = tied[:4], tied[4:]
    middle_one, second = middle_of(terms, left_zero, tables[1])

    mlp_kept_one, mlp_back_one, hidden_one, mine, other, left_mine, left_other = mlp_both(
        gather_tokens(second), final_blocks, everything, tables[1]
    )
    terms = ring_pieces(mine, swap_cores(other))
    left_total = ring_order(left_mine, swap_cores(left_other))
    *terms, left_total = tie(*terms, left_total)
    left_total = offload_sum(left_total, "x")
    branch_grad, sums_one = middle_back(terms, final_blocks[0], middle_one, tables[1])
    grads_shape = (width, 12 * local)
    grads_one = grad_part(mlp_part_kernel, 2 * 10**9, [mlp_kept_one, mlp_back_one], grads_shape, 8 * local)
    blocks, grads_one = gather_tokens(branch_grad, grads_one)
    back, projected_one, mine, other = attend_back(1, blocks, kept_one, everything)
    terms = ring_pieces(mine, swap_cores(other))
    grads_one = grad_part(attention_part_kernel, 10**9, [kept_one, back, grads_one], grads_shape, 4 * local)
    *terms, left_total = tie(*terms, left_total)
    grads_one = offload_sum(grads_one, "z")
    down_grad, norm_one = input_back(terms, branch_grad, left_zero, tables[1])

    back, hidden_zero, mine, other = mlp_back(gather_tokens(down_grad), mlp_kept_zero, everything)
    terms = ring_pieces(mine, swap_cores(other))
    mlp_zero = mlp_grad(mlp_kept_zero, back, (width, 8 * local), True)
    mlp_zero = offload_sum(mlp_zero, RING)
    *terms, grads_one = tie(*terms, grads_one)
    grads_one = offload_sum(grads_one, RING)
    branch_grad, sums_zero = middle_back(terms, down_grad, middle_zero, tables[0])
    vectors = [sums_zero, hidden_zero, norm_one, sums_one, projected_one, hidden_one]

    mine, other, *slabs = attend_back(0, gather_tokens(branch_grad), kept_zero, first, vectors)
    other, mlp_zero = tie(other, mlp_zero)
    mlp_zero = offload_sum(mlp_zero, "z")

    sent = [along(slab, "z", k) for k, slab in enumerate(slabs) if k > 0]
    sums = ring_sums(mine, swap_cores(other))
    terms = around_pieces(sums)
    terms[0], grads_one = tie(terms[0], grads_one)
    slab = added(slabs[0].astype(wide), [piece.astype(wide) for piece in sent]).astype(narrow)
    slab, *terms = tie(slab, *terms)
    grad_zero, _ = input_back(terms, branch_grad, entering, tables[0])
    left_one = (middle_one + left_total.astype(wide) + tables[1][5:6]).astype(narrow)

    done_zero = jnp.concatenate([left_zero, grad_zero], axis=0)
    done_one = jnp.concatenate([left_one, down_grad], axis=0)
    done_mine = turn_back(jnp.where(low == 0, done_zero, done_one), 0)
    done_other = turn_back(jnp.where(low == 0, done_one, done_zero), 1)
    count, rows = lax.axis_size(RING), own_rows // 2
    turn_rows = lax.axis_index(RING) * rows

    def ring_slab(k):
        start = (turn_rows + k * rows) % (count * rows)
        return jnp.concatenate(
            [lax.dynamic_slice_in_dim(slab, start, rows, 0), slab[count * rows :]], axis=0
        )

    sent = [along(ring_slab(k), RING, k) for k in range(1, count)]
    slab = added(ring_slab(0).astype(wide), [piece.astype(wide) for piece in sent])

    done = jnp.stack([jnp.where(core == 0, done_mine, done_other), jnp.where(core == 0, done_other, done_mine)])
    tokens = entering.shape[0]
    activations = done[None, :, :tokens, None]
    input_grads = done[None, :, tokens:, None].astype(wide)
    grads_one, activations, input_grads = tie(grads_one, activations, input_grads)

    owned_zero = jnp.concatenate([slab[:rows].astype(narrow), mlp_zero], axis=1)
    owned_one = grads_one
    got_mine = turn_back(jnp.where(low == 0, owned_zero, owned_one), 0)
    got_other = turn_back(jnp.where(low == 0, owned_one, owned_zero), 1)
    vector_sum = slab[rows:]
    vector_sum = added(vector_sum, around(vector_sum, "x"))
    vector_sum, got_mine, got_other = tie(vector_sum, got_mine, got_other)
    vector_zero, vector_one = vector_sum[:, : 2 * local], vector_sum[:, 2 * local :]
    vector_sum = jnp.where(core == 0, vector_zero, vector_one) + swap_cores(
        jnp.where(core == 0, vector_one, vector_zero)
    )
    start = turn_rows + lax.axis_index("x") * 16
    vector_owned = lax.dynamic_slice_in_dim(vector_sum[:12], start, 16, 1)
    qkv_grad, proj_grad, fc1_grad, fc2_grad = finish(got_mine, got_other, local)
    return (
        activations,
        input_grads,
        jnp.transpose(qkv_grad, (1, 0, 2))[None],
        proj_grad[None],
        fc1_grad[None],
        fc2_grad[None],
        vector_owned[None],
    )


def solution(mesh):
    fine = Mesh(mesh.devices.reshape(2, 4, 2, 2, 4), ("core", "z", "yhi", "ylo", "x"))
    tensor = ("ylo", "x")
    dp = ("z", "yhi")
    in_specs = (
        P(None, tensor, dp, None),
        P(None, tensor, dp, None),
        P("core", dp, None, tensor),
        P("core", tensor, dp),
        P("core", dp, None, tensor),
        P("core", None, tensor, dp),
        P("core", None, dp + tensor),
    )
    out_specs = (
        P("core", None, tensor, dp, None),
        P("core", None, tensor, dp, None),
        P("core", dp, None, tensor),
        P("core", tensor, dp),
        P("core", dp, None, tensor),
        P("core", None, tensor, dp),
        P("core", None, dp + tensor),
    )
    return jax.shard_map(
        per_device, mesh=fine, in_specs=in_specs, out_specs=out_specs, check_vma=False
    )
```
